32 devices in a mesh: fsdp: 8 (over z, y), tensor: 4 (over x, core).
Axes of the slice: x: 2, y: 2, z: 4, core: 2. Of those that a mesh axis runs over, the one named last changes fastest.
Arguments:
- inputs: bfloat16 [16384, 1280], P(('fsdp', 'tensor')), may hold values from -6 to 6
- doc_ids: int32 [16384], P('fsdp'), may hold values from 0 to 175, as said below
- w_qkv: float32 [1280, 3, 1280], P('fsdp', None, 'tensor'), may hold values from -0.15625 to 0.15625
- w_out: float32 [1280, 1280], P('tensor', 'fsdp'), may hold values from -0.625 to 0.625
- w_up: float32 [1280, 1280], P('fsdp', 'tensor'), may hold values from -0.15625 to 0.15625
- up_bias: float32 [1280], P('tensor'), may hold values from -3 to 3
- w_down: float32 [1280, 1280], P('tensor', 'fsdp'), may hold values from -0.15625 to 0.15625
- down_bias: float32 [1280], P('fsdp'), may hold values from -3 to 3
- attn_gain: float32 [1280], P('fsdp'), may hold values from 0.5 to 1.5
- mlp_gain: float32 [1280], P('fsdp'), may hold values from 0.5 to 1.5
- dim_scale: float32 [80], replicated, may hold values from -0.5 to 1.5
- cotangent: bfloat16 [16384, 1280], P(('fsdp', 'tensor')), may hold values from -6 to 6
Outputs:
- layer_out: bfloat16 [16384, 1280], P(('fsdp', 'tensor'))
- input_grad: bfloat16 [16384, 1280], P(('fsdp', 'tensor'))
- qkv_grad: float32 [1280, 3, 1280], P('fsdp', None, 'tensor')
- out_grad: float32 [1280, 1280], P('tensor', 'fsdp')
- up_grad: float32 [1280, 1280], P('fsdp', 'tensor')
- upbias_grad: float32 [1280], P('tensor')
- down_grad: float32 [1280, 1280], P('tensor', 'fsdp')
- downbias_grad: float32 [1280], P('fsdp')
- attngain_grad: float32 [1280], P('fsdp')
- mlpgain_grad: float32 [1280], P('fsdp')
- scale_grad: float32 [80], replicated
The draws below stay inside these ranges and needn't reach their ends.
Inputs may be any that keep to these rules, and one draw needn't show every extreme that they name: `doc_ids`: document numbers never fall along the tokens and rise by one from one document to the next within a sequence, and a document lies inside one sequence of 1024 consecutive tokens (sequences follow one another from token 0). A document has 102 to 999 tokens, except a sequence's last one, which may be shorter. The last document of the sequence with number s has number (s + 1) * (1024 // max(102, 1) + 1) - 1.
All inputs are finite; a program needn't handle non-finite values.
Results may differ from the reference program's by a relative error of at most 0.018.
Values may be sent and summed in bfloat16 or wider, within the bound.
No kernel may reach another device: no remote copies, remote signals or barrier semaphores. Data moves between devices by JAX's collectives and lax.ppermute only.
A program may use at most 192 MiB of HBM per device.

```python
import math
import jax
import jax.numpy as jnp
from jax import lax

D = 1280
H = 16
HD = 80
FF = 1280
LEN = 1024
TOKENS = 16384


def draw_doc_ids(key, part):
    key = jax.random.fold_in(key, 7)
    shortest = max(LEN // 10, 1)
    longest = LEN - LEN // 40
    doc_slots = LEN // shortest + 1
    seq_count = TOKENS // LEN
    lengths = jax.random.randint(key, (seq_count, doc_slots), shortest, longest + 1)
    boundary = jnp.cumsum(lengths, axis=1)
    position = jnp.arange(LEN)
    within = jnp.sum((boundary[:, None, :] <= position[None, :, None]).astype(jnp.int32), axis=2)
    last_within = within[:, LEN - 1:LEN]
    doc_index = doc_slots - 1 - (last_within - within) + doc_slots * jnp.arange(seq_count)[:, None]
    return doc_index.reshape(TOKENS).astype(jnp.int32)


def strengthened(drawn, own_key, source, target, parts, factor):
    owner, partner = [(jnp.arange(drawn.shape[dim]) // (drawn.shape[dim] // parts)).reshape([-1 if axis == dim else 1 for axis in range(drawn.ndim)]) for dim in (source, target)]
    chosen = jax.random.permutation(own_key, parts)[partner]
    strong = (owner == chosen) | (owner == (partner + parts // 2) % parts)
    return jnp.where(strong, factor * drawn, drawn)


def shard_levels(key, dims, cuts, least, top_value):
    gain = 1.0
    for dim, blocks in cuts:
        heights = jax.random.uniform(jax.random.fold_in(jax.random.fold_in(key, 6), dim), (blocks,), jnp.float32, least / len(cuts), top_value / len(cuts))
        gain = gain * jnp.repeat(jnp.exp(heights), dims[dim] // blocks).reshape((-1,) + (1,) * (len(dims) - 1 - dim))
    return gain


def noise(rng, shape, spread, reach, pieces=(), held_as=jnp.bfloat16):
    values = spread * jax.random.normal(rng, shape, jnp.float32)
    if pieces:
        values = values * shard_levels(rng, shape, pieces, -0.22, 0.18)
    return jnp.clip(values, -reach, reach).astype(held_as)


def gaussian_with(key, dims, scale, reach, split, heavy, kind=jnp.bfloat16):
    result = scale * jax.random.normal(key, dims, jnp.float32)
    if split:
        result = result * shard_levels(key, dims, split, -0.22, 0.18)
    return jnp.clip(strengthened(result, jax.random.fold_in(key, 3), *heavy), -reach, reach).astype(kind)


def setup_inputs(seed: int = 0) -> dict:
    key_list = jax.random.split(jax.random.key(seed), 13)
    return {
        "inputs": noise(key_list[0], (TOKENS, D), 1.0, 6.0, ((0, 32),)),
        "doc_ids": draw_doc_ids(jax.random.fold_in(key_list[12], 71), 0),
        "w_qkv": noise(key_list[2], (D, 3, H * HD), D ** -0.5, 0.15625, ((0, 8), (2, 4)), jnp.float32),
        "w_out": noise(key_list[3], (H * HD, D), (H * HD // 16) ** -0.5, 0.625, ((0, 4), (1, 8)), jnp.float32),
        "w_up": noise(key_list[4], (D, FF), D ** -0.5, 0.15625, ((0, 8), (1, 4)), jnp.float32),
        "up_bias": noise(key_list[5], (FF,), 0.5, 3.0, ((0, 4),), jnp.float32),
        "w_down": noise(key_list[6], (FF, D), FF ** -0.5, 0.15625, ((0, 4), (1, 8)), jnp.float32),
        "down_bias": noise(key_list[7], (D,), 0.5, 3.0, ((0, 8),), jnp.float32),
        "attn_gain": jnp.clip(1.0 + 0.1 * jax.random.normal(key_list[8], (D,), jnp.float32), 0.5, 1.5),
        "mlp_gain": jnp.clip(1.0 + 0.1 * jax.random.normal(key_list[9], (D,), jnp.float32), 0.5, 1.5),
        "dim_scale": jnp.clip(jax.random.uniform(key_list[10], (HD,), jnp.float32, -0.5, 1.5), -0.5, 1.5),
        "cotangent": gaussian_with(key_list[11], (TOKENS, D), 1.0, 6.0, ((0, 32),), (0, 1, 32, 2.75)),
    }


NORM_EPS = 1e-06
PERDIM_BASE = 1.442695041
NEG_FILL = -1e+30
HIGHEST = lax.Precision.HIGHEST

@jax.custom_vjp
def low(v):
    return lax.optimization_barrier(v.astype(jnp.bfloat16)).astype(jnp.float32)

@jax.custom_vjp
def low_back(v):
    return v

def low_keep(v):
    return (low(v), None)

def low_pass(kept, grad):
    return (grad,)

def back_keep(v):
    return (v, None)

def back_low(kept, grad):
    return (low(grad),)
low.defvjp(low_keep, low_pass)
low_back.defvjp(back_keep, back_low)

def attend(query_seq, key_seq, value_seq, doc_seq):
    scores = low_back(jnp.einsum('qhe,khe->hqk', query_seq, key_seq, precision=HIGHEST))
    position = jnp.arange(query_seq.shape[0])
    allowed = (doc_seq[:, None] == doc_seq[None, :]) & (position[:, None] >= position[None, :])
    weights = jax.nn.softmax(jnp.where(allowed[None], scores, NEG_FILL), axis=-1)
    return jnp.einsum('hqk,khe->qhe', low(weights), value_seq, precision=HIGHEST)

def block_forward(values, doc_block, w_qkv, w_out, w_up, up_bias, w_down, down_bias, attn_gain, mlp_gain, dim_scale):
    row_count = values.shape[0]
    seq_count = row_count // LEN
    recip_first = lax.rsqrt(lax.optimization_barrier(jnp.mean(values * values, axis=-1, keepdims=True)) + NORM_EPS)
    normed_first = low(values * recip_first * low(attn_gain))
    projected = jnp.einsum('td,dch->cth', normed_first, low(w_qkv), precision=HIGHEST)
    query_scale = PERDIM_BASE / math.sqrt(HD) * jax.nn.softplus(dim_scale)
    query_rows = low(low_back(projected[0]).reshape(row_count, H, HD) * query_scale)
    key_rows = low(low_back(projected[1])).reshape(row_count, H, HD)
    value_rows = low(low_back(projected[2])).reshape(row_count, H, HD)
    attended = lax.map(lambda seq_parts: jax.checkpoint(attend)(*seq_parts), (query_rows.reshape(seq_count, LEN, H, HD), key_rows.reshape(seq_count, LEN, H, HD), value_rows.reshape(seq_count, LEN, H, HD), doc_block.reshape(seq_count, LEN)))
    attn_heads = low(low_back(attended.reshape(row_count, H * HD)))
    attn_sum = low_back(jnp.dot(attn_heads, low(w_out), precision=HIGHEST))
    resid_first = values + attn_sum
    recip_second = lax.rsqrt(lax.optimization_barrier(jnp.mean(resid_first * resid_first, axis=-1, keepdims=True)) + NORM_EPS)
    normed_second = low(resid_first * recip_second * low(mlp_gain))
    hidden_pre = low_back(jnp.dot(normed_second, low(w_up), precision=HIGHEST) + up_bias)
    hidden_rows = low(jax.nn.silu(hidden_pre))
    mlp_sum = low_back(jnp.dot(hidden_rows, low(w_down), precision=HIGHEST))
    return resid_first + mlp_sum + low(down_bias)

def reference(inputs, doc_ids, w_qkv, w_out, w_up, up_bias, w_down, down_bias, attn_gain, mlp_gain, dim_scale, cotangent):
    token_count = inputs.shape[0]
    seq_count = token_count // LEN
    per_block = math.gcd(seq_count, max(1, 4096 // LEN))
    block_count = seq_count // per_block
    block_rows = per_block * LEN
    masters = (w_qkv, w_out, w_up, up_bias, w_down, down_bias, attn_gain, mlp_gain, dim_scale)
    input_blocks = inputs.astype(jnp.float32).reshape(block_count, block_rows, D)
    cot_blocks = cotangent.astype(jnp.float32).reshape(block_count, block_rows, D)
    doc_blocks = doc_ids.reshape(block_count, block_rows)

    def scan_step(carried, scan_item):
        input_block, doc_block, cot_block = scan_item

        def forward(values, *weights):
            return block_forward(values, doc_block, *weights)
        layer_block, pullback = jax.vjp(forward, input_block, *masters)
        gradients = pullback(cot_block)
        summed = tuple((running + update for running, update in zip(carried, gradients[1:])))
        return (summed, (layer_block.astype(jnp.bfloat16), gradients[0].astype(jnp.bfloat16)))
    initial = tuple((jnp.zeros_like(weight) for weight in masters))
    summed_grads, (out_blocks, grad_blocks) = lax.scan(scan_step, initial, (input_blocks, doc_blocks, cot_blocks))
    return (out_blocks.reshape(token_count, D), grad_blocks.reshape(token_count, D), summed_grads[0], summed_grads[1], summed_grads[2], summed_grads[3], summed_grads[4], summed_grads[5], summed_grads[6], summed_grads[7], summed_grads[8])
```

```python
import math

import jax
import jax.numpy as jnp
from jax import lax
from jax.experimental import pallas as pl
from jax.experimental.pallas import tpu as pltpu
from jax.sharding import Mesh
from jax.sharding import PartitionSpec as P

HD = 80
LEN = 1024
BQ = 256
NORM_EPS = 1e-06
PERDIM_BASE = 1.442695041
NEG_FILL = -1e30
VMEM_BYTES = 56 << 20
BF16 = jnp.bfloat16
F32 = jnp.float32
NT = (((1,), (1,)), ((), ()))
NN = (((1,), (0,)), ((), ()))
TN = (((0,), (0,)), ((), ()))


def dot(a, b, dims=NN):
    return lax.dot_general(a, b, dims, preferred_element_type=F32)


def swap(value, axis, bit):
    size = lax.axis_size(axis)
    return lax.ppermute(value, axis, [(i, i ^ bit) for i in range(size)])


def rms_scale(values):
    return lax.rsqrt(jnp.mean(values * values, axis=-1, keepdims=True) + NORM_EPS)


def by_position(pieces, me):
    bit = 1
    while bit < len(pieces):
        flip = (me & bit) != 0
        pieces = [jnp.where(flip, pieces[i ^ bit], pieces[i]) for i in range(len(pieces))]
        bit *= 2
    return pieces


def gather_rows(shard):
    half = shard.shape[0] // 2
    parts = [shard] + [swap(shard, "fsdp", 2 * j) for j in (1, 2, 3)]
    first = jnp.stack([p[:half] for p in parts])
    second = jnp.stack([p[half:] for p in parts])
    first_y = swap(first, "fsdp", 1)
    second_x = swap(second, "tx", 1)
    first_x = swap(first, "tx", 1)
    second_y = swap(second, "fsdp", 1)
    first_yx = swap(first_y, "tx", 1)
    second_xy = swap(second_x, "fsdp", 1)
    own = [first, first_y, second, second_y]
    other = [first_x, first_yx, second_x, second_xy]
    return own, other


def reduce_rows(grads_own, grads_other, rank):
    size = lax.axis_size("fsdp")
    rows, cols = grads_own.shape
    if size != 8:
        total = grads_own + swap(grads_other, "tx", 1)
        return lax.psum_scatter(total, "fsdp", scatter_dimension=0, tiled=True).astype(F32)
    shard = rows // size
    own = grads_own.reshape(4, 2, 2, shard // 2, cols)
    other = grads_other.reshape(4, 2, 2, shard // 2, cols)
    y, z = rank % 2, rank // 2

    def at_y(value, index):
        return lax.dynamic_index_in_dim(value, index, 1, keepdims=False)

    def add(a, b):
        return (a.astype(F32) + b.astype(F32)).astype(BF16)

    first = add(own[:, :, 0], swap(other[:, :, 0], "tx", 1))
    second_other = add(at_y(other[:, :, 1], y), swap(at_y(other[:, :, 1], 1 - y), "fsdp", 1))
    second_own = add(at_y(own[:, :, 1], y), swap(at_y(own[:, :, 1], 1 - y), "fsdp", 1))
    first = add(at_y(first, y), swap(at_y(first, 1 - y), "fsdp", 1))
    second = add(second_own, swap(second_other, "tx", 1))
    both = jnp.concatenate([first, second], axis=1)
    total = lax.dynamic_index_in_dim(both, z, 0, keepdims=False).astype(F32)
    for j in (1, 2, 3):
        piece = lax.dynamic_index_in_dim(both, z ^ j, 0, keepdims=False)
        total = total + swap(piece, "fsdp", 2 * j).astype(F32)
    return total


def sum_everywhere(value, axes):
    for axis in axes:
        bit = 1
        while bit < lax.axis_size(axis):
            value = value + swap(value, axis, bit)
            bit *= 2
    return value


def mask_bias(doc_col, doc_row, bias):
    for i in range(LEN // BQ):
        lo, hi = i * BQ, (i + 1) * BQ
        same = doc_col[:hi, :] == doc_row[:, lo:hi]
        keys = lax.broadcasted_iota(jnp.int32, (hi, BQ), 0)
        queries = lax.broadcasted_iota(jnp.int32, (hi, BQ), 1) + lo
        bias[i, :hi, :] = jnp.where(same & (keys <= queries), 0.0, NEG_FILL)


def attn_fwd_kernel(place, *refs):
    *pieces, x, colscale, doc_col, doc_row, attn, lse, qkv, weight, bias, sems = refs
    width = attn.shape[1]
    heads = width // HD
    half_rows = LEN // 2
    core, rank = place[0], place[1]
    copies = []
    if len(pieces) == 1:
        copies.append(pltpu.make_async_copy(pieces[0], weight, sems.at[0]))
    else:
        shard = weight.shape[0] // 8
        for n, piece in enumerate(pieces):
            for zj in range(4):
                start = (rank ^ (2 * zj + n % 2)) * shard + (n // 2) * (shard // 2)
                start = pl.multiple_of(start, 16)
                copies.append(
                    pltpu.make_async_copy(
                        piece.at[zj], weight.at[pl.ds(start, shard // 2)], sems.at[4 * n + zj]
                    )
                )
    for copy in copies:
        copy.start()
    mask_bias(doc_col, doc_row, bias)
    for copy in copies:
        copy.wait()
    for i in range(LEN // BQ):
        lo = i * BQ
        src = pl.multiple_of(((lo // half_rows) ^ core) * half_rows + lo % half_rows, BQ)
        qkv[lo : lo + BQ, :] = (dot(x[pl.ds(src, BQ), :], weight[...]) * colscale[...]).astype(BF16)
    outs = []
    for h in range(heads):
        key = qkv[:, width + h * HD : width + (h + 1) * HD]
        value_t = qkv[:, 2 * width + h * HD : 2 * width + (h + 1) * HD].T
        cols = []
        for i in range(LEN // BQ):
            lo, hi = i * BQ, (i + 1) * BQ
            query = qkv[lo:hi, h * HD : (h + 1) * HD]
            scores = dot(key[:hi], query, NT) + bias[i, :hi, :]
            top = jnp.max(scores, axis=0, keepdims=True)
            probs = jnp.exp(scores - top)
            total = jnp.sum(probs, axis=0, keepdims=True)
            cols.append(dot(value_t[:, :hi], probs.astype(BF16)) / total)
            lse[h : h + 1, lo:hi] = top + jnp.log(total)
        outs.append(jnp.concatenate(cols, axis=1).T.astype(BF16))
    for a in range(2):
        dst = pl.multiple_of((a ^ core) * half_rows, half_rows)
        attn[pl.ds(dst, half_rows), :] = jnp.concatenate(
            [o[a * half_rows : (a + 1) * half_rows] for o in outs], axis=1
        )


def attn_forward(place, pieces, x, colscale, doc_col, doc_row):
    depth, cols = x.shape[1], colscale.shape[1]
    vmem = pl.BlockSpec(memory_space=pltpu.VMEM)
    return pl.pallas_call(
        attn_fwd_kernel,
        in_specs=[pl.BlockSpec(memory_space=pltpu.SMEM)]
        + [pl.BlockSpec(memory_space=pl.ANY)] * len(pieces)
        + [vmem] * 4,
        out_specs=[vmem] * 4,
        out_shape=(
            jax.ShapeDtypeStruct((LEN, cols // 3), BF16),
            jax.ShapeDtypeStruct((8, LEN), F32),
            jax.ShapeDtypeStruct((LEN, cols), BF16),
            jax.ShapeDtypeStruct((depth, cols), BF16),
        ),
        scratch_shapes=[
            pltpu.VMEM((LEN // BQ, LEN, BQ), F32),
            pltpu.SemaphoreType.DMA((16,)),
        ],
        compiler_params=pltpu.CompilerParams(vmem_limit_bytes=VMEM_BYTES),
        name="attn_forward",
    )(place, *pieces, x, colscale, doc_col, doc_row)


def attn_bwd_kernel(place, qkv, attn, dout, lse, doc_col, doc_row, scale, grad, scale_sum, dkey, dvalue, bias, *, first):
    width = attn.shape[1]
    heads = width // HD
    blocks = LEN // BQ
    half_rows = LEN // 2
    core = place[0]

    def outer(lo):
        return pl.ds(pl.multiple_of(((lo // half_rows) ^ core) * half_rows + lo % half_rows, BQ), BQ)

    selector = jnp.where(
        lax.broadcasted_iota(jnp.int32, (8, width), 1) // HD == lax.broadcasted_iota(jnp.int32, (8, width), 0),
        1.0,
        0.0,
    )
    mask_bias(doc_col, doc_row, bias)
    douts, deltas = [], []
    for i in range(blocks):
        dout_block = dout[outer(i * BQ), first : first + width]
        products = attn[outer(i * BQ), :].astype(F32) * dout_block.astype(F32)
        deltas.append(
            lax.dot_general(selector, products, NT, precision=lax.Precision.HIGHEST, preferred_element_type=F32)
        )
        douts.append(dout_block)
    sums = jnp.zeros((1, HD), F32)
    grads = [[], [], []]
    for h in range(heads):
        key = qkv[:, width + h * HD : width + (h + 1) * HD]
        key_t = key.T
        dquery_parts = []
        for i in range(blocks):
            lo, hi = i * BQ, (i + 1) * BQ
            query = qkv[lo:hi, h * HD : (h + 1) * HD]
            value = qkv[:hi, 2 * width + h * HD : 2 * width + (h + 1) * HD]
            dout_head = douts[i][:, h * HD : (h + 1) * HD]
            scores = dot(key[:hi], query, NT) + bias[i, :hi, :]
            probs = jnp.exp(scores - lse[h : h + 1, lo:hi])
            dprobs = dot(value, dout_head, NT)
            dscores = (probs * (dprobs - deltas[i][h : h + 1, :])).astype(BF16)
            dv = dot(probs.astype(BF16), dout_head)
            dk = dot(dscores, query)
            dquery_parts.append(dot(key_t[:, :hi], dscores))
            if i:
                dkey[:lo] += dk[:lo]
                dvalue[:lo] += dv[:lo]
            dkey[lo:hi] = dk[lo:]
            dvalue[lo:hi] = dv[lo:]
        dquery = jnp.concatenate(dquery_parts, axis=1).T
        sums = sums + jnp.sum(dquery * qkv[:, h * HD : (h + 1) * HD].astype(F32), axis=0, keepdims=True)
        grads[0].append((dquery * scale[...]).astype(BF16))
        grads[1].append(dkey[...].astype(BF16))
        grads[2].append(dvalue[...].astype(BF16))
    for part in range(3):
        joined = jnp.concatenate(grads[part], axis=1)
        for a in range(2):
            dst = pl.multiple_of((a ^ core) * half_rows, half_rows)
            grad[pl.ds(dst, half_rows), part * width : (part + 1) * width] = joined[
                a * half_rows : (a + 1) * half_rows
            ]
    scale_sum[...] = sums / scale[...]


def attn_backward(place, qkv, attn, dout, lse, doc_col, doc_row, scale, first):
    def kernel(*refs):
        attn_bwd_kernel(*refs, first=first)

    vmem = pl.BlockSpec(memory_space=pltpu.VMEM)
    return pl.pallas_call(
        kernel,
        in_specs=[pl.BlockSpec(memory_space=pltpu.SMEM)] + [vmem] * 7,
        out_specs=[vmem] * 2,
        out_shape=(
            jax.ShapeDtypeStruct(qkv.shape, BF16),
            jax.ShapeDtypeStruct((1, HD), F32),
        ),
        scratch_shapes=[
            pltpu.VMEM((LEN, HD), F32),
            pltpu.VMEM((LEN, HD), F32),
            pltpu.VMEM((LEN // BQ, LEN, BQ), F32),
        ],
        compiler_params=pltpu.CompilerParams(vmem_limit_bytes=VMEM_BYTES),
        name="attn_backward",
    )(place, qkv, attn, dout, lse, doc_col, doc_row, scale)


def local(
    inputs,
    doc_ids,
    w_qkv,
    w_out,
    w_up,
    up_bias,
    w_down,
    down_bias,
    attn_gain,
    mlp_gain,
    dim_scale,
    cotangent,
):
    shard, _, width = w_qkv.shape
    size = lax.axis_size("fsdp")
    depth = shard * size
    rows = inputs.shape[0]
    core, tx, rank = lax.axis_index("core"), lax.axis_index("tx"), lax.axis_index("fsdp")
    place = jnp.stack([core, rank]).astype(jnp.int32)

    shard_qkv = w_qkv.astype(BF16).reshape(shard, 3 * width)
    shard_mlp = jnp.concatenate([w_out.T, w_up, w_down.T], axis=1).astype(BF16)
    gathered = lax.all_gather(shard_mlp, ("fsdp", "tx"), axis=0, tiled=False).reshape(size, 2, shard, 3 * width)
    if size == 8:
        pieces = gather_rows(shard_qkv)
    else:
        whole = lax.all_gather(shard_qkv, "fsdp", axis=0, tiled=True)
        pieces = [whole], [swap(whole, "tx", 1)]

    vectors = jnp.stack([attn_gain, mlp_gain, down_bias]).astype(BF16)
    if size == 8:
        parts = [vectors] + [swap(vectors, "fsdp", 2 * j) for j in (1, 2, 3)]
        parts_y = [swap(jnp.stack(parts), "fsdp", 1)[j] for j in range(4)]
        mixed = [p for pair in zip(parts, parts_y) for p in pair]
        vectors_full = jnp.concatenate(by_position(mixed, rank), axis=1)
    else:
        vectors_full = lax.all_gather(vectors, "fsdp", axis=1, tiled=True)
    gain_first, gain_second, bias_second = [vectors_full[i : i + 1].astype(F32) for i in range(3)]
    bias_up = jnp.concatenate([up_bias, swap(up_bias, "tx", 1)])[None]

    input_rows = jnp.concatenate([inputs, swap(inputs, "core", 1)]).astype(F32)
    cot_rows = jnp.concatenate([cotangent, swap(cotangent, "core", 1)])
    docs = lax.dynamic_slice_in_dim(doc_ids, tx * LEN, LEN, 0)
    doc_col, doc_row = docs[:, None], docs[None, :]

    recip_first = rms_scale(input_rows)
    unit_first = input_rows * recip_first
    normed_first = (unit_first * gain_first).astype(BF16)
    scale_base = PERDIM_BASE / math.sqrt(HD)
    query_scale = scale_base * jax.nn.softplus(dim_scale)
    heads = width // HD
    colscale = jnp.concatenate([jnp.tile(query_scale, heads), jnp.ones((2 * width,), F32)])[None]
    forward = [attn_forward(place, pieces[r], normed_first, colscale, doc_col, doc_row) for r in range(2)]
    attn_heads = jnp.concatenate([forward[0][0], forward[1][0]], axis=1)

    mlp_weights = [
        lax.dynamic_index_in_dim(gathered, tx ^ r, 1, keepdims=False).reshape(depth, 3 * width) for r in range(2)
    ]
    out_t, up, down_t = [
        jnp.concatenate([w[:, i * width : (i + 1) * width] for w in mlp_weights], axis=1) for i in range(3)
    ]

    def row_sum(left, weight, dims):
        sent = swap(dot(left[rows:], weight, dims).astype(BF16), "core", 1)
        return dot(left[:rows], weight, dims) + sent.astype(F32)

    own_inputs = inputs.astype(F32)
    resid_first = own_inputs + row_sum(attn_heads, out_t, NT)
    recip_second = rms_scale(resid_first)
    unit_second = resid_first * recip_second
    normed_own = (unit_second * gain_second).astype(BF16)
    normed_second = jnp.concatenate([normed_own, swap(normed_own, "core", 1)])
    hidden_pre = dot(normed_second, up) + bias_up
    sigmoid_pre = jax.nn.sigmoid(hidden_pre)
    hidden = (hidden_pre * sigmoid_pre).astype(BF16)
    layer_out = (resid_first + row_sum(hidden, down_t, NT) + bias_second).astype(BF16)

    grad_hidden = dot(cot_rows, down_t)
    grad_pre = (grad_hidden * (sigmoid_pre + hidden_pre * sigmoid_pre * (1.0 - sigmoid_pre))).astype(BF16)
    down_grad_t = dot(cot_rows, hidden, TN).astype(BF16)
    up_grad = dot(normed_second, grad_pre, TN).astype(BF16)
    upbias_part = jnp.sum(grad_pre.astype(F32), axis=0)
    grad_normed_second = row_sum(grad_pre, up, NT)
    scaled_second = grad_normed_second * gain_second
    mlpgain_part = jnp.sum(grad_normed_second * unit_second, axis=0)
    cot_float = cotangent.astype(F32)
    grad_resid = cot_float + recip_second * (
        scaled_second - unit_second * jnp.mean(scaled_second * unit_second, axis=-1, keepdims=True)
    )
    grad_own = grad_resid.astype(BF16)
    grad_attn = jnp.concatenate([grad_own, swap(grad_own, "core", 1)])
    grad_heads = dot(grad_attn, out_t).astype(BF16)
    out_grad_t = dot(grad_attn, attn_heads, TN).astype(BF16)
    mlp_grads = [
        jnp.concatenate([g[:, r * width : (r + 1) * width] for g in (out_grad_t, up_grad, down_grad_t)], axis=1)
        for r in range(2)
    ]
    mlp_grad = reduce_rows(mlp_grads[0], mlp_grads[1], rank)

    backward = [
        attn_backward(
            place,
            forward[r][2],
            forward[r][0],
            grad_heads,
            forward[r][1],
            doc_col,
            doc_row,
            query_scale[None],
            r * width,
        )
        for r in (1, 0)
    ][::-1]
    grad_qkv = [b[0] for b in backward]
    qkv_weights = [f[3] for f in forward]
    qkv_grads = [dot(normed_first, g, TN).astype(BF16) for g in grad_qkv]
    sent = dot(grad_qkv[0][rows:], qkv_weights[0], NT) + dot(grad_qkv[1][rows:], qkv_weights[1], NT)
    sent = swap(sent.astype(BF16), "core", 1)
    grad_normed_first = (
        dot(grad_qkv[0][:rows], qkv_weights[0], NT) + dot(grad_qkv[1][:rows], qkv_weights[1], NT) + sent.astype(F32)
    )
    unit_own, recip_own = unit_first[:rows], recip_first[:rows]
    scaled_first = grad_normed_first * gain_first
    attngain_part = jnp.sum(grad_normed_first * unit_own, axis=0)
    input_grad = (
        grad_resid
        + recip_own * (scaled_first - unit_own * jnp.mean(scaled_first * unit_own, axis=-1, keepdims=True))
    ).astype(BF16)
    qkv_grad = reduce_rows(qkv_grads[0], qkv_grads[1], rank)

    downbias_part = jnp.sum(cot_float, axis=0)
    features = sum_everywhere(jnp.concatenate([mlpgain_part, downbias_part]), ("core",))
    received = swap(jnp.concatenate([features, upbias_part[width:]]), "tx", 1)
    early = sum_everywhere(jnp.concatenate([features, upbias_part[:width]]) + received, ("fsdp",))
    scale_part = scale_base * jax.nn.sigmoid(dim_scale) * (backward[0][1][0] + backward[1][1][0])
    late = sum_everywhere(jnp.concatenate([attngain_part, scale_part]), ("core", "tx", "fsdp"))

    def own_shard(vector):
        return lax.dynamic_slice_in_dim(vector, rank * shard, shard, 0)

    return (
        layer_out,
        input_grad,
        qkv_grad.reshape(shard, 3, width),
        mlp_grad[:, :width].T,
        mlp_grad[:, width : 2 * width],
        early[2 * depth :],
        mlp_grad[:, 2 * width :].T,
        own_shard(early[depth : 2 * depth]),
        own_shard(late[:depth]),
        own_shard(early[:depth]),
        late[depth:],
    )


def solution(mesh):
    size, tensor = mesh.shape["fsdp"], mesh.shape["tensor"]
    split = Mesh(mesh.devices.reshape(size, tensor // 2, 2), ("fsdp", "tx", "core"))
    tokens = P(("fsdp", "tx", "core"), None)
    tensor_axes = ("tx", "core")
    in_specs = (
        tokens,
        P("fsdp"),
        P("fsdp", None, tensor_axes),
        P(tensor_axes, "fsdp"),
        P("fsdp", tensor_axes),
        P(tensor_axes),
        P(tensor_axes, "fsdp"),
        P("fsdp"),
        P("fsdp"),
        P("fsdp"),
        P(),
        tokens,
    )
    out_specs = (
        tokens,
        tokens,
        P("fsdp", None, tensor_axes),
        P(tensor_axes, "fsdp"),
        P("fsdp", tensor_axes),
        P(tensor_axes),
        P(tensor_axes, "fsdp"),
        P("fsdp"),
        P("fsdp"),
        P("fsdp"),
        P(),
    )
    return jax.shard_map(local, mesh=split, in_specs=in_specs, out_specs=out_specs, check_vma=False)
```

```python
import math

import jax
import jax.numpy as jnp
from jax import lax
from jax.experimental import pallas as pl
from jax.experimental.pallas import tpu as pltpu
from jax.sharding import Mesh
from jax.sharding import PartitionSpec as P

HD = 80
LEN = 1024
BQ = 256
NORM_EPS = 1e-06
PERDIM_BASE = 1.442695041
NEG_FILL = -1e30
VMEM_BYTES = 56 << 20
BF16 = jnp.bfloat16
F32 = jnp.float32
NT = (((1,), (1,)), ((), ()))
NN = (((1,), (0,)), ((), ()))
TN = (((0,), (0,)), ((), ()))


def dot(a, b, dims=NN):
    return lax.dot_general(a, b, dims, preferred_element_type=F32)


def swap(value, axis, bit):
    size = lax.axis_size(axis)
    return lax.ppermute(value, axis, [(i, i ^ bit) for i in range(size)])


def tie(value, *others):
    return lax.optimization_barrier((value, *others))[0] if others else value


def rms_scale(values):
    return lax.rsqrt(jnp.mean(values * values, axis=-1, keepdims=True) + NORM_EPS)


class Gather:
    def __init__(self, shard):
        self.whole = lax.axis_size("fsdp") != 8
        self.shard = shard

    def start(self, *after):
        shard = tie(self.shard, *after)
        if self.whole:
            gathered = lax.all_gather(shard, "fsdp", axis=0, tiled=True)
            self.own, self.other = [(gathered, 0, 0)], [(swap(gathered, "tx", 1), 0, 0)]
            self.along_z = self.along_xy = self.last = self.ready = (gathered,)
            return
        self.along_z = tuple(swap(shard, "fsdp", 2 * j) for j in (1, 2, 3))

    def middle(self, *after):
        if self.whole:
            return
        stacked = jnp.stack((self.shard, tie(self.along_z[0], *after), *self.along_z[1:]))
        self.ready = (stacked,)
        self.along_xy = (swap(stacked, "fsdp", 1), swap(stacked, "tx", 1))
        self.own = [(stacked, 0, 0), (self.along_xy[0], 1, 0)]

    def finish(self, *after):
        if self.whole:
            return
        half = self.shard.shape[0] // 2
        from_y, from_x = tie(self.along_xy[0], *after), tie(self.along_xy[1], *after)
        self.last = (swap(from_y[:, :half], "tx", 1), swap(from_x[:, half:], "fsdp", 1))
        self.other = [(self.along_xy[1], 0, 0), (self.last[0], 1, 0), (self.last[1], 1, half)]


class Reduction:
    def __init__(self):
        self.whole = lax.axis_size("fsdp") != 8

    def send_far(self, other):
        self.other = other
        if self.whole:
            self.sent_far = other
            return
        self.sent_far = (swap(other[0], "tx", 1), swap(other[1], "fsdp", 1))

    def split(self, count):
        parts = [Reduction() for _ in range(count)]
        for c, p in enumerate(parts):
            if self.whole:
                p.other = p.sent_far = (self.other[c],)
            else:
                p.sent_far = tuple(r[c] for r in self.sent_far)
                p.other = (None, None, self.other[2 + c])
        return parts

    def send_xy(self, own, *after):
        self.own = own
        if self.whole:
            self.from_x, self.from_y = swap(self.other[0], "tx", 1), own[0]
            self.ready = (own[0],)
            return
        self.ready = add_halves(self.other[2], own[0], self.sent_far, after)
        self.from_x, self.from_y = swap(self.ready[0], "tx", 1), swap(self.ready[1], "fsdp", 1)

    def send_z(self, *after):
        if self.whole:
            total = self.own[0] + tie(self.from_x, *after)
            self.ready = (total,)
            self.parts = (lax.psum_scatter(total, "fsdp", scatter_dimension=0, tiled=True),)
            return
        from_x = tie(self.from_x, *after)
        both = (self.own[1].astype(F32) + from_x.astype(F32) + self.from_y.astype(F32)).astype(BF16)
        self.ready = (both,)
        self.parts = (both[0], *(swap(both[j], "fsdp", 2 * j) for j in (1, 2, 3)))

    def total(self):
        return sum(piece.astype(F32) for piece in self.parts)


def add_halves(near, far, sent_far, after):
    def kernel(near, far, from_x, from_y, along_x, along_y):
        half = near.shape[1] // 2
        along_x[:, :half] = near[:, :half]
        along_x[:, half:] = (near[:, half:].astype(F32) + from_y[...].astype(F32)).astype(BF16)
        along_y[:, :half] = (far[:, :half].astype(F32) + from_x[...].astype(F32)).astype(BF16)
        along_y[:, half:] = far[:, half:]

    out_shape = (jax.ShapeDtypeStruct(near.shape, BF16), jax.ShapeDtypeStruct(far.shape, BF16))
    return call(kernel, "add_halves", [VMEM] * 4, out_shape, [], 1, tie(near, *after), far, *sent_far)


def sum_fsdp(value):
    size = lax.axis_size("fsdp")
    if size != 8:
        return lax.psum(value, "fsdp")
    value = value + swap(value, "fsdp", 1)
    return value + sum(swap(value, "fsdp", 2 * j) for j in (1, 2, 3))


VMEM = pl.BlockSpec(memory_space=pltpu.VMEM)
SMEM = pl.BlockSpec(memory_space=pltpu.SMEM)
ANY = pl.BlockSpec(memory_space=pl.ANY)


def call(kernel, name, in_specs, out_shape, scratch_shapes, micros, *args):
    return pl.pallas_call(
        kernel,
        in_specs=in_specs,
        out_specs=jax.tree.map(lambda _: VMEM, out_shape),
        out_shape=out_shape,
        scratch_shapes=scratch_shapes,
        compiler_params=pltpu.CompilerParams(vmem_limit_bytes=VMEM_BYTES),
        cost_estimate=pl.CostEstimate(flops=int(micros * 1e6), bytes_accessed=1 << 10, transcendentals=0),
        name=name,
    )(*args)


def piece_copies(pieces, places, weight, sems, rank):
    if len(pieces) == 1:
        return [pltpu.make_async_copy(pieces[0], weight, sems.at[0])]
    shard = weight.shape[0] // 8
    copies = []
    for piece, (yj, first) in zip(pieces, places):
        for zj in range(4):
            start = pl.multiple_of((rank ^ (2 * zj + yj)) * shard + first, 16)
            target = weight.at[pl.ds(start, piece.shape[1])]
            copies.append(pltpu.make_async_copy(piece.at[zj], target, sems.at[len(copies)]))
    return copies


def far_shapes(depth, cols, size, own, parts=1):
    if size != 8:
        return (jax.ShapeDtypeStruct((depth, cols // parts), BF16),) * parts
    rows = depth // 8
    near = (jax.ShapeDtypeStruct((4, rows, cols // parts), BF16),) * parts
    if own:
        return (*near, *near)
    lead = (parts,) if parts > 1 else ()
    return (jax.ShapeDtypeStruct((*lead, 4, rows // 2, cols // parts), BF16),) * 2 + near


def put_pieces(refs, block, start, rank, own, part=None):
    if len(refs) == 1 or (part is not None and len(refs) == 2):
        refs[part or 0][start : start + block.shape[0], :] = block
        return
    near = refs[1] if own else refs[2 + (part or 0)]
    rows = near.shape[1]
    for n in range(block.shape[0] // rows):
        j = (start // rows + n) ^ rank
        yj, zj = j & 1, j >> 1
        piece = block[n * rows : (n + 1) * rows]

        @pl.when(yj == 0)
        def _():
            near[zj] = piece

        @pl.when(yj == 1)
        def _():
            if own:
                refs[0][zj] = piece
            elif part is None:
                refs[0][zj] = piece[: rows // 2]
                refs[1][zj] = piece[rows // 2 :]
            else:
                refs[0][part, zj] = piece[: rows // 2]
                refs[1][part, zj] = piece[rows // 2 :]


def assemble(place, gather, depth, name):
    lists = (gather.own, gather.other)
    arrays = [[p[0] for p in pieces] for pieces in lists]
    places = [[p[1:] for p in pieces] for pieces in lists]
    cols = arrays[0][0].shape[-1]
    width = 320
    parts = cols // width

    def kernel(place, *refs):
        pieces, outs, held, sems = refs[: -parts - 2], refs[-parts - 2 : -2], refs[-2], refs[-1]
        copies, at = [], 0
        for r in range(2):
            count = len(arrays[r])
            copies += piece_copies(pieces[at : at + count], places[r], held.at[r], sems.at[r], place[1])
            at += count
        for copy in copies:
            copy.start()
        for copy in copies:
            copy.wait()
        for n, out in enumerate(outs):
            out[...] = jnp.concatenate([held[r, :, n * width : (n + 1) * width] for r in range(2)], axis=1)

    out_shape = tuple(jax.ShapeDtypeStruct((depth, 2 * width), BF16) for _ in range(parts))
    scratch = [pltpu.VMEM((2, depth, cols), BF16), pltpu.SemaphoreType.DMA((2, 16))]
    flat = arrays[0] + arrays[1]
    return call(kernel, name, [SMEM] + [ANY] * len(flat), out_shape, scratch, 3, place, *flat)


def mask_bias(doc_col, doc_row, bias):
    for i in range(LEN // BQ):
        lo, hi = i * BQ, (i + 1) * BQ
        same = doc_col[:hi, :] == doc_row[:, lo:hi]
        keys = lax.broadcasted_iota(jnp.int32, (hi, BQ), 0)
        queries = lax.broadcasted_iota(jnp.int32, (hi, BQ), 1) + lo
        bias[i, :hi, :] = jnp.where(same & (keys <= queries), 0.0, NEG_FILL)


def outer_rows(lo, rows, core):
    half = LEN // 2
    return pl.ds(pl.multiple_of(((lo // half) ^ core) * half + lo % half, rows), rows)


def attn_forward(place, pieces, rows_in, scale, doc_col, doc_row, chunks, depth):
    arrays, places = [p[0] for p in pieces], [p[1:] for p in pieces]
    cols = arrays[0].shape[-1]
    fresh = len(rows_in) == 2
    part = scale.shape[1] // 3
    heads = part // HD

    def kernel(place, *refs):
        pieces, refs = refs[: len(arrays)], refs[len(arrays) :]
        sources, (scale, doc_col, doc_row) = refs[: len(rows_in)], refs[len(rows_in) : len(rows_in) + 3]
        outs = refs[len(rows_in) + 3 :]
        attns, qkvs = outs[:chunks], outs[chunks : 2 * chunks]
        lse, weight = outs[2 * chunks : 2 * chunks + 2]
        if fresh:
            x, gains, bias, sems = outs[2 * chunks + 2 :]
        else:
            x, bias, sems = outs[2 * chunks + 2 :]
        core, rank = place[0], place[1]
        copies = piece_copies(pieces, places, weight, sems, rank)
        if not fresh:
            copies.append(pltpu.make_async_copy(sources[0], x, sems.at[len(copies)]))
        for copy in copies:
            copy.start()
        mask_bias(doc_col, doc_row, bias)
        for copy in copies:
            copy.wait()
        if fresh:
            gains[...] = weight[:, cols - 128 :].astype(F32).T
            gain = gains[64:65, :]
            half = LEN // 2
            for i in range(LEN // BQ):
                lo = i * BQ
                values = sources[lo // half][lo % half : lo % half + BQ, :].astype(F32)
                x[lo : lo + BQ, :] = (values * rms_scale(values) * gain).astype(BF16)
        for i in range(LEN // BQ):
            lo = i * BQ
            block = dot(x[outer_rows(lo, BQ, core), :], weight[...])
            for c in range(chunks):
                wide = block[:, c * 3 * part : (c + 1) * 3 * part]
                qkvs[c][lo : lo + BQ, :] = (wide * scale[...]).astype(BF16)
        for c in range(chunks):
            qkv = qkvs[c]
            done = []
            for h in range(heads):
                key = qkv[:, part + h * HD : part + (h + 1) * HD]
                value_t = qkv[:, 2 * part + h * HD : 2 * part + (h + 1) * HD].T
                blocks = []
                for i in range(LEN // BQ):
                    lo, hi = i * BQ, (i + 1) * BQ
                    query = qkv[lo:hi, h * HD : (h + 1) * HD]
                    scores = dot(key[:hi], query, NT) + bias[i, :hi, :]
                    top = jnp.max(scores, axis=0, keepdims=True)
                    probs = jnp.exp(scores - top)
                    total = jnp.sum(probs, axis=0, keepdims=True)
                    blocks.append(dot(value_t[:, :hi], probs.astype(BF16)) / total)
                    row = c * heads + h
                    lse[row : row + 1, lo:hi] = top + jnp.log(total)
                done.append(jnp.concatenate(blocks, axis=1).T.astype(BF16))
            half = LEN // 2
            for a in range(2):
                attns[c][outer_rows(a * half, half, core), :] = jnp.concatenate(
                    [o[a * half : (a + 1) * half] for o in done], axis=1
                )

    out_shape = (
        *(jax.ShapeDtypeStruct((LEN, part), BF16),) * chunks,
        *(jax.ShapeDtypeStruct((LEN, 3 * part), BF16),) * chunks,
        jax.ShapeDtypeStruct((8, LEN), F32),
        jax.ShapeDtypeStruct((depth, cols), BF16),
    )
    scratch = [pltpu.VMEM((LEN // BQ, LEN, BQ), F32), pltpu.SemaphoreType.DMA((17,))]
    if fresh:
        out_shape += (jax.ShapeDtypeStruct((LEN, depth), BF16), jax.ShapeDtypeStruct((128, depth), F32))
    else:
        scratch = [pltpu.VMEM((LEN, depth), BF16)] + scratch
    specs = [SMEM] + [ANY] * len(arrays) + [VMEM if fresh else ANY] * len(rows_in) + [VMEM] * 3
    outs = call(
        kernel, "attn_forward", specs, out_shape, scratch, 8, place, *arrays, *rows_in, scale, doc_col, doc_row
    )
    return list(zip(outs[:chunks], outs[chunks : 2 * chunks])), outs[2 * chunks :]


def attn_backward(place, saved, lse, dout, x, doc_col, doc_row, scale, first, own):
    part = saved[0][1].shape[1]
    heads = part // HD
    count = len(saved)
    depth = x.shape[1]
    pieces_shape = far_shapes(depth, 3 * part * count, lax.axis_size("fsdp"), own, count)

    def kernel(place, *refs):
        saved_refs = [(saved[n][0], refs[2 * n], refs[2 * n + 1]) for n in range(count)]
        lse, dout, x_far, doc_col, doc_row, scale, *refs = refs[2 * count :]
        grads_out, sums_out, refs = refs[:count], refs[count], refs[count + 1 :]
        pieces, (x, dkey, dvalue, bias, sem) = refs[:-5], refs[-5:]
        copy = pltpu.make_async_copy(x_far, x, sem)
        copy.start()
        core, rank = place[0], place[1]
        lanes = lax.broadcasted_iota(jnp.int32, (8, part), 1) // HD
        selector = jnp.where(lanes == lax.broadcasted_iota(jnp.int32, (8, part), 0), 1.0, 0.0)
        mask_bias(doc_col, doc_row, bias)
        sums = jnp.zeros((1, HD), F32)
        for n, (c, attn, qkv) in enumerate(saved_refs):
            douts, deltas = [], []
            for i in range(LEN // BQ):
                rows = outer_rows(i * BQ, BQ, core)
                dout_block = dout[rows, first + c * part : first + (c + 1) * part]
                products = attn[rows, :].astype(F32) * dout_block.astype(F32)
                deltas.append(
                    lax.dot_general(
                        selector, products, NT, precision=lax.Precision.HIGHEST, preferred_element_type=F32
                    )
                )
                douts.append(dout_block)
            grads = [[], [], []]
            for h in range(heads):
                key = qkv[:, part + h * HD : part + (h + 1) * HD]
                key_t = key.T
                row = c * heads + h
                dquery_parts = []
                for i in range(LEN // BQ):
                    lo, hi = i * BQ, (i + 1) * BQ
                    query = qkv[lo:hi, h * HD : (h + 1) * HD]
                    value = qkv[:hi, 2 * part + h * HD : 2 * part + (h + 1) * HD]
                    dout_head = douts[i][:, h * HD : (h + 1) * HD]
                    scores = dot(key[:hi], query, NT) + bias[i, :hi, :]
                    probs = jnp.exp(scores - lse[row : row + 1, lo:hi])
                    dprobs = dot(value, dout_head, NT)
                    dscores = (probs * (dprobs - deltas[i][h : h + 1, :])).astype(BF16)
                    dv = dot(probs.astype(BF16), dout_head)
                    dk = dot(dscores, query)
                    dquery_parts.append(dot(key_t[:, :hi], dscores))
                    if i:
                        dkey[:lo] += dk[:lo]
                        dvalue[:lo] += dv[:lo]
                    dkey[lo:hi] = dk[lo:]
                    dvalue[lo:hi] = dv[lo:]
                dquery = jnp.concatenate(dquery_parts, axis=1).T
                query = qkv[:, h * HD : (h + 1) * HD].astype(F32)
                sums = sums + jnp.sum(dquery * query, axis=0, keepdims=True)
                grads[0].append((dquery * scale[...]).astype(BF16))
                grads[1].append(dkey[...].astype(BF16))
                grads[2].append(dvalue[...].astype(BF16))
            joined = jnp.concatenate(grads[0] + grads[1] + grads[2], axis=1)
            half = LEN // 2
            for a in range(2):
                grads_out[n][outer_rows(a * half, half, core), :] = joined[a * half : (a + 1) * half]
            if n == 0:
                copy.wait()
            for g in range(2):
                start = g * depth // 2
                block = dot(x[:, start : start + depth // 2], grads_out[n][...], TN).astype(BF16)
                put_pieces(pieces, block, start, rank, own, n if count > 1 else None)
        sums_out[...] = sums / scale[...]

    out_shape = (
        *(jax.ShapeDtypeStruct(s[2].shape, BF16) for s in saved),
        jax.ShapeDtypeStruct((1, HD), F32),
        *pieces_shape,
    )
    scratch = [
        pltpu.VMEM(x.shape, BF16),
        pltpu.VMEM((LEN, HD), F32),
        pltpu.VMEM((LEN, HD), F32),
        pltpu.VMEM((LEN // BQ, LEN, BQ), F32),
        pltpu.SemaphoreType.DMA(()),
    ]
    args = [a for s in saved for a in s[1:]]
    specs = [SMEM] + [VMEM] * (len(args) + 2) + [ANY] + [VMEM] * 3
    outs = call(
        kernel, "attn_backward", specs, out_shape, scratch, 10, place, *args, lse, dout, x, doc_col, doc_row, scale
    )
    return outs[:count], outs[count], outs[count + 1 :]


def put_both(outs, block, start, rank, size):
    width = block.shape[1] // 2
    count = len(outs) // 2 if size != 8 else 2
    put_pieces(outs[:count], block[:, :width], start, rank, True)
    put_pieces(outs[count:], block[:, width:], start, rank, False)


def weight_grads(place, pairs, name):
    rows, depth = pairs[0][0][0].shape
    width = pairs[0][1].shape[1] // 2
    size = lax.axis_size("fsdp")
    shapes = [far_shapes(depth, width * len(pairs), size, own) for own in (True, False)]

    def kernel(place, *refs):
        ins, outs = refs[: 3 * len(pairs)], refs[3 * len(pairs) :]
        for g in range(2):
            cols = slice(g * depth // 2, (g + 1) * depth // 2)
            blocks = []
            for n in range(len(pairs)):
                near, far, right = ins[3 * n : 3 * n + 3]
                block = dot(near[:, cols], right[:rows, :], TN) + dot(far[:, cols], right[rows:, :], TN)
                blocks.append(block.astype(BF16))
            joined = [b[:, r * width : (r + 1) * width] for r in range(2) for b in blocks]
            put_both(outs, jnp.concatenate(joined, axis=1), g * depth // 2, place[1], size)

    args = [a for halves, right in pairs for a in (*halves, right)]
    outs = call(
        kernel, name, [SMEM] + [VMEM] * len(args), (*shapes[0], *shapes[1]), [], 4 * len(pairs), place, *args
    )
    return outs[: len(shapes[0])], outs[len(shapes[0]) :]


def out_forward(attns, out_t, inputs):
    rows, depth = inputs.shape

    def kernel(*refs):
        attns, (out_t, inputs, sent, kept) = refs[:-4], refs[-4:]
        heads = jnp.concatenate([a[...] for a in attns], axis=1)
        for i in range(rows // BQ):
            lo, hi = i * BQ, (i + 1) * BQ
            sent[lo:hi, :] = dot(heads[rows + lo : rows + hi], out_t[...], NT).astype(BF16)
            kept[lo:hi, :] = inputs[lo:hi, :].astype(F32) + dot(heads[lo:hi], out_t[...], NT)

    out_shape = (jax.ShapeDtypeStruct((rows, depth), BF16), jax.ShapeDtypeStruct((rows, depth), F32))
    return call(kernel, "out_forward", [VMEM] * (len(attns) + 2), out_shape, [], 3, *attns, out_t, inputs)


def second_norm(kept, received, gain):
    def kernel(kept, received, gain, resid_out, normed_out):
        resid = kept[...] + received[...].astype(F32)
        resid_out[...] = resid
        normed_out[...] = (resid * rms_scale(resid) * gain[...]).astype(BF16)

    out_shape = (jax.ShapeDtypeStruct(kept.shape, F32), jax.ShapeDtypeStruct(kept.shape, BF16))
    return call(kernel, "second_norm", [VMEM] * 3, out_shape, [], 1, kept, received, gain)


def mlp(normed, cot, up, down_t, bias_up):
    rows, depth = normed[0].shape
    units = up.shape[1]

    def kernel(n_near, n_far, c_near, c_far, up, down_t, bias, hidden, grad_pre, bias_sum, *outs):
        sums = jnp.zeros((1, units), F32)
        for i in range(2 * rows // BQ):
            n, c = (n_near, c_near) if i < rows // BQ else (n_far, c_far)
            out_mlp, out_grad = outs[:2] if i < rows // BQ else outs[2:]
            lo, hi = i * BQ, (i + 1) * BQ
            block = slice(lo % rows, lo % rows + BQ)
            pre = dot(n[block, :], up[...]) + bias[...]
            sig = 1.0 / (1.0 + jnp.exp(-pre))
            units_low = (pre * sig).astype(BF16)
            grad = dot(c[block, :], down_t[...])
            grad_low = (grad * (sig + pre * sig * (1.0 - sig))).astype(BF16)
            hidden[lo:hi, :] = units_low
            grad_pre[lo:hi, :] = grad_low
            sums = sums + jnp.sum(grad_low.astype(F32), axis=0, keepdims=True)
            out_mlp[block, :] = dot(units_low, down_t[...], NT).astype(BF16)
            out_grad[block, :] = dot(grad_low, up[...], NT).astype(BF16)
        bias_sum[...] = sums

    low = jax.ShapeDtypeStruct((rows, depth), BF16)
    out_shape = (
        jax.ShapeDtypeStruct((2 * rows, units), BF16),
        jax.ShapeDtypeStruct((2 * rows, units), BF16),
        jax.ShapeDtypeStruct((1, units), F32),
        low,
        low,
        low,
        low,
    )
    return call(kernel, "mlp", [VMEM] * 7, out_shape, [], 10, *normed, *cot, up, down_t, bias_up)


def resid_grads(grads, mlps, resid, cot, gain, bias):
    def kernel(grad_near, grad_far, mlp_near, mlp_far, resid, cot, gain, bias, grad_out, low_out, sum_out, layer):
        for i in range(resid.shape[0] // BQ):
            block = slice(i * BQ, (i + 1) * BQ)
            held = resid[block, :]
            grad = grad_near[block, :].astype(F32) + grad_far[block, :].astype(F32)
            recip = rms_scale(held)
            unit = held * recip
            part = jnp.sum(grad * unit, axis=0, keepdims=True)
            sum_out[...] = part if i == 0 else sum_out[...] + part
            scaled = grad * gain[...]
            mean = jnp.mean(scaled * unit, axis=-1, keepdims=True)
            total = cot[block, :].astype(F32) + recip * (scaled - unit * mean)
            grad_out[block, :] = total
            low_out[block, :] = total.astype(BF16)
            mlp = mlp_near[block, :].astype(F32) + mlp_far[block, :].astype(F32)
            layer[block, :] = (held + mlp + bias[...]).astype(BF16)

    out_shape = (
        jax.ShapeDtypeStruct(resid.shape, F32),
        jax.ShapeDtypeStruct(resid.shape, BF16),
        jax.ShapeDtypeStruct((1, resid.shape[1]), F32),
        jax.ShapeDtypeStruct(resid.shape, BF16),
    )
    return call(kernel, "resid_grads", [VMEM] * 8, out_shape, [], 2, *grads, *mlps, resid, cot, gain, bias)


def head_grads(place, grads, out_t, attns):
    rows, depth = grads[0].shape
    width = out_t.shape[1] // 2
    size = lax.axis_size("fsdp")
    shapes = [far_shapes(depth, width, size, own) for own in (True, False)]

    def kernel(place, near, far, out_t, *refs):
        attns, heads_out, pieces = refs[: len(attns_in)], refs[len(attns_in)], refs[len(attns_in) + 1 :]
        for i in range(2 * rows // BQ):
            source = near if i < rows // BQ else far
            block = slice(i * BQ % rows, i * BQ % rows + BQ)
            heads_out[i * BQ : (i + 1) * BQ, :] = dot(source[block, :], out_t[...]).astype(BF16)
        heads = jnp.concatenate([a[...] for a in attns], axis=1)
        for g in range(2):
            cols = slice(g * depth // 2, (g + 1) * depth // 2)
            block = (dot(near[:, cols], heads[:rows], TN) + dot(far[:, cols], heads[rows:], TN)).astype(BF16)
            put_both(pieces, block, g * depth // 2, place[1], size)

    attns_in = attns
    out_shape = (jax.ShapeDtypeStruct((2 * rows, 2 * width), BF16), *shapes[0], *shapes[1])
    outs = call(
        kernel, "head_grads", [SMEM] + [VMEM] * (3 + len(attns)), out_shape, [], 6, place, *grads, out_t, *attns
    )
    return outs[0], outs[1 : 1 + len(shapes[0])], outs[1 + len(shapes[0]) :]


def input_grads(grads, weights, rows):
    depth = weights[0].shape[0]
    counts = [len(g) for g in grads]

    def kernel(*refs):
        ins, weights, (sent, kept) = refs[: sum(counts)], refs[sum(counts) : -2], refs[-2:]
        for i in range(2 * rows // BQ):
            total, at = None, 0
            block = slice(i * BQ, (i + 1) * BQ)
            for count, weight in zip(counts, weights):
                left = jnp.concatenate([g[block, :] for g in ins[at : at + count]], axis=1)
                at += count
                partial = dot(left, weight[:, : left.shape[1]], NT)
                total = partial if total is None else total + partial
            if i < rows // BQ:
                kept[block, :] = total
            else:
                sent[i * BQ - rows : (i + 1) * BQ - rows, :] = total.astype(BF16)

    out_shape = (jax.ShapeDtypeStruct((rows, depth), BF16), jax.ShapeDtypeStruct((rows, depth), F32))
    flat = [g for pair in grads for g in pair]
    return call(
        kernel, "input_grads", [VMEM] * (len(flat) + len(weights)), out_shape, [], 10, *flat, *weights
    )


def first_norm_grads(kept, received, inputs, resid_grad, gain):
    def kernel(kept, received, inputs, resid_grad, gain, grad_out, sum_out):
        for i in range(inputs.shape[0] // BQ):
            block = slice(i * BQ, (i + 1) * BQ)
            values = inputs[block, :].astype(F32)
            recip = rms_scale(values)
            unit = values * recip
            grad = kept[block, :] + received[block, :].astype(F32)
            part = jnp.sum(grad * unit, axis=0, keepdims=True)
            sum_out[...] = part if i == 0 else sum_out[...] + part
            scaled = grad * gain[...]
            mean = jnp.mean(scaled * unit, axis=-1, keepdims=True)
            grad_out[block, :] = (resid_grad[block, :] + recip * (scaled - unit * mean)).astype(BF16)

    out_shape = (jax.ShapeDtypeStruct(inputs.shape, BF16), jax.ShapeDtypeStruct((1, inputs.shape[1]), F32))
    return call(kernel, "first_norm_grads", [VMEM] * 5, out_shape, [], 2, kept, received, inputs, resid_grad, gain)


def join_chunks(parts, width):
    counts = [len(p) for p in parts]
    shard = parts[0][0].shape[0]
    part = parts[0][0].shape[1] // 3

    def kernel(*refs):
        at = 0
        sums = []
        for count in counts:
            sums.append(sum(ref[...].astype(F32) for ref in refs[at : at + count]))
            at += count
        for i in range(3):
            refs[-1][i] = jnp.concatenate([total[:, i * part : (i + 1) * part] for total in sums], axis=1)

    flat = [p for pieces in parts for p in pieces]
    out_shape = jax.ShapeDtypeStruct((3, shard, width), F32)
    return call(kernel, "join_chunks", [VMEM] * len(flat), out_shape, [], 1, *flat)


def local(
    inputs,
    doc_ids,
    w_qkv,
    w_out,
    w_up,
    up_bias,
    w_down,
    down_bias,
    attn_gain,
    mlp_gain,
    dim_scale,
    cotangent,
):
    shard, _, width = w_qkv.shape
    size = lax.axis_size("fsdp")
    depth = shard * size
    rows = inputs.shape[0]
    core, tx, rank = lax.axis_index("core"), lax.axis_index("tx"), lax.axis_index("fsdp")
    place = jnp.stack([core, rank]).astype(jnp.int32)

    chunks = 2
    heads = width // HD
    part = width // chunks
    parts = [w_qkv[:, :, c * part : (c + 1) * part].reshape(shard, 3 * part) for c in range(chunks)]
    vectors = jnp.stack([attn_gain, mlp_gain, down_bias], axis=1)
    qkv = Gather(jnp.concatenate([*parts, vectors, jnp.zeros((shard, 61), F32)], axis=1).astype(BF16))
    rest = Gather(jnp.concatenate([w_out.T, w_up, w_down.T], axis=1).astype(BF16))
    qkv.start()

    input_rows = (inputs, swap(inputs, "core", 1))
    cots = (cotangent, swap(cotangent, "core", 1))
    docs = lax.dynamic_slice_in_dim(doc_ids, tx * LEN, LEN, 0)
    doc_col, doc_row = docs[:, None], docs[None, :]
    scale_base = PERDIM_BASE / math.sqrt(HD)
    query_scale = scale_base * jax.nn.softplus(dim_scale)
    colscale = jnp.concatenate([jnp.tile(query_scale, heads // chunks), jnp.ones((2 * part,), F32)])[None]

    now = (*qkv.along_z, input_rows[1], cots[1])
    qkv.middle(*now)
    rest.start(*now)
    now = (*qkv.along_xy, *rest.along_z)
    qkv.finish(*now)
    own_heads, (lse_own, weight_own, normed_first, gains) = attn_forward(
        place, qkv.own, (tie(inputs, *now), input_rows[1]), colscale, doc_col, doc_row, chunks, depth
    )
    now = (lse_own, *qkv.last)
    rest.middle(*now)
    bias_far = swap(tie(up_bias, *now), "tx", 1)
    other_heads, (lse_other, weight_other) = attn_forward(
        place, qkv.other, (tie(normed_first, *now, *rest.ready),), colscale, doc_col, doc_row, chunks, depth
    )
    now = (lse_other, *rest.along_xy, bias_far)
    rest.finish(*now)
    bias_up = jnp.concatenate([up_bias, bias_far])[None]
    attns = [pair[0] for pair in own_heads + other_heads]
    gain_first, gain_second, bias_second = [gains[64 + i : 65 + i] for i in range(3)]
    out_t, up, down_t = assemble(place, rest, depth, "assemble")
    sent, kept = out_forward(attns, out_t, inputs)
    resid_first, normed_own = second_norm(kept, swap(sent, "core", 1), gain_second)
    normeds = (normed_own, swap(normed_own, "core", 1))
    hidden, grad_pre, upbias_sum, mlp_kept, grad_kept, mlp_sent, grad_sent = mlp(normeds, cots, up, down_t, bias_up)
    grads = (grad_kept, swap(grad_sent, "core", 1))
    mlps = (mlp_kept, swap(mlp_sent, "core", 1))
    updown_own, updown_other = weight_grads(place, [(normeds, grad_pre), (cots, hidden)], "updown_grads")
    updown, out, both = Reduction(), Reduction(), Reduction()
    now = (updown_own[-1], grads[1], mlps[1])
    updown.send_far([tie(p, *now) for p in updown_other[:2]] + list(updown_other[2:]))
    grad_resid, grad_own, mlpgain_sum, layer_out = resid_grads(
        (tie(grad_kept, *now), grads[1]), mlps, resid_first, cotangent, gain_second, bias_second
    )
    now = (grad_own, *updown.sent_far)
    grad_attn = (grad_own, swap(tie(grad_own, *now), "core", 1))
    updown.send_xy(updown_own, *now)
    grad_heads, out_own, out_other = head_grads(
        place, (tie(grad_own, *now, *updown.ready), grad_attn[1]), out_t, attns
    )
    out.send_far(out_other)

    def back(pairs, which, lse, first_col, own, *now):
        saved = [(c, *pairs[c]) for c in which]
        return attn_backward(
            place, saved, lse, tie(grad_heads, *now), normed_first, doc_col, doc_row, query_scale[None], first_col, own
        )

    grad_other, sums_other, pieces_other = back(other_heads, range(chunks), lse_other, width, False, out_own[0])
    now = (sums_other, *out.sent_far, updown.from_x, updown.from_y)
    both.send_far([tie(p, *now) for p in pieces_other[:2]] + list(pieces_other[2:]))
    updown.send_z(*now)
    grad_first, sums_first, pieces_first = back(own_heads, [0], lse_own, 0, True, *now, *updown.ready)
    now = (sums_first, *both.sent_far, *updown.parts[1:])
    first, second = both.split(chunks)
    first.send_xy(pieces_first, *now)
    grad_second, sums_second, pieces_second = back(own_heads, [1], lse_own, 0, True, *now, *first.ready)
    now = (sums_second, first.from_x, first.from_y)
    second.send_xy(pieces_second, *now)
    first.send_z(*now)
    sent, kept = input_grads(
        [[tie(grad_first[0], *now, *second.ready, *first.ready), grad_second[0]], list(grad_other)],
        [weight_own, weight_other], rows,
    )
    now = (sent, second.from_x, second.from_y, *first.parts[1:])
    received = swap(tie(sent, *now), "core", 1)
    second.send_z(*now)
    input_grad, attngain_sum = first_norm_grads(
        tie(kept, *now, *second.ready), received, inputs, grad_resid, gain_first
    )
    out.send_xy(out_own, attngain_sum)
    attngain_part = tie(attngain_sum[0], *out.ready)
    out.send_z(*second.parts[1:])

    downbias_part = jnp.sum(cotangent.astype(F32), axis=0)
    scale_part = scale_base * jax.nn.sigmoid(dim_scale) * (sums_other + sums_first + sums_second)[0]
    features = jnp.concatenate([mlpgain_sum[0], downbias_part, attngain_part, scale_part])
    features = features + swap(features, "core", 1)
    received = swap(jnp.concatenate([features, upbias_sum[0, width:]]), "tx", 1)
    sums = sum_fsdp(jnp.concatenate([features, upbias_sum[0, :width]]) + received)

    def own_shard(index):
        return lax.dynamic_slice_in_dim(sums, index * depth + rank * shard, shard, 0)

    updown_grad, out_grad = updown.total(), out.total()
    qkv_grad = join_chunks([first.parts, second.parts], width)
    return (
        layer_out,
        input_grad,
        jnp.transpose(qkv_grad, (1, 0, 2)),
        out_grad.T,
        updown_grad[:, :width],
        sums[3 * depth + HD :],
        updown_grad[:, width:].T,
        own_shard(1),
        own_shard(2),
        own_shard(0),
        sums[3 * depth : 3 * depth + HD],
    )


def solution(mesh):
    size, tensor = mesh.shape["fsdp"], mesh.shape["tensor"]
    split = Mesh(mesh.devices.reshape(size, tensor // 2, 2), ("fsdp", "tx", "core"))
    tokens = P(("fsdp", "tx", "core"), None)
    tensor_axes = ("tx", "core")
    in_specs = (
        tokens,
        P("fsdp"),
        P("fsdp", None, tensor_axes),
        P(tensor_axes, "fsdp"),
        P("fsdp", tensor_axes),
        P(tensor_axes),
        P(tensor_axes, "fsdp"),
        P("fsdp"),
        P("fsdp"),
        P("fsdp"),
        P(),
        tokens,
    )
    out_specs = (
        tokens,
        tokens,
        P("fsdp", None, tensor_axes),
        P(tensor_axes, "fsdp"),
        P("fsdp", tensor_axes),
        P(tensor_axes),
        P(tensor_axes, "fsdp"),
        P("fsdp"),
        P("fsdp"),
        P("fsdp"),
        P(),
    )
    return jax.shard_map(local, mesh=split, in_specs=in_specs, out_specs=out_specs, check_vma=False)
```

```python
import math

import jax
import jax.numpy as jnp
from jax import lax
from jax.experimental import pallas as pl
from jax.experimental.pallas import tpu as pltpu
from jax.sharding import Mesh
from jax.sharding import PartitionSpec as P

HD = 80
LEN = 1024
BQ = 256
NORM_EPS = 1e-06
PERDIM_BASE = 1.442695041
NEG_FILL = -1e30
VMEM_BYTES = 24 << 20
BF16 = jnp.bfloat16
F32 = jnp.float32
NT = (((1,), (1,)), ((), ()))
NN = (((1,), (0,)), ((), ()))
TN = (((0,), (0,)), ((), ()))


def dot(a, b, dims=NN):
    return lax.dot_general(a, b, dims, preferred_element_type=F32)


def swap(value, axis, bit):
    size = lax.axis_size(axis)
    return lax.ppermute(value, axis, [(i, i ^ bit) for i in range(size)])


def tie(value, *others):
    return lax.optimization_barrier((value, *others))[0] if others else value


def rms_scale(values):
    return lax.rsqrt(jnp.mean(values * values, axis=-1, keepdims=True) + NORM_EPS)


class Gather:
    def __init__(self, shard):
        self.whole = lax.axis_size("fsdp") != 8
        self.shard = shard

    def start(self, *after):
        shard = tie(self.shard, *after)
        if self.whole:
            gathered = lax.all_gather(shard, "fsdp", axis=0, tiled=True)
            self.own, self.other = [(gathered, 0, 0)], [(swap(gathered, "tx", 1), 0, 0)]
            self.along_z = self.along_xy = self.last = self.ready = (gathered,)
            return
        self.along_z = tuple(swap(shard, "fsdp", 2 * j) for j in (1, 2, 3))

    def middle(self, *after):
        if self.whole:
            return
        stacked = jnp.stack((self.shard, tie(self.along_z[0], *after), *self.along_z[1:]))
        self.ready = (stacked,)
        self.along_xy = (swap(stacked, "fsdp", 1), swap(stacked, "tx", 1))
        self.own = [(stacked, 0, 0), (self.along_xy[0], 1, 0)]

    def finish(self, *after):
        if self.whole:
            return
        half = self.shard.shape[0] // 2
        from_y, from_x = tie(self.along_xy[0], *after), tie(self.along_xy[1], *after)
        self.last = (swap(from_y[:, :half], "tx", 1), swap(from_x[:, half:], "fsdp", 1))
        self.other = [(self.along_xy[1], 0, 0), (self.last[0], 1, 0), (self.last[1], 1, half)]


class Reduction:
    def __init__(self):
        self.whole = lax.axis_size("fsdp") != 8

    def send_far(self, other):
        self.other = other
        if self.whole:
            self.sent_far = other
            return
        self.sent_far = (swap(other[0], "tx", 1), swap(other[1], "fsdp", 1))

    def split(self, count):
        parts = [Reduction() for _ in range(count)]
        for c, p in enumerate(parts):
            if self.whole:
                p.other = p.sent_far = (self.other[c],)
            else:
                p.sent_far = tuple(r[c] for r in self.sent_far)
                p.other = (None, None, self.other[2 + c])
        return parts

    def send_xy(self, own, *after):
        self.own = own
        if self.whole:
            self.from_x, self.from_y = swap(self.other[0], "tx", 1), own[0]
            self.ready = (own[0],)
            return
        self.ready = add_halves(self.other[2], own[0], self.sent_far, after)
        self.from_x, self.from_y = swap(self.ready[0], "tx", 1), swap(self.ready[1], "fsdp", 1)

    def send_z(self, *after):
        if self.whole:
            total = self.own[0] + tie(self.from_x, *after)
            self.ready = (total,)
            self.parts = (lax.psum_scatter(total, "fsdp", scatter_dimension=0, tiled=True),)
            return
        from_x = tie(self.from_x, *after)
        both = (self.own[1].astype(F32) + from_x.astype(F32) + self.from_y.astype(F32)).astype(BF16)
        self.ready = (both,)
        self.parts = (both[0], *(swap(both[j], "fsdp", 2 * j) for j in (1, 2, 3)))

    def total(self):
        return sum(piece.astype(F32) for piece in self.parts)


def add_halves(near, far, sent_far, after):
    def kernel(near, far, from_x, from_y, along_x, along_y):
        half = near.shape[1] // 2
        along_x[:, :half] = near[:, :half]
        along_x[:, half:] = (near[:, half:].astype(F32) + from_y[...].astype(F32)).astype(BF16)
        along_y[:, :half] = (far[:, :half].astype(F32) + from_x[...].astype(F32)).astype(BF16)
        along_y[:, half:] = far[:, half:]

    out_shape = (jax.ShapeDtypeStruct(near.shape, BF16), jax.ShapeDtypeStruct(far.shape, BF16))
    return call(kernel, "add_halves", [VMEM] * 4, out_shape, [], 1, tie(near, *after), far, *sent_far, near=True)


def sum_fsdp(value):
    size = lax.axis_size("fsdp")
    if size != 8:
        return lax.psum(value, "fsdp")
    value = value + swap(value, "fsdp", 1)
    return value + sum(swap(value, "fsdp", 2 * j) for j in (1, 2, 3))


VMEM = pl.BlockSpec(memory_space=pltpu.VMEM)
SMEM = pl.BlockSpec(memory_space=pltpu.SMEM)
ANY = pl.BlockSpec(memory_space=pl.ANY)


def call(kernel, name, in_specs, out_shape, scratch_shapes, micros, *args, near=False):
    if near:
        args = [pltpu.with_memory_space_constraint(a, pltpu.VMEM) if s is VMEM else a for a, s in zip(args, in_specs)]
        out_shape = jax.tree.map(lambda o: pltpu.VMEM(o.shape, o.dtype), out_shape)
    return pl.pallas_call(
        kernel,
        in_specs=in_specs,
        out_specs=jax.tree.map(lambda _: VMEM, out_shape),
        out_shape=out_shape,
        scratch_shapes=scratch_shapes,
        compiler_params=pltpu.CompilerParams(vmem_limit_bytes=VMEM_BYTES),
        cost_estimate=pl.CostEstimate(flops=int(micros * 1e6), bytes_accessed=1 << 10, transcendentals=0),
        name=name,
    )(*args)


def piece_copies(pieces, places, weight, sems, rank):
    if len(pieces) == 1:
        return [pltpu.make_async_copy(pieces[0], weight, sems.at[0])]
    shard = weight.shape[0] // 8
    copies = []
    for piece, (yj, first) in zip(pieces, places):
        for zj in range(4):
            start = pl.multiple_of((rank ^ (2 * zj + yj)) * shard + first, 16)
            target = weight.at[pl.ds(start, piece.shape[1])]
            copies.append(pltpu.make_async_copy(piece.at[zj], target, sems.at[len(copies)]))
    return copies


def far_shapes(depth, cols, size, own, parts=1):
    if size != 8:
        return (jax.ShapeDtypeStruct((depth, cols // parts), BF16),) * parts
    rows = depth // 8
    near = (jax.ShapeDtypeStruct((4, rows, cols // parts), BF16),) * parts
    if own:
        return (*near, *near)
    lead = (parts,) if parts > 1 else ()
    return (jax.ShapeDtypeStruct((*lead, 4, rows // 2, cols // parts), BF16),) * 2 + near


def put_pieces(refs, block, start, rank, own, part=None):
    if len(refs) == 1 or (part is not None and len(refs) == 2):
        refs[part or 0][start : start + block.shape[0], :] = block
        return
    near = refs[1] if own else refs[2 + (part or 0)]
    rows = near.shape[1]
    for n in range(block.shape[0] // rows):
        j = (start // rows + n) ^ rank
        yj, zj = j & 1, j >> 1
        piece = block[n * rows : (n + 1) * rows]

        @pl.when(yj == 0)
        def _():
            near[zj] = piece

        @pl.when(yj == 1)
        def _():
            if own:
                refs[0][zj] = piece
            elif part is None:
                refs[0][zj] = piece[: rows // 2]
                refs[1][zj] = piece[rows // 2 :]
            else:
                refs[0][part, zj] = piece[: rows // 2]
                refs[1][part, zj] = piece[rows // 2 :]


def assemble(place, gather, depth, name):
    lists = (gather.own, gather.other)
    arrays = [[p[0] for p in pieces] for pieces in lists]
    places = [[p[1:] for p in pieces] for pieces in lists]
    cols = arrays[0][0].shape[-1]
    width = 320
    parts = cols // width

    def kernel(place, *refs):
        pieces, outs, held, sems = refs[: -parts - 2], refs[-parts - 2 : -2], refs[-2], refs[-1]
        copies, at = [], 0
        for r in range(2):
            count = len(arrays[r])
            copies += piece_copies(pieces[at : at + count], places[r], held.at[r], sems.at[r], place[1])
            at += count
        for copy in copies:
            copy.start()
        for copy in copies:
            copy.wait()
        for n, out in enumerate(outs):
            out[...] = jnp.concatenate([held[r, :, n * width : (n + 1) * width] for r in range(2)], axis=1)

    out_shape = tuple(jax.ShapeDtypeStruct((depth, 2 * width), BF16) for _ in range(parts))
    scratch = [pltpu.VMEM((2, depth, cols), BF16), pltpu.SemaphoreType.DMA((2, 16))]
    flat = arrays[0] + arrays[1]
    return call(kernel, name, [SMEM] + [ANY] * len(flat), out_shape, scratch, 3, place, *flat)


def mask_bias(doc_col, doc_row, bias):
    for i in range(LEN // BQ):
        lo, hi = i * BQ, (i + 1) * BQ
        same = doc_col[:hi, :] == doc_row[:, lo:hi]
        keys = lax.broadcasted_iota(jnp.int32, (hi, BQ), 0)
        queries = lax.broadcasted_iota(jnp.int32, (hi, BQ), 1) + lo
        bias[i, :hi, :] = jnp.where(same & (keys <= queries), 0.0, NEG_FILL)


def outer_rows(lo, rows, core):
    half = LEN // 2
    return pl.ds(pl.multiple_of(((lo // half) ^ core) * half + lo % half, rows), rows)


def attn_forward(place, pieces, rows_in, scale, doc_col, doc_row, chunks, depth):
    arrays, places = [p[0] for p in pieces], [p[1:] for p in pieces]
    cols = arrays[0].shape[-1]
    fresh = len(rows_in) == 2
    part = scale.shape[1] // 3
    heads = part // HD

    def kernel(place, *refs):
        pieces, refs = refs[: len(arrays)], refs[len(arrays) :]
        sources, (scale, doc_col, doc_row) = refs[: len(rows_in)], refs[len(rows_in) : len(rows_in) + 3]
        outs = refs[len(rows_in) + 3 :]
        attns, qkvs = outs[:chunks], outs[chunks : 2 * chunks]
        lse, weight = outs[2 * chunks : 2 * chunks + 2]
        if fresh:
            x, gains, bias, sems = outs[2 * chunks + 2 :]
        else:
            x, bias, sems = outs[2 * chunks + 2 :]
        core, rank = place[0], place[1]
        copies = piece_copies(pieces, places, weight, sems, rank)
        if not fresh:
            copies.append(pltpu.make_async_copy(sources[0], x, sems.at[len(copies)]))
        for copy in copies:
            copy.start()
        mask_bias(doc_col, doc_row, bias)
        for copy in copies:
            copy.wait()
        if fresh:
            gains[...] = weight[:, cols - 128 :].astype(F32).T
            gain = gains[64:65, :]
            half = LEN // 2
            for i in range(LEN // BQ):
                lo = i * BQ
                values = sources[lo // half][lo % half : lo % half + BQ, :].astype(F32)
                x[lo : lo + BQ, :] = (values * rms_scale(values) * gain).astype(BF16)
        for i in range(LEN // BQ):
            lo = i * BQ
            block = dot(x[outer_rows(lo, BQ, core), :], weight[...])
            for c in range(chunks):
                wide = block[:, c * 3 * part : (c + 1) * 3 * part]
                qkvs[c][lo : lo + BQ, :] = (wide * scale[...]).astype(BF16)
        for c in range(chunks):
            qkv = qkvs[c]
            done = []
            for h in range(heads):
                key = qkv[:, part + h * HD : part + (h + 1) * HD]
                value_t = qkv[:, 2 * part + h * HD : 2 * part + (h + 1) * HD].T
                blocks = []
                for i in range(LEN // BQ):
                    lo, hi = i * BQ, (i + 1) * BQ
                    query = qkv[lo:hi, h * HD : (h + 1) * HD]
                    scores = dot(key[:hi], query, NT) + bias[i, :hi, :]
                    top = jnp.max(scores, axis=0, keepdims=True)
                    probs = jnp.exp(scores - top)
                    total = jnp.sum(probs, axis=0, keepdims=True)
                    blocks.append(dot(value_t[:, :hi], probs.astype(BF16)) / total)
                    row = c * heads + h
                    lse[row : row + 1, lo:hi] = top + jnp.log(total)
                done.append(jnp.concatenate(blocks, axis=1).T.astype(BF16))
            half = LEN // 2
            for a in range(2):
                attns[c][outer_rows(a * half, half, core), :] = jnp.concatenate(
                    [o[a * half : (a + 1) * half] for o in done], axis=1
                )

    out_shape = (
        *(jax.ShapeDtypeStruct((LEN, part), BF16),) * chunks,
        *(jax.ShapeDtypeStruct((LEN, 3 * part), BF16),) * chunks,
        jax.ShapeDtypeStruct((8, LEN), F32),
        jax.ShapeDtypeStruct((depth, cols), BF16),
    )
    scratch = [pltpu.VMEM((LEN // BQ, LEN, BQ), F32), pltpu.SemaphoreType.DMA((17,))]
    if fresh:
        out_shape += (jax.ShapeDtypeStruct((LEN, depth), BF16), jax.ShapeDtypeStruct((128, depth), F32))
    else:
        scratch = [pltpu.VMEM((LEN, depth), BF16)] + scratch
    specs = [SMEM] + [ANY] * len(arrays) + [VMEM if fresh else ANY] * len(rows_in) + [VMEM] * 3
    outs = call(
        kernel, "attn_forward", specs, out_shape, scratch, 8, place, *arrays, *rows_in, scale, doc_col, doc_row
    )
    return list(zip(outs[:chunks], outs[chunks : 2 * chunks])), outs[2 * chunks :]


def attn_backward(place, saved, lse, dout, x, doc_col, doc_row, scale, first, own):
    part = saved[0][1].shape[1]
    heads = part // HD
    count = len(saved)
    depth = x.shape[1]
    pieces_shape = far_shapes(depth, 3 * part * count, lax.axis_size("fsdp"), own, count)

    def kernel(place, *refs):
        saved_refs = [(saved[n][0], refs[2 * n], refs[2 * n + 1]) for n in range(count)]
        lse, dout, x_far, doc_col, doc_row, scale, *refs = refs[2 * count :]
        grads_out, sums_out, refs = refs[:count], refs[count], refs[count + 1 :]
        pieces, (x, dkey, dvalue, bias, sem) = refs[:-5], refs[-5:]
        copy = pltpu.make_async_copy(x_far, x, sem)
        copy.start()
        core, rank = place[0], place[1]
        lanes = lax.broadcasted_iota(jnp.int32, (8, part), 1) // HD
        selector = jnp.where(lanes == lax.broadcasted_iota(jnp.int32, (8, part), 0), 1.0, 0.0)
        mask_bias(doc_col, doc_row, bias)
        sums = jnp.zeros((1, HD), F32)
        for n, (c, attn, qkv) in enumerate(saved_refs):
            douts, deltas = [], []
            for i in range(LEN // BQ):
                rows = outer_rows(i * BQ, BQ, core)
                dout_block = dout[rows, first + c * part : first + (c + 1) * part]
                products = attn[rows, :].astype(F32) * dout_block.astype(F32)
                deltas.append(
                    lax.dot_general(
                        selector, products, NT, precision=lax.Precision.HIGHEST, preferred_element_type=F32
                    )
                )
                douts.append(dout_block)
            grads = [[], [], []]
            for h in range(heads):
                key = qkv[:, part + h * HD : part + (h + 1) * HD]
                key_t = key.T
                row = c * heads + h
                dquery_parts = []
                for i in range(LEN // BQ):
                    lo, hi = i * BQ, (i + 1) * BQ
                    query = qkv[lo:hi, h * HD : (h + 1) * HD]
                    value = qkv[:hi, 2 * part + h * HD : 2 * part + (h + 1) * HD]
                    dout_head = douts[i][:, h * HD : (h + 1) * HD]
                    scores = dot(key[:hi], query, NT) + bias[i, :hi, :]
                    probs = jnp.exp(scores - lse[row : row + 1, lo:hi])
                    dprobs = dot(value, dout_head, NT)
                    dscores = (probs * (dprobs - deltas[i][h : h + 1, :])).astype(BF16)
                    dv = dot(probs.astype(BF16), dout_head)
                    dk = dot(dscores, query)
                    dquery_parts.append(dot(key_t[:, :hi], dscores))
                    if i:
                        dkey[:lo] += dk[:lo]
                        dvalue[:lo] += dv[:lo]
                    dkey[lo:hi] = dk[lo:]
                    dvalue[lo:hi] = dv[lo:]
                dquery = jnp.concatenate(dquery_parts, axis=1).T
                query = qkv[:, h * HD : (h + 1) * HD].astype(F32)
                sums = sums + jnp.sum(dquery * query, axis=0, keepdims=True)
                grads[0].append((dquery * scale[...]).astype(BF16))
                grads[1].append(dkey[...].astype(BF16))
                grads[2].append(dvalue[...].astype(BF16))
            joined = jnp.concatenate(grads[0] + grads[1] + grads[2], axis=1)
            half = LEN // 2
            for a in range(2):
                grads_out[n][outer_rows(a * half, half, core), :] = joined[a * half : (a + 1) * half]
            if n == 0:
                copy.wait()
            for g in range(2):
                start = g * depth // 2
                block = dot(x[:, start : start + depth // 2], grads_out[n][...], TN).astype(BF16)
                put_pieces(pieces, block, start, rank, own, n if count > 1 else None)
        sums_out[...] = sums / scale[...]

    out_shape = (
        *(jax.ShapeDtypeStruct(s[2].shape, BF16) for s in saved),
        jax.ShapeDtypeStruct((1, HD), F32),
        *pieces_shape,
    )
    scratch = [
        pltpu.VMEM(x.shape, BF16),
        pltpu.VMEM((LEN, HD), F32),
        pltpu.VMEM((LEN, HD), F32),
        pltpu.VMEM((LEN // BQ, LEN, BQ), F32),
        pltpu.SemaphoreType.DMA(()),
    ]
    args = [a for s in saved for a in s[1:]]
    specs = [SMEM] + [VMEM] * (len(args) + 2) + [ANY] + [VMEM] * 3
    outs = call(
        kernel, "attn_backward", specs, out_shape, scratch, 10, place, *args, lse, dout, x, doc_col, doc_row, scale
    )
    return outs[:count], outs[count], outs[count + 1 :]


def put_both(outs, block, start, rank, size):
    width = block.shape[1] // 2
    count = len(outs) // 2 if size != 8 else 2
    put_pieces(outs[:count], block[:, :width], start, rank, True)
    put_pieces(outs[count:], block[:, width:], start, rank, False)


def weight_grads(place, pairs, name):
    rows, depth = pairs[0][0][0].shape
    width = pairs[0][1].shape[1] // 2
    size = lax.axis_size("fsdp")
    shapes = [far_shapes(depth, width * len(pairs), size, own) for own in (True, False)]

    def kernel(place, *refs):
        ins, outs = refs[: 3 * len(pairs)], refs[3 * len(pairs) :]
        for g in range(2):
            cols = slice(g * depth // 2, (g + 1) * depth // 2)
            blocks = []
            for n in range(len(pairs)):
                near, far, right = ins[3 * n : 3 * n + 3]
                block = dot(near[:, cols], right[:rows, :], TN) + dot(far[:, cols], right[rows:, :], TN)
                blocks.append(block.astype(BF16))
            joined = [b[:, r * width : (r + 1) * width] for r in range(2) for b in blocks]
            put_both(outs, jnp.concatenate(joined, axis=1), g * depth // 2, place[1], size)

    args = [a for halves, right in pairs for a in (*halves, right)]
    outs = call(
        kernel, name, [SMEM] + [VMEM] * len(args), (*shapes[0], *shapes[1]), [], 4 * len(pairs), place, *args, near=True
    )
    return outs[: len(shapes[0])], outs[len(shapes[0]) :]


def out_forward(attns, out_t, inputs):
    rows, depth = inputs.shape

    def kernel(*refs):
        attns, (out_t, inputs, sent, kept) = refs[:-4], refs[-4:]
        heads = jnp.concatenate([a[...] for a in attns], axis=1)
        for i in range(rows // BQ):
            lo, hi = i * BQ, (i + 1) * BQ
            sent[lo:hi, :] = dot(heads[rows + lo : rows + hi], out_t[...], NT).astype(BF16)
            kept[lo:hi, :] = inputs[lo:hi, :].astype(F32) + dot(heads[lo:hi], out_t[...], NT)

    out_shape = (jax.ShapeDtypeStruct((rows, depth), BF16), jax.ShapeDtypeStruct((rows, depth), F32))
    return call(kernel, "out_forward", [VMEM] * (len(attns) + 2), out_shape, [], 3, *attns, out_t, inputs, near=True)


def second_norm(kept, received, gain):
    def kernel(kept, received, gain, resid_out, normed_out):
        resid = kept[...] + received[...].astype(F32)
        resid_out[...] = resid
        normed_out[...] = (resid * rms_scale(resid) * gain[...]).astype(BF16)

    out_shape = (jax.ShapeDtypeStruct(kept.shape, F32), jax.ShapeDtypeStruct(kept.shape, BF16))
    return call(kernel, "second_norm", [VMEM] * 3, out_shape, [], 1, kept, received, gain, near=True)


def mlp(normed, cot, up, down_t, bias_up):
    rows, depth = normed[0].shape
    units = up.shape[1]

    def kernel(n_near, n_far, c_near, c_far, up, down_t, bias, hidden, grad_pre, bias_sum, *outs):
        sums = jnp.zeros((1, units), F32)
        for i in range(2 * rows // BQ):
            n, c = (n_near, c_near) if i < rows // BQ else (n_far, c_far)
            out_mlp, out_grad = outs[:2] if i < rows // BQ else outs[2:]
            lo, hi = i * BQ, (i + 1) * BQ
            block = slice(lo % rows, lo % rows + BQ)
            pre = dot(n[block, :], up[...]) + bias[...]
            sig = 1.0 / (1.0 + jnp.exp(-pre))
            units_low = (pre * sig).astype(BF16)
            grad = dot(c[block, :], down_t[...])
            grad_low = (grad * (sig + pre * sig * (1.0 - sig))).astype(BF16)
            hidden[lo:hi, :] = units_low
            grad_pre[lo:hi, :] = grad_low
            sums = sums + jnp.sum(grad_low.astype(F32), axis=0, keepdims=True)
            out_mlp[block, :] = dot(units_low, down_t[...], NT).astype(BF16)
            out_grad[block, :] = dot(grad_low, up[...], NT).astype(BF16)
        bias_sum[...] = sums

    low = jax.ShapeDtypeStruct((rows, depth), BF16)
    out_shape = (
        jax.ShapeDtypeStruct((2 * rows, units), BF16),
        jax.ShapeDtypeStruct((2 * rows, units), BF16),
        jax.ShapeDtypeStruct((1, units), F32),
        low,
        low,
        low,
        low,
    )
    return call(kernel, "mlp", [VMEM] * 7, out_shape, [], 10, *normed, *cot, up, down_t, bias_up, near=True)


def resid_grads(grads, mlps, resid, cot, gain, bias):
    def kernel(grad_near, grad_far, mlp_near, mlp_far, resid, cot, gain, bias, grad_out, low_out, sum_out, layer):
        for i in range(resid.shape[0] // BQ):
            block = slice(i * BQ, (i + 1) * BQ)
            held = resid[block, :]
            grad = grad_near[block, :].astype(F32) + grad_far[block, :].astype(F32)
            recip = rms_scale(held)
            unit = held * recip
            part = jnp.sum(grad * unit, axis=0, keepdims=True)
            sum_out[...] = part if i == 0 else sum_out[...] + part
            scaled = grad * gain[...]
            mean = jnp.mean(scaled * unit, axis=-1, keepdims=True)
            total = cot[block, :].astype(F32) + recip * (scaled - unit * mean)
            grad_out[block, :] = total
            low_out[block, :] = total.astype(BF16)
            mlp = mlp_near[block, :].astype(F32) + mlp_far[block, :].astype(F32)
            layer[block, :] = (held + mlp + bias[...]).astype(BF16)

    out_shape = (
        jax.ShapeDtypeStruct(resid.shape, F32),
        jax.ShapeDtypeStruct(resid.shape, BF16),
        jax.ShapeDtypeStruct((1, resid.shape[1]), F32),
        jax.ShapeDtypeStruct(resid.shape, BF16),
    )
    return call(kernel, "resid_grads", [VMEM] * 8, out_shape, [], 2, *grads, *mlps, resid, cot, gain, bias, near=True)


def head_grads(place, grads, out_t, attns):
    rows, depth = grads[0].shape
    width = out_t.shape[1] // 2
    size = lax.axis_size("fsdp")
    shapes = [far_shapes(depth, width, size, own) for own in (True, False)]

    def kernel(place, near, far, out_t, *refs):
        attns, heads_out, pieces = refs[: len(attns_in)], refs[len(attns_in)], refs[len(attns_in) + 1 :]
        for i in range(2 * rows // BQ):
            source = near if i < rows // BQ else far
            block = slice(i * BQ % rows, i * BQ % rows + BQ)
            heads_out[i * BQ : (i + 1) * BQ, :] = dot(source[block, :], out_t[...]).astype(BF16)
        heads = jnp.concatenate([a[...] for a in attns], axis=1)
        for g in range(2):
            cols = slice(g * depth // 2, (g + 1) * depth // 2)
            block = (dot(near[:, cols], heads[:rows], TN) + dot(far[:, cols], heads[rows:], TN)).astype(BF16)
            put_both(pieces, block, g * depth // 2, place[1], size)

    attns_in = attns
    out_shape = (jax.ShapeDtypeStruct((2 * rows, 2 * width), BF16), *shapes[0], *shapes[1])
    outs = call(
        kernel, "head_grads", [SMEM] + [VMEM] * (3 + len(attns)), out_shape, [], 6, place, *grads, out_t, *attns, near=True
    )
    return outs[0], outs[1 : 1 + len(shapes[0])], outs[1 + len(shapes[0]) :]


def input_grads(grads, weights, rows):
    depth = weights[0].shape[0]
    counts = [len(g) for g in grads]

    def kernel(*refs):
        ins, weights, (sent, kept) = refs[: sum(counts)], refs[sum(counts) : -2], refs[-2:]
        for i in range(2 * rows // BQ):
            total, at = None, 0
            block = slice(i * BQ, (i + 1) * BQ)
            for count, weight in zip(counts, weights):
                left = jnp.concatenate([g[block, :] for g in ins[at : at + count]], axis=1)
                at += count
                partial = dot(left, weight[:, : left.shape[1]], NT)
                total = partial if total is None else total + partial
            if i < rows // BQ:
                kept[block, :] = total
            else:
                sent[i * BQ - rows : (i + 1) * BQ - rows, :] = total.astype(BF16)

    out_shape = (jax.ShapeDtypeStruct((rows, depth), BF16), jax.ShapeDtypeStruct((rows, depth), F32))
    flat = [g for pair in grads for g in pair]
    return call(
        kernel, "input_grads", [VMEM] * (len(flat) + len(weights)), out_shape, [], 10, *flat, *weights
    )


def first_norm_grads(kept, received, inputs, resid_grad, gain):
    def kernel(kept, received, inputs, resid_grad, gain, grad_out, sum_out):
        for i in range(inputs.shape[0] // BQ):
            block = slice(i * BQ, (i + 1) * BQ)
            values = inputs[block, :].astype(F32)
            recip = rms_scale(values)
            unit = values * recip
            grad = kept[block, :] + received[block, :].astype(F32)
            part = jnp.sum(grad * unit, axis=0, keepdims=True)
            sum_out[...] = part if i == 0 else sum_out[...] + part
            scaled = grad * gain[...]
            mean = jnp.mean(scaled * unit, axis=-1, keepdims=True)
            grad_out[block, :] = (resid_grad[block, :] + recip * (scaled - unit * mean)).astype(BF16)

    out_shape = (jax.ShapeDtypeStruct(inputs.shape, BF16), jax.ShapeDtypeStruct((1, inputs.shape[1]), F32))
    return call(kernel, "first_norm_grads", [VMEM] * 5, out_shape, [], 2, kept, received, inputs, resid_grad, gain)


def join_chunks(parts, width):
    counts = [len(p) for p in parts]
    shard = parts[0][0].shape[0]
    part = parts[0][0].shape[1] // 3

    def kernel(*refs):
        at = 0
        sums = []
        for count in counts:
            sums.append(sum(ref[...].astype(F32) for ref in refs[at : at + count]))
            at += count
        for i in range(3):
            refs[-1][i] = jnp.concatenate([total[:, i * part : (i + 1) * part] for total in sums], axis=1)

    flat = [p for pieces in parts for p in pieces]
    out_shape = jax.ShapeDtypeStruct((3, shard, width), F32)
    return call(kernel, "join_chunks", [VMEM] * len(flat), out_shape, [], 1, *flat)


def local(
    inputs,
    doc_ids,
    w_qkv,
    w_out,
    w_up,
    up_bias,
    w_down,
    down_bias,
    attn_gain,
    mlp_gain,
    dim_scale,
    cotangent,
):
    shard, _, width = w_qkv.shape
    size = lax.axis_size("fsdp")
    depth = shard * size
    rows = inputs.shape[0]
    core, tx, rank = lax.axis_index("core"), lax.axis_index("tx"), lax.axis_index("fsdp")
    place = jnp.stack([core, rank]).astype(jnp.int32)

    chunks = 2
    heads = width // HD
    part = width // chunks
    parts = [w_qkv[:, :, c * part : (c + 1) * part].reshape(shard, 3 * part) for c in range(chunks)]
    vectors = jnp.stack([attn_gain, mlp_gain, down_bias], axis=1)
    qkv = Gather(jnp.concatenate([*parts, vectors, jnp.zeros((shard, 61), F32)], axis=1).astype(BF16))
    rest = Gather(jnp.concatenate([w_out.T, w_up, w_down.T], axis=1).astype(BF16))
    qkv.start()

    input_rows = (inputs, swap(inputs, "core", 1))
    cots = (cotangent, swap(cotangent, "core", 1))
    docs = lax.dynamic_slice_in_dim(doc_ids, tx * LEN, LEN, 0)
    doc_col, doc_row = docs[:, None], docs[None, :]
    scale_base = PERDIM_BASE / math.sqrt(HD)
    query_scale = scale_base * jax.nn.softplus(dim_scale)
    colscale = jnp.concatenate([jnp.tile(query_scale, heads // chunks), jnp.ones((2 * part,), F32)])[None]

    now = (*qkv.along_z, input_rows[1], cots[1])
    qkv.middle(*now)
    rest.start(*now)
    now = (*qkv.along_xy, *rest.along_z)
    qkv.finish(*now)
    own_heads, (lse_own, weight_own, normed_first, gains) = attn_forward(
        place, qkv.own, (tie(inputs, *now), input_rows[1]), colscale, doc_col, doc_row, chunks, depth
    )
    now = (lse_own, *qkv.last)
    rest.middle(*now)
    bias_far = swap(tie(up_bias, *now), "tx", 1)
    other_heads, (lse_other, weight_other) = attn_forward(
        place, qkv.other, (tie(normed_first, *now, *rest.ready),), colscale, doc_col, doc_row, chunks, depth
    )
    now = (lse_other, *rest.along_xy, bias_far)
    rest.finish(*now)
    bias_up = jnp.concatenate([up_bias, bias_far])[None]
    attns = [pair[0] for pair in own_heads + other_heads]
    gain_first, gain_second, bias_second = [gains[64 + i : 65 + i] for i in range(3)]
    out_t, up, down_t = assemble(place, rest, depth, "assemble")
    sent, kept = out_forward(attns, out_t, inputs)
    resid_first, normed_own = second_norm(kept, swap(sent, "core", 1), gain_second)
    normeds = (normed_own, swap(normed_own, "core", 1))
    hidden, grad_pre, upbias_sum, mlp_kept, grad_kept, mlp_sent, grad_sent = mlp(normeds, cots, up, down_t, bias_up)
    grads = (grad_kept, swap(grad_sent, "core", 1))
    mlps = (mlp_kept, swap(mlp_sent, "core", 1))
    updown_own, updown_other = weight_grads(place, [(normeds, grad_pre), (cots, hidden)], "updown_grads")
    updown, out, both = Reduction(), Reduction(), Reduction()
    now = (updown_own[-1], grads[1], mlps[1])
    updown.send_far([tie(p, *now) for p in updown_other[:2]] + list(updown_other[2:]))
    grad_resid, grad_own, mlpgain_sum, layer_out = resid_grads(
        (tie(grad_kept, *now), grads[1]), mlps, resid_first, cotangent, gain_second, bias_second
    )
    now = (grad_own, *updown.sent_far)
    grad_attn = (grad_own, swap(tie(grad_own, *now), "core", 1))
    updown.send_xy(updown_own, *now)
    grad_heads, out_own, out_other = head_grads(
        place, (tie(grad_own, *now, *updown.ready), grad_attn[1]), out_t, attns
    )
    out.send_far(out_other)

    def back(pairs, which, lse, first_col, own, *now):
        saved = [(c, *pairs[c]) for c in which]
        return attn_backward(
            place, saved, lse, tie(grad_heads, *now), normed_first, doc_col, doc_row, query_scale[None], first_col, own
        )

    grad_other, sums_other, pieces_other = back(other_heads, range(chunks), lse_other, width, False, out_own[0])
    now = (sums_other, *out.sent_far, updown.from_x, updown.from_y)
    both.send_far([tie(p, *now) for p in pieces_other[:2]] + list(pieces_other[2:]))
    updown.send_z(*now)
    grad_first, sums_first, pieces_first = back(own_heads, [0], lse_own, 0, True, *now, *updown.ready)
    now = (sums_first, *both.sent_far, *updown.parts[1:])
    first, second = both.split(chunks)
    first.send_xy(pieces_first, *now)
    grad_second, sums_second, pieces_second = back(own_heads, [1], lse_own, 0, True, *now, *first.ready)
    now = (sums_second, first.from_x, first.from_y)
    second.send_xy(pieces_second, *now)
    first.send_z(*now)
    sent, kept = input_grads(
        [[tie(grad_first[0], *now, *second.ready, *first.ready), grad_second[0]], list(grad_other)],
        [weight_own, weight_other], rows,
    )
    now = (sent, second.from_x, second.from_y, *first.parts[1:])
    received = swap(tie(sent, *now), "core", 1)
    second.send_z(*now)
    input_grad, attngain_sum = first_norm_grads(
        tie(kept, *now, *second.ready), received, inputs, grad_resid, gain_first
    )
    out.send_xy(out_own, attngain_sum)
    attngain_part = tie(attngain_sum[0], *out.ready)
    out.send_z(*second.parts[1:])

    downbias_part = jnp.sum(cotangent.astype(F32), axis=0)
    scale_part = scale_base * jax.nn.sigmoid(dim_scale) * (sums_other + sums_first + sums_second)[0]
    features = jnp.concatenate([mlpgain_sum[0], downbias_part, attngain_part, scale_part])
    features = features + swap(features, "core", 1)
    received = swap(jnp.concatenate([features, upbias_sum[0, width:]]), "tx", 1)
    sums = sum_fsdp(jnp.concatenate([features, upbias_sum[0, :width]]) + received)

    def own_shard(index):
        return lax.dynamic_slice_in_dim(sums, index * depth + rank * shard, shard, 0)

    updown_grad, out_grad = updown.total(), out.total()
    qkv_grad = join_chunks([first.parts, second.parts], width)
    return (
        layer_out,
        input_grad,
        jnp.transpose(qkv_grad, (1, 0, 2)),
        out_grad.T,
        updown_grad[:, :width],
        sums[3 * depth + HD :],
        updown_grad[:, width:].T,
        own_shard(1),
        own_shard(2),
        own_shard(0),
        sums[3 * depth : 3 * depth + HD],
    )


def solution(mesh):
    size, tensor = mesh.shape["fsdp"], mesh.shape["tensor"]
    split = Mesh(mesh.devices.reshape(size, tensor // 2, 2), ("fsdp", "tx", "core"))
    tokens = P(("fsdp", "tx", "core"), None)
    tensor_axes = ("tx", "core")
    in_specs = (
        tokens,
        P("fsdp"),
        P("fsdp", None, tensor_axes),
        P(tensor_axes, "fsdp"),
        P("fsdp", tensor_axes),
        P(tensor_axes),
        P(tensor_axes, "fsdp"),
        P("fsdp"),
        P("fsdp"),
        P("fsdp"),
        P(),
        tokens,
    )
    out_specs = (
        tokens,
        tokens,
        P("fsdp", None, tensor_axes),
        P(tensor_axes, "fsdp"),
        P("fsdp", tensor_axes),
        P(tensor_axes),
        P(tensor_axes, "fsdp"),
        P("fsdp"),
        P("fsdp"),
        P("fsdp"),
        P(),
    )
    return jax.shard_map(local, mesh=split, in_specs=in_specs, out_specs=out_specs, check_vma=False)
```

```python
import math

import jax
import jax.numpy as jnp
from jax import lax
from jax.experimental import pallas as pl
from jax.experimental.pallas import tpu as pltpu
from jax.sharding import Mesh
from jax.sharding import PartitionSpec as P

HD = 80
LEN = 1024
BQ = 256
NORM_EPS = 1e-06
PERDIM_BASE = 1.442695041
NEG_FILL = -1e30
VMEM_BYTES = 14 << 20
BF16 = jnp.bfloat16
F32 = jnp.float32
NT = (((1,), (1,)), ((), ()))
NN = (((1,), (0,)), ((), ()))
TN = (((0,), (0,)), ((), ()))


def dot(a, b, dims=NN):
    return lax.dot_general(a, b, dims, preferred_element_type=F32)


def swap(value, axis, bit):
    size = lax.axis_size(axis)
    return lax.ppermute(value, axis, [(i, i ^ bit) for i in range(size)])


def tie(value, *others):
    return lax.optimization_barrier((value, *others))[0] if others else value


def rms_scale(values):
    return lax.rsqrt(jnp.mean(values * values, axis=-1, keepdims=True) + NORM_EPS)


def along_z(yj, first=0):
    return [((zj,), 2 * zj + yj, first) for zj in range(4)]


class Gather:
    def __init__(self, shard):
        self.whole = lax.axis_size("fsdp") != 8
        self.shard = shard

    def start(self, *after):
        shard = tie(self.shard, *after)
        if self.whole:
            gathered = lax.all_gather(shard, "fsdp", axis=0, tiled=True)
            self.own, self.other = [(gathered, [])], [(swap(gathered, "tx", 1), [])]
            self.along_z = self.along_xy = self.last = self.ready = (gathered,)
            return
        self.along_z = tuple(swap(shard, "fsdp", 2 * j) for j in (1, 2, 3))

    def middle(self, *after):
        if self.whole:
            return
        stacked = jnp.stack((self.shard, tie(self.along_z[0], *after), *self.along_z[1:]))
        self.ready = (stacked,)
        self.along_xy = (swap(stacked, "fsdp", 1), swap(stacked, "tx", 1))
        self.own = [(stacked, along_z(0)), (self.along_xy[0], along_z(1))]

    def finish(self, *after):
        if self.whole:
            return
        half = self.shard.shape[0] // 2
        from_y, from_x = tie(self.along_xy[0], *after), tie(self.along_xy[1], *after)
        self.last = (swap(from_y[:, :half], "tx", 1), swap(from_x[:, half:], "fsdp", 1))
        self.other = [(self.along_xy[1], along_z(0)), (self.last[0], along_z(1)), (self.last[1], along_z(1, half))]


class GatherLastZ:
    def __init__(self, shard):
        self.whole = lax.axis_size("fsdp") != 8
        self.shard = shard
        self.from_x = swap(shard, "tx", 1)
        self.from_y = self.last = (self.from_x,)

    def middle(self, *after):
        if self.whole:
            return
        self.pair = jnp.stack([self.shard, tie(self.from_x, *after)])
        self.from_y = (swap(self.pair, "fsdp", 1),)

    def finish(self, *after):
        if self.whole:
            shards = (tie(self.shard, *after), self.from_x)
            self.own, self.other = [
                [(lax.all_gather(part, "fsdp", axis=0, tiled=True), [])] for part in shards
            ]
            self.last = (self.own[0][0], self.other[0][0])
            return
        square = jnp.stack([self.pair, tie(self.from_y[0], *after)])
        self.last = tuple(swap(square, "fsdp", 2 * j) for j in (1, 2, 3))
        self.own, self.other = [
            [
                (array, [((yj, r), 2 * zj + yj, 0) for yj in range(2)])
                for zj, array in enumerate((square, *self.last))
            ]
            for r in range(2)
        ]


class HalvesGather:
    def __init__(self, halves):
        self.whole = lax.axis_size("fsdp") != 8
        self.halves = halves
        self.along_z, self.along_xy, self.stacked = [None, None], [None, None], [None, None]

    def start(self, n, *after):
        half = tie(self.halves[n], *after)
        if self.whole:
            self.along_z[n] = (half,)
            return
        self.along_z[n] = tuple(swap(half, "fsdp", 2 * j) for j in (1, 2, 3))

    def middle(self, n, *after):
        if self.whole:
            self.along_xy[n] = self.along_z[n]
            return
        self.stacked[n] = jnp.stack((self.halves[n], tie(self.along_z[n][0], *after), *self.along_z[n][1:]))
        self.along_xy[n] = (swap(self.stacked[n], "fsdp", 1), swap(self.stacked[n], "tx", 1))

    def finish(self, *after):
        if self.whole:
            shard = tie(jnp.concatenate(self.halves), *after)
            gathered = lax.all_gather(shard, "fsdp", axis=0, tiled=True)
            self.own, self.other = [(gathered, [])], [(swap(gathered, "tx", 1), [])]
            self.last = (self.other[0][0],)
            return
        (first_y, first_x), (second_y, second_x) = self.along_xy
        half = self.halves[0].shape[0]
        self.last = (swap(tie(first_y, *after), "tx", 1), swap(tie(second_x, *after), "fsdp", 1))
        self.own = [
            (self.stacked[0], along_z(0)), (first_y, along_z(1)), (self.stacked[1], along_z(0, half)), (second_y, along_z(1, half)),
        ]
        self.other = [
            (first_x, along_z(0)), (self.last[0], along_z(1)), (second_x, along_z(0, half)), (self.last[1], along_z(1, half)),
        ]


class Reduction:
    def __init__(self):
        self.whole = lax.axis_size("fsdp") != 8

    def send_far(self, other):
        self.other = other
        if self.whole:
            self.sent_far = other
            return
        self.sent_far = (swap(other[0], "tx", 1), swap(other[1], "fsdp", 1))

    def split(self, count):
        parts = [Reduction() for _ in range(count)]
        for c, p in enumerate(parts):
            if self.whole:
                p.other = p.sent_far = (self.other[c],)
            else:
                p.sent_far = tuple(r[c] for r in self.sent_far)
                p.other = (None, None, self.other[2 + c])
        return parts

    def send_xy(self, own, *after):
        self.own = own
        if self.whole:
            self.from_x, self.from_y = swap(self.other[0], "tx", 1), own[0]
            self.ready = (own[0],)
            return
        self.ready = add_halves(self.other[2], own[0], self.sent_far, after)
        self.from_x, self.from_y = swap(self.ready[0], "tx", 1), swap(self.ready[1], "fsdp", 1)

    def send_z(self, *after):
        if self.whole:
            total = self.own[0] + tie(self.from_x, *after)
            self.ready = (total,)
            self.parts = (lax.psum_scatter(total, "fsdp", scatter_dimension=0, tiled=True),)
            return
        self.ready = sum_pieces(tie(self.own[1], *after), self.from_x, self.from_y)
        self.parts = (self.ready[0], *(swap(self.ready[j], "fsdp", 2 * j) for j in (1, 2, 3)))

    def total(self):
        return sum(piece.astype(F32) for piece in self.parts)


def sum_pieces(near, from_x, from_y):
    def kernel(near, from_x, from_y, *outs):
        for j, out in enumerate(outs):
            total = near[j].astype(F32) + from_x[j].astype(F32) + from_y[j].astype(F32)
            out[...] = total.astype(out.dtype)

    _, rows, cols = near.shape
    out_shape = tuple(jax.ShapeDtypeStruct((rows, cols), BF16 if j else F32) for j in range(4))
    return call(kernel, "sum_pieces", [VMEM] * 3, out_shape, [], 0.01, near, from_x, from_y)


def add_halves(near, far, sent_far, after):
    def kernel(near, far, from_x, from_y, along_x, along_y):
        half = near.shape[1] // 2
        along_x[:, :half] = near[:, :half]
        along_x[:, half:] = (near[:, half:].astype(F32) + from_y[...].astype(F32)).astype(BF16)
        along_y[:, :half] = (far[:, :half].astype(F32) + from_x[...].astype(F32)).astype(BF16)
        along_y[:, half:] = far[:, half:]

    out_shape = (jax.ShapeDtypeStruct(near.shape, BF16), jax.ShapeDtypeStruct(far.shape, BF16))
    return call(kernel, "add_halves", [VMEM] * 4, out_shape, [], 0.01, tie(near, *after), far, *sent_far, near=True)


def sum_fsdp(value, *after):
    size = lax.axis_size("fsdp")
    if size != 8:
        return lax.psum(value, "fsdp")
    value = value + swap(value, "fsdp", 1)
    value = value + swap(value, "fsdp", 2)
    return value + swap(tie(value, *after), "fsdp", 4)


VMEM = pl.BlockSpec(memory_space=pltpu.VMEM)
SMEM = pl.BlockSpec(memory_space=pltpu.SMEM)


def call(kernel, name, in_specs, out_shape, scratch_shapes, micros, *args, near=False):
    if near:
        args = [pltpu.with_memory_space_constraint(a, pltpu.VMEM) if s is VMEM else a for a, s in zip(args, in_specs)]
        out_shape = jax.tree.map(lambda o: pltpu.VMEM(o.shape, o.dtype), out_shape)
    return pl.pallas_call(
        kernel,
        in_specs=in_specs,
        out_specs=jax.tree.map(lambda _: VMEM, out_shape),
        out_shape=out_shape,
        scratch_shapes=scratch_shapes,
        compiler_params=pltpu.CompilerParams(vmem_limit_bytes=VMEM_BYTES),
        cost_estimate=pl.CostEstimate(flops=int(micros * 1e9), bytes_accessed=1 << 10, transcendentals=0),
        name=name,
    )(*args)


def place_pieces(refs, entries, weight, rank, cols=slice(None), width=None, first_col=0):
    if len(refs) == 1 and not entries[0]:
        weight[:, first_col : first_col + width] = refs[0][:, cols]
        return
    shard = weight.shape[0] // 8
    for ref, places in zip(refs, entries):
        for index, j, first in places:
            piece = ref[(*index, slice(None), cols)]
            start = pl.multiple_of((rank ^ j) * shard + first, 16)
            weight[pl.ds(start, piece.shape[0]), first_col : first_col + width] = piece


def far_shapes(depth, cols, size, own, parts=1):
    if size != 8:
        return (jax.ShapeDtypeStruct((depth, cols // parts), BF16),) * parts
    rows = depth // 8
    near = (jax.ShapeDtypeStruct((4, rows, cols // parts), BF16),) * parts
    if own:
        return (*near, *near)
    lead = (parts,) if parts > 1 else ()
    return (jax.ShapeDtypeStruct((*lead, 4, rows // 2, cols // parts), BF16),) * 2 + near


def put_pieces(refs, block, start, rank, own, part=None):
    if len(refs[0].shape) == 2:
        refs[part or 0][start : start + block.shape[0], :] = block
        return
    near = refs[len(refs) // 2 + (part or 0)] if own else refs[2 + (part or 0)]
    rows = near.shape[1]
    for n in range(block.shape[0] // rows):
        j = (start // rows + n) ^ rank
        yj, zj = j & 1, j >> 1
        piece = block[n * rows : (n + 1) * rows]

        @pl.when(yj == 0)
        def _():
            near[zj] = piece

        @pl.when(yj == 1)
        def _():
            if own:
                refs[part or 0][zj] = piece
            elif part is None:
                refs[0][zj] = piece[: rows // 2]
                refs[1][zj] = piece[rows // 2 :]
            else:
                refs[0][part, zj] = piece[: rows // 2]
                refs[1][part, zj] = piece[rows // 2 :]


def assemble(place, gathers, depth, width):
    lists = [pieces for g in gathers for pieces in (g.own, g.other)]
    entries = [[p[1] for p in pieces] for pieces in lists]
    arrays = [p[0] for pieces in lists for p in pieces]
    counts = [pieces[0][0].shape[-1] for pieces in lists[::2]]
    parts = sum(counts) // width

    def kernel(place, *refs):
        pieces, outs = refs[: len(arrays)], refs[len(arrays) :]
        at, first = 0, 0
        for n, places in enumerate(entries):
            refs_n = pieces[at : at + len(places)]
            at += len(places)
            for i in range(counts[n // 2] // width):
                cols = slice(i * width, (i + 1) * width)
                place_pieces(refs_n, places, outs[first + i], place[1], cols, width, n % 2 * width)
            if n % 2:
                first += counts[n // 2] // width

    out_shape = tuple(jax.ShapeDtypeStruct((depth, 2 * width), BF16) for _ in range(parts))
    return call(kernel, "assemble", [SMEM] + [VMEM] * len(arrays), out_shape, [], 3, place, *arrays, near=True)


def pack_qkv(weights, vectors, chunks):
    _, shard, width = weights.shape
    part = width // chunks
    cols = -(-(3 * width + 8) // 128) * 128

    def kernel(weights, vectors, *outs):
        blocks = [weights[i, :, c * part : (c + 1) * part] for c in range(chunks) for i in range(3)]
        blocks += [vectors[...].T, jnp.zeros((shard, cols - 3 * width - 8), F32)]
        packed = jnp.concatenate(blocks, axis=1).astype(BF16)
        for n, out in enumerate(outs):
            out[...] = packed[n * shard // 2 : (n + 1) * shard // 2]

    out_shape = (jax.ShapeDtypeStruct((shard // 2, cols), BF16),) * 2
    return call(kernel, "pack_qkv", [VMEM] * 2, out_shape, [], 1, weights, vectors)


def mask_bias(doc_col, doc_row, bias):
    for i in range(LEN // BQ):
        lo, hi = i * BQ, (i + 1) * BQ
        same = doc_col[:hi, :] == doc_row[:, lo:hi]
        keys = lax.broadcasted_iota(jnp.int32, (hi, BQ), 0)
        queries = lax.broadcasted_iota(jnp.int32, (hi, BQ), 1) + lo
        bias[i, :hi, :] = jnp.where(same & (keys <= queries), 0.0, NEG_FILL)


def outer_rows(lo, rows, core):
    half = LEN // 2
    return pl.ds(pl.multiple_of(((lo // half) ^ core) * half + lo % half, rows), rows)


def head_rows(ref, block, columns, rows):
    for h in range(ref.shape[0]):
        ref[h, rows, :] = block[:, columns[h] : columns[h] + HD].astype(ref.dtype)


def join_heads(ref, heads):
    return jnp.concatenate([ref[h] for h in heads], axis=1)


def attn_forward(place, pieces, rows_in, scale, doc_col, doc_row, chunks, depth):
    arrays, places = [p[0] for p in pieces], [p[1] for p in pieces]
    cols = arrays[0].shape[-1]
    fresh = len(rows_in) == 2
    part = scale.shape[1] // 3
    per_chunk = part // HD
    heads = per_chunk * chunks
    starts = [[c * 3 * part + n * part + h * HD for c in range(chunks) for h in range(per_chunk)] for n in range(3)]

    def kernel(place, *refs):
        pieces, refs = refs[: len(arrays)], refs[len(arrays) :]
        sources, (scale, doc_col, doc_row) = refs[: len(rows_in)], refs[len(rows_in) : len(rows_in) + 3]
        outs = refs[len(rows_in) + 3 :]
        attns, (query, key, value, lse, weight) = outs[:chunks], outs[chunks : chunks + 5]
        if fresh:
            x, gains, bias, out_heads = outs[chunks + 5 :]
        else:
            x, (bias, out_heads) = sources[0], outs[chunks + 5 :]
        core, rank = place[0], place[1]
        half = LEN // 2
        place_pieces(pieces, places, weight, rank, slice(None), cols)
        mask_bias(doc_col, doc_row, bias)
        if fresh:
            gains[...] = weight[:, cols - 128 :].astype(F32).T
            gain = gains[64:65, :]
            for n, source in enumerate(sources):

                def norm(i, _, source=source, n=n):
                    block = pl.ds(pl.multiple_of(i * 128, 128), 128)
                    values = source[block, :].astype(F32)
                    target = pl.ds(pl.multiple_of(i * 128 + n * half, 128), 128)
                    x[target, :] = (values * rms_scale(values) * gain).astype(BF16)
                    return 0

                lax.fori_loop(0, half // 128, norm, 0)

        def project(i, _):
            lo = i * BQ
            block = dot(x[outer_rows(lo, BQ, core), :], weight[...])
            rows = pl.ds(pl.multiple_of(lo, BQ), BQ)
            scaled = jnp.concatenate(
                [block[:, c * 3 * part : c * 3 * part + part] * scale[:, :part] for c in range(chunks)], axis=1
            )
            head_rows(query, scaled, [h * HD for h in range(heads)], rows)
            head_rows(key, block, starts[1], rows)
            head_rows(value, block, starts[2], rows)
            return 0

        lax.fori_loop(0, LEN // BQ, project, 0)

        def attend(h, _):
            keys = key[h]
            value_t = value[h].T
            blocks = []
            for i in range(LEN // BQ):
                lo, hi = i * BQ, (i + 1) * BQ
                scores = dot(keys[:hi], query[h, lo:hi, :], NT) + bias[i, :hi, :]
                top = jnp.max(scores, axis=0, keepdims=True)
                probs = jnp.exp(scores - top)
                total = jnp.sum(probs, axis=0, keepdims=True)
                blocks.append(dot(value_t[:, :hi], probs.astype(BF16)) / total)
                lse[h, :, lo:hi] = top + jnp.log(total)
            out_heads[h] = jnp.concatenate(blocks, axis=1).T.astype(BF16)
            return 0

        def attend_two(n, _):
            attend(2 * n, 0)
            return attend(2 * n + 1, 0)

        lax.fori_loop(0, heads // 2, attend_two, 0)
        for c in range(chunks):
            joined = join_heads(out_heads, range(c * per_chunk, (c + 1) * per_chunk))
            for a in range(2):
                attns[c][outer_rows(a * half, half, core), :] = joined[a * half : (a + 1) * half]

    per_head = jax.ShapeDtypeStruct((heads, LEN, HD), BF16)
    out_shape = (
        *(jax.ShapeDtypeStruct((LEN, part), BF16),) * chunks,
        per_head,
        per_head,
        per_head,
        jax.ShapeDtypeStruct((heads, 1, LEN), F32),
        jax.ShapeDtypeStruct((depth, cols), BF16),
    )
    scratch = [pltpu.VMEM((LEN // BQ, LEN, BQ), F32), pltpu.VMEM((heads, LEN, HD), BF16)]
    if fresh:
        out_shape += (jax.ShapeDtypeStruct((LEN, depth), BF16), jax.ShapeDtypeStruct((128, depth), F32))
    specs = [SMEM] + [VMEM] * (len(arrays) + len(rows_in) + 3)
    args = (place, *arrays, *rows_in, scale, doc_col, doc_row)
    outs = call(kernel, "attn_forward", specs, out_shape, scratch, 8, *args, near=True)
    return outs[:chunks], outs[chunks : chunks + 4], outs[chunks + 4 :]


def attn_backward(place, attns, saved, dout, x, doc_col, doc_row, scale, first, own):
    part = attns[0].shape[1]
    per_chunk = part // HD
    count = len(attns)
    heads = per_chunk * count
    depth = x.shape[1]
    pieces_shape = far_shapes(depth, 3 * part * count, lax.axis_size("fsdp"), own, count)

    def kernel(place, *refs):
        attns, refs = refs[:count], refs[count:]
        query, key, value, lse, dout, x, doc_col, doc_row, scale, *refs = refs
        grads_out, sums_out, refs = refs[:count], refs[count], refs[count + 1 :]
        pieces, (dkey, dvalue, bias, douts, deltas, grads) = refs[:-6], refs[-6:]
        core, rank = place[0], place[1]
        half = LEN // 2
        lanes = lax.broadcasted_iota(jnp.int32, (8, part), 1) // HD
        selector = jnp.where(lanes == lax.broadcasted_iota(jnp.int32, (8, part), 0), 1.0, 0.0)
        mask_bias(doc_col, doc_row, bias)
        for c in range(count):
            for i in range(LEN // BQ):
                lo, hi = i * BQ, (i + 1) * BQ
                rows = outer_rows(lo, BQ, core)
                dout_block = dout[rows, first + c * part : first + (c + 1) * part]
                products = attns[c][rows, :].astype(F32) * dout_block.astype(F32)
                delta = lax.dot_general(
                    selector, products, NT, precision=lax.Precision.HIGHEST, preferred_element_type=F32
                )
                for h in range(per_chunk):
                    deltas[c * per_chunk + h, :, lo:hi] = delta[h : h + 1, :]
                    douts[c * per_chunk + h, lo:hi, :] = dout_block[:, h * HD : (h + 1) * HD]

        def attend(h, sums):
            keys = key[h]
            key_t = keys.T
            dquery_parts = []
            for i in range(LEN // BQ):
                lo, hi = i * BQ, (i + 1) * BQ
                queries = query[h, lo:hi, :]
                dout_head = douts[h, lo:hi, :]
                scores = dot(keys[:hi], queries, NT) + bias[i, :hi, :]
                probs = jnp.exp(scores - lse[h, :, lo:hi])
                dprobs = dot(value[h, :hi, :], dout_head, NT)
                dscores = (probs * (dprobs - deltas[h, :, lo:hi])).astype(BF16)
                dv = dot(probs.astype(BF16), dout_head)
                dk = dot(dscores, queries)
                dquery_parts.append(dot(key_t[:, :hi], dscores))
                if i:
                    dkey[:lo] += dk[:lo]
                    dvalue[:lo] += dv[:lo]
                dkey[lo:hi] = dk[lo:]
                dvalue[lo:hi] = dv[lo:]
            dquery = jnp.concatenate(dquery_parts, axis=1).T
            grads[0, h] = (dquery * scale[...]).astype(BF16)
            grads[1, h] = dkey[...].astype(BF16)
            grads[2, h] = dvalue[...].astype(BF16)
            return sums + jnp.sum(dquery * query[h].astype(F32), axis=0, keepdims=True)

        def attend_two(n, sums):
            return attend(2 * n + 1, attend(2 * n, sums))

        sums = lax.fori_loop(0, heads // 2, attend_two, jnp.zeros((1, HD), F32))
        sums_out[...] = sums / scale[...]
        for c in range(count):
            mine = range(c * per_chunk, (c + 1) * per_chunk)
            joined = jnp.concatenate([grads[n, h] for n in range(3) for h in mine], axis=1)
            for a in range(2):
                grads_out[c][outer_rows(a * half, half, core), :] = joined[a * half : (a + 1) * half]
            for g in range(2):
                start = g * depth // 2
                block = dot(x[:, start : start + depth // 2], grads_out[c][...], TN).astype(BF16)
                put_pieces(pieces, block, start, rank, own, c if count > 1 else None)

    out_shape = (
        *(jax.ShapeDtypeStruct((LEN, 3 * part), BF16),) * count,
        jax.ShapeDtypeStruct((1, HD), F32),
        *pieces_shape,
    )
    scratch = [
        pltpu.VMEM((LEN, HD), F32),
        pltpu.VMEM((LEN, HD), F32),
        pltpu.VMEM((LEN // BQ, LEN, BQ), F32),
        pltpu.VMEM((heads, LEN, HD), BF16),
        pltpu.VMEM((heads, 1, LEN), F32),
        pltpu.VMEM((3, heads, LEN, HD), BF16),
    ]
    args = (place, *attns, *saved, dout, x, doc_col, doc_row, scale)
    specs = [SMEM] + [VMEM] * (len(args) - 1)
    outs = call(kernel, "attn_backward", specs, out_shape, scratch, 10, *args, near=True)
    return outs[:count], outs[count], outs[count + 1 :]


def put_both(outs, block, start, rank, size):
    width = block.shape[1] // 2
    count = len(outs) // 2 if size != 8 else 2
    put_pieces(outs[:count], block[:, :width], start, rank, True)
    put_pieces(outs[count:], block[:, width:], start, rank, False)


def weight_grads(place, pairs, name):
    rows, depth = pairs[0][0][0].shape
    width = pairs[0][1].shape[1] // 2
    size = lax.axis_size("fsdp")
    shapes = [far_shapes(depth, width * len(pairs), size, own) for own in (True, False)]

    def kernel(place, *refs):
        ins, outs = refs[: 3 * len(pairs)], refs[3 * len(pairs) :]
        for g in range(2):
            cols = slice(g * depth // 2, (g + 1) * depth // 2)
            blocks = []
            for n in range(len(pairs)):
                near, far, right = ins[3 * n : 3 * n + 3]
                block = dot(near[:, cols], right[:rows, :], TN) + dot(far[:, cols], right[rows:, :], TN)
                blocks.append(block.astype(BF16))
            joined = [b[:, r * width : (r + 1) * width] for r in range(2) for b in blocks]
            put_both(outs, jnp.concatenate(joined, axis=1), g * depth // 2, place[1], size)

    args = [a for halves, right in pairs for a in (*halves, right)]
    outs = call(
        kernel, name, [SMEM] + [VMEM] * len(args), (*shapes[0], *shapes[1]), [], 4 * len(pairs), place, *args, near=True
    )
    return outs[: len(shapes[0])], outs[len(shapes[0]) :]


def out_forward(attns, out_t, inputs):
    rows, depth = inputs.shape

    def kernel(*refs):
        attns, (out_t, inputs, sent, kept) = refs[:-4], refs[-4:]
        heads = jnp.concatenate([a[...] for a in attns], axis=1)
        for i in range(rows // BQ):
            lo, hi = i * BQ, (i + 1) * BQ
            sent[lo:hi, :] = dot(heads[rows + lo : rows + hi], out_t[...], NT).astype(BF16)
            kept[lo:hi, :] = inputs[lo:hi, :].astype(F32) + dot(heads[lo:hi], out_t[...], NT)

    out_shape = (jax.ShapeDtypeStruct((rows, depth), BF16), jax.ShapeDtypeStruct((rows, depth), F32))
    return call(kernel, "out_forward", [VMEM] * (len(attns) + 2), out_shape, [], 3, *attns, out_t, inputs, near=True)


def second_norm(kept, received, gain):
    def kernel(kept, received, gain, resid_out, normed_out):
        resid = kept[...] + received[...].astype(F32)
        resid_out[...] = resid
        normed_out[...] = (resid * rms_scale(resid) * gain[...]).astype(BF16)

    out_shape = (jax.ShapeDtypeStruct(kept.shape, F32), jax.ShapeDtypeStruct(kept.shape, BF16))
    return call(kernel, "second_norm", [VMEM] * 3, out_shape, [], 1, kept, received, gain, near=True)


def mlp(normed, cot, up, down_t, bias_up):
    rows, depth = normed[0].shape
    units = up.shape[1]

    def kernel(n_near, n_far, c_near, c_far, up, down_t, bias, hidden, grad_pre, bias_sum, *outs):
        sums = jnp.zeros((1, units), F32)
        for side, (n, c) in enumerate(((n_near, c_near), (n_far, c_far))):
            out_mlp, out_grad = outs[2 * side : 2 * side + 2]

            def step(i, sums, n=n, c=c, side=side, out_mlp=out_mlp, out_grad=out_grad):
                block = pl.ds(pl.multiple_of(i * BQ, BQ), BQ)
                target = pl.ds(pl.multiple_of(i * BQ + side * rows, BQ), BQ)
                pre = dot(n[block, :], up[...]) + bias[...]
                sig = 1.0 / (1.0 + jnp.exp(-pre))
                units_low = (pre * sig).astype(BF16)
                grad = dot(c[block, :], down_t[...])
                grad_low = (grad * (sig + pre * sig * (1.0 - sig))).astype(BF16)
                hidden[target, :] = units_low
                grad_pre[target, :] = grad_low
                out_mlp[block, :] = dot(units_low, down_t[...], NT).astype(BF16)
                out_grad[block, :] = dot(grad_low, up[...], NT).astype(BF16)
                return sums + jnp.sum(grad_low.astype(F32), axis=0, keepdims=True)

            sums = lax.fori_loop(0, rows // BQ, step, sums)
        bias_sum[...] = sums

    low = jax.ShapeDtypeStruct((rows, depth), BF16)
    out_shape = (
        jax.ShapeDtypeStruct((2 * rows, units), BF16),
        jax.ShapeDtypeStruct((2 * rows, units), BF16),
        jax.ShapeDtypeStruct((1, units), F32),
        low,
        low,
        low,
        low,
    )
    return call(kernel, "mlp", [VMEM] * 7, out_shape, [], 10, *normed, *cot, up, down_t, bias_up, near=True)


def resid_grads(grads, mlps, resid, cot, gain, bias):
    def kernel(grad_near, grad_far, mlp_near, mlp_far, resid, cot, gain, bias, low_out, sum_out, layer):
        for i in range(resid.shape[0] // BQ):
            block = slice(i * BQ, (i + 1) * BQ)
            held = resid[block, :]
            grad = grad_near[block, :].astype(F32) + grad_far[block, :].astype(F32)
            recip = rms_scale(held)
            unit = held * recip
            part = jnp.sum(grad * unit, axis=0, keepdims=True)
            sum_out[...] = part if i == 0 else sum_out[...] + part
            scaled = grad * gain[...]
            mean = jnp.mean(scaled * unit, axis=-1, keepdims=True)
            total = cot[block, :].astype(F32) + recip * (scaled - unit * mean)
            low_out[block, :] = total.astype(BF16)
            mlp = mlp_near[block, :].astype(F32) + mlp_far[block, :].astype(F32)
            layer[block, :] = (held + mlp + bias[...]).astype(BF16)

    out_shape = (
        jax.ShapeDtypeStruct(resid.shape, BF16),
        jax.ShapeDtypeStruct((1, resid.shape[1]), F32),
        jax.ShapeDtypeStruct(resid.shape, BF16),
    )
    return call(kernel, "resid_grads", [VMEM] * 8, out_shape, [], 2, *grads, *mlps, resid, cot, gain, bias, near=True)


def head_grads(place, grads, out_t, attns):
    rows, depth = grads[0].shape
    width = out_t.shape[1] // 2
    size = lax.axis_size("fsdp")
    shapes = [far_shapes(depth, width, size, own) for own in (True, False)]

    def kernel(place, near, far, out_t, *refs):
        attns, heads_out, pieces = refs[: len(attns_in)], refs[len(attns_in)], refs[len(attns_in) + 1 :]
        for i in range(2 * rows // BQ):
            source = near if i < rows // BQ else far
            block = slice(i * BQ % rows, i * BQ % rows + BQ)
            heads_out[i * BQ : (i + 1) * BQ, :] = dot(source[block, :], out_t[...]).astype(BF16)
        heads = jnp.concatenate([a[...] for a in attns], axis=1)
        for g in range(2):
            cols = slice(g * depth // 2, (g + 1) * depth // 2)
            block = (dot(near[:, cols], heads[:rows], TN) + dot(far[:, cols], heads[rows:], TN)).astype(BF16)
            put_both(pieces, block, g * depth // 2, place[1], size)

    attns_in = attns
    out_shape = (jax.ShapeDtypeStruct((2 * rows, 2 * width), BF16), *shapes[0], *shapes[1])
    args = (place, *grads, out_t, *attns)
    outs = call(kernel, "head_grads", [SMEM] + [VMEM] * (len(args) - 1), out_shape, [], 6, *args, near=True)
    return outs[0], outs[1 : 1 + len(shapes[0])], outs[1 + len(shapes[0]) :]


def input_grads(grads, weights, rows):
    depth = weights[0].shape[0]
    counts = [len(g) for g in grads]

    def kernel(*refs):
        ins, weights, (sent, kept) = refs[: sum(counts)], refs[sum(counts) : -2], refs[-2:]
        for side, out in enumerate((kept, sent)):

            def step(i, _, side=side, out=out):
                total, at = None, 0
                block = pl.ds(pl.multiple_of(i * BQ + side * rows, BQ), BQ)
                for count, weight in zip(counts, weights):
                    left = jnp.concatenate([g[block, :] for g in ins[at : at + count]], axis=1)
                    at += count
                    partial = dot(left, weight[:, : left.shape[1]], NT)
                    total = partial if total is None else total + partial
                out[pl.ds(pl.multiple_of(i * BQ, BQ), BQ), :] = total.astype(BF16)
                return 0

            lax.fori_loop(0, rows // BQ, step, 0)

    out_shape = (jax.ShapeDtypeStruct((rows, depth), BF16),) * 2
    flat = [g for pair in grads for g in pair]
    return call(
        kernel, "input_grads", [VMEM] * (len(flat) + len(weights)), out_shape, [], 10, *flat, *weights, near=True
    )


def first_norm_grads(kept, received, inputs, resid_grad, gain):
    def kernel(kept, received, inputs, resid_grad, gain, grad_out, sum_out):
        for i in range(inputs.shape[0] // BQ):
            block = slice(i * BQ, (i + 1) * BQ)
            values = inputs[block, :].astype(F32)
            recip = rms_scale(values)
            unit = values * recip
            grad = kept[block, :].astype(F32) + received[block, :].astype(F32)
            part = jnp.sum(grad * unit, axis=0, keepdims=True)
            sum_out[...] = part if i == 0 else sum_out[...] + part
            scaled = grad * gain[...]
            mean = jnp.mean(scaled * unit, axis=-1, keepdims=True)
            grad_out[block, :] = (resid_grad[block, :].astype(F32) + recip * (scaled - unit * mean)).astype(BF16)

    out_shape = (jax.ShapeDtypeStruct(inputs.shape, BF16), jax.ShapeDtypeStruct((1, inputs.shape[1]), F32))
    args = (kept, received, inputs, resid_grad, gain)
    return call(kernel, "first_norm_grads", [VMEM] * 5, out_shape, [], 0.01, *args)


def join_chunks(parts, width):
    counts = [len(p) for p in parts]
    shard = parts[0][0].shape[0]
    part = parts[0][0].shape[1] // 3

    def kernel(*refs):
        at = 0
        sums = []
        for count in counts:
            sums.append(sum(ref[...].astype(F32) for ref in refs[at : at + count]))
            at += count
        for i in range(3):
            refs[-1][i] = jnp.concatenate([total[:, i * part : (i + 1) * part] for total in sums], axis=1)

    flat = [p for pieces in parts for p in pieces]
    out_shape = jax.ShapeDtypeStruct((3, shard, width), F32)
    return call(kernel, "join_chunks", [VMEM] * len(flat), out_shape, [], 1, *flat)


def local(
    inputs,
    doc_ids,
    w_qkv,
    w_out,
    w_up,
    up_bias,
    w_down,
    down_bias,
    attn_gain,
    mlp_gain,
    dim_scale,
    cotangent,
):
    shard, _, width = w_qkv.shape
    size = lax.axis_size("fsdp")
    depth = shard * size
    rows = inputs.shape[0]
    core, tx, rank = lax.axis_index("core"), lax.axis_index("tx"), lax.axis_index("fsdp")
    place = jnp.stack([core, rank]).astype(jnp.int32)

    chunks = 2
    heads = width // HD
    part = width // chunks
    vectors = jnp.concatenate([jnp.stack([attn_gain, mlp_gain, down_bias]), jnp.zeros((5, shard), F32)])
    qkv = HalvesGather(pack_qkv(jnp.transpose(w_qkv, (1, 0, 2)), vectors, chunks))
    rest = Gather(jnp.concatenate([w_out.T, w_up, w_down.T], axis=1).astype(BF16))
    qkv.start(0)

    input_rows = (inputs, swap(inputs, "core", 1))
    cots = (cotangent, swap(cotangent, "core", 1))
    docs = lax.dynamic_slice_in_dim(doc_ids, tx * LEN, LEN, 0)
    doc_col, doc_row = docs[:, None], docs[None, :]
    scale_base = PERDIM_BASE / math.sqrt(HD)
    query_scale = scale_base * jax.nn.softplus(dim_scale)
    colscale = jnp.concatenate([jnp.tile(query_scale, heads // chunks), jnp.ones((2 * part,), F32)])[None]

    now = (*qkv.along_z[0], input_rows[1], cots[1])
    qkv.middle(0, *now)
    qkv.start(1, *now)
    now = (*qkv.along_xy[0], *qkv.along_z[1])
    qkv.middle(1, *now)
    rest.start(*now)
    now = qkv.along_xy[1]
    qkv.finish(*now)
    own_attns, own_saved, (weight_own, normed_first, gains) = attn_forward(
        place, qkv.own, (tie(inputs, *now), input_rows[1]), colscale, doc_col, doc_row, chunks, depth
    )
    now = (own_saved[3], *rest.along_z, *qkv.last)
    rest.middle(*now)
    other_attns, other_saved, (weight_other,) = attn_forward(
        place, qkv.other, (tie(normed_first, *now, *rest.ready, *qkv.last),), colscale, doc_col, doc_row, chunks, depth
    )
    now = (other_saved[3], *rest.along_xy)
    rest.finish(*now)
    bias_far = swap(tie(up_bias, *now), "tx", 1)
    rest.other[-1] = (tie(rest.other[-1][0], bias_far), rest.other[-1][1])
    bias_up = jnp.concatenate([up_bias, bias_far])[None]
    attns = [*own_attns, *other_attns]
    gain_first, gain_second, bias_second = [gains[64 + i : 65 + i] for i in range(3)]
    out_t, up, down_t = assemble(place, (rest,), depth, width)
    sent, kept = out_forward(attns, out_t, inputs)
    resid_first, normed_own = second_norm(kept, swap(sent, "core", 1), gain_second)
    normeds = (normed_own, swap(normed_own, "core", 1))
    hidden, grad_pre, upbias_sum, mlp_kept, grad_kept, mlp_sent, grad_sent = mlp(normeds, cots, up, down_t, bias_up)
    grads = (grad_kept, swap(grad_sent, "core", 1))
    mlps = (mlp_kept, swap(mlp_sent, "core", 1))
    updown_own, updown_other = weight_grads(place, [(normeds, grad_pre), (cots, hidden)], "updown_grads")
    updown, out, both = Reduction(), Reduction(), Reduction()
    now = (updown_own[-1], grads[1], mlps[1])
    updown.send_far([tie(p, *now) for p in updown_other[:2]] + list(updown_other[2:]))
    grad_own, mlpgain_sum, layer_out = resid_grads(
        (tie(grad_kept, *now), grads[1]), mlps, resid_first, cotangent, gain_second, bias_second
    )
    grad_attn = (grad_own, swap(grad_own, "core", 1))
    grad_heads, out_own, out_other = head_grads(place, grad_attn, out_t, attns)
    now = (grad_heads, *updown.sent_far)
    updown.send_xy(updown_own, *now)
    out.send_far([tie(p, *now) for p in out_other[:2]] + list(out_other[2:]))

    def back(attns, saved, first_col, own, *now):
        dout = tie(grad_heads, *now)
        return attn_backward(
            place, attns, saved, dout, normed_first, doc_col, doc_row, query_scale[None], first_col, own
        )

    grad_other, sums_other, pieces_other = back(other_attns, other_saved, width, False, *now, *updown.ready)
    now = (sums_other, *out.sent_far)
    both.send_far([tie(p, *now) for p in pieces_other[:2]] + list(pieces_other[2:]))
    grad_first, sums_first, pieces_first = back(own_attns, own_saved, 0, True, *now)
    now = (sums_first, updown.from_x, updown.from_y, *both.sent_far)
    first, second = both.split(chunks)
    near_far = [pieces_first[c::chunks] for c in range(chunks)]
    first.send_xy(near_far[0], *now)
    updown.send_z(*now)
    sent, kept = input_grads(
        [[tie(grad_first[0], *first.ready, *updown.ready), grad_first[1]], list(grad_other)],
        [weight_own, weight_other], rows,
    )
    now = (sent, first.from_x, first.from_y, *updown.parts[1:])
    second.send_xy(near_far[1], *now)
    received = swap(tie(sent, *now, *second.ready), "core", 1)
    first.send_z(*now, *second.ready)
    input_grad, attngain_sum = first_norm_grads(tie(kept, *first.ready), received, inputs, grad_own, gain_first)
    attngain_part = attngain_sum[0]
    now = (attngain_sum, second.from_x, second.from_y, *first.parts[1:])

    downbias_part = jnp.sum(cotangent.astype(F32), axis=0)
    scale_part = scale_base * jax.nn.sigmoid(dim_scale) * (sums_other + sums_first)[0]
    features = jnp.concatenate([mlpgain_sum[0], downbias_part, attngain_part, scale_part])
    features = features + swap(tie(features, *now), "core", 1)
    received = swap(tie(jnp.concatenate([features, upbias_sum[0, width:]]), *now), "tx", 1)
    second.send_z(*now)
    out.send_xy(out_own, received, *second.ready)
    vector = jnp.concatenate([features, upbias_sum[0, :width]]) + received
    out.send_z(*second.parts[1:])
    sums = sum_fsdp(tie(vector, out.from_x, out.from_y), *out.parts[1:2])

    def own_shard(index):
        return lax.dynamic_slice_in_dim(sums, index * depth + rank * shard, shard, 0)

    updown_grad, out_grad = updown.total(), out.total()
    qkv_grad = join_chunks([first.parts, second.parts], width)
    return (
        layer_out,
        input_grad,
        jnp.transpose(qkv_grad, (1, 0, 2)),
        out_grad.T,
        updown_grad[:, :width],
        sums[3 * depth + HD :],
        updown_grad[:, width:].T,
        own_shard(1),
        own_shard(2),
        own_shard(0),
        sums[3 * depth : 3 * depth + HD],
    )


def solution(mesh):
    size, tensor = mesh.shape["fsdp"], mesh.shape["tensor"]
    split = Mesh(mesh.devices.reshape(size, tensor // 2, 2), ("fsdp", "tx", "core"))
    tokens = P(("fsdp", "tx", "core"), None)
    tensor_axes = ("tx", "core")
    in_specs = (
        tokens,
        P("fsdp"),
        P("fsdp", None, tensor_axes),
        P(tensor_axes, "fsdp"),
        P("fsdp", tensor_axes),
        P(tensor_axes),
        P(tensor_axes, "fsdp"),
        P("fsdp"),
        P("fsdp"),
        P("fsdp"),
        P(),
        tokens,
    )
    out_specs = (
        tokens,
        tokens,
        P("fsdp", None, tensor_axes),
        P(tensor_axes, "fsdp"),
        P("fsdp", tensor_axes),
        P(tensor_axes),
        P(tensor_axes, "fsdp"),
        P("fsdp"),
        P("fsdp"),
        P("fsdp"),
        P(),
    )
    return jax.shard_map(local, mesh=split, in_specs=in_specs, out_specs=out_specs, check_vma=False)
```

```python
import math

import jax
import jax.numpy as jnp
from jax import lax
from jax.experimental import pallas as pl
from jax.experimental.pallas import tpu as pltpu
from jax.sharding import Mesh
from jax.sharding import PartitionSpec as P

HD = 80
LEN = 1024
BQ = 256
NORM_EPS = 1e-06
PERDIM_BASE = 1.442695041
NEG_FILL = -1e30
VMEM_BYTES = 16 << 20
BF16 = jnp.bfloat16
F32 = jnp.float32
NT = (((1,), (1,)), ((), ()))
NN = (((1,), (0,)), ((), ()))
TN = (((0,), (0,)), ((), ()))


def dot(a, b, dims=NN):
    return lax.dot_general(a, b, dims, preferred_element_type=F32)


def swap(value, axis, bit):
    size = lax.axis_size(axis)
    return lax.ppermute(value, axis, [(i, i ^ bit) for i in range(size)])


def tie(value, *others):
    return lax.optimization_barrier((value, *others))[0] if others else value


def rms_scale(values):
    return lax.rsqrt(jnp.mean(values * values, axis=-1, keepdims=True) + NORM_EPS)


def along_z(yj, first=0):
    return [((zj,), 2 * zj + yj, first) for zj in range(4)]


class Gather:
    def __init__(self, shard):
        self.whole = lax.axis_size("fsdp") != 8
        self.shard = shard

    def start(self, *after):
        shard = tie(self.shard, *after)
        if self.whole:
            gathered = lax.all_gather(shard, "fsdp", axis=0, tiled=True)
            self.own, self.other = [(gathered, [])], [(swap(gathered, "tx", 1), [])]
            self.along_z = self.along_xy = self.last = self.ready = (gathered,)
            return
        self.along_z = tuple(swap(shard, "fsdp", 2 * j) for j in (1, 2, 3))

    def middle(self, *after):
        if self.whole:
            return
        stacked = jnp.stack((self.shard, tie(self.along_z[0], *after), *self.along_z[1:]))
        self.ready = (stacked,)
        self.along_xy = (swap(stacked, "fsdp", 1), swap(stacked, "tx", 1))
        self.own = [(stacked, along_z(0)), (self.along_xy[0], along_z(1))]

    def finish(self, *after):
        if self.whole:
            return
        half = self.shard.shape[0] // 2
        from_y, from_x = tie(self.along_xy[0], *after), tie(self.along_xy[1], *after)
        self.last = (swap(from_y[:, :half], "tx", 1), swap(from_x[:, half:], "fsdp", 1))
        self.other = [(self.along_xy[1], along_z(0)), (self.last[0], along_z(1)), (self.last[1], along_z(1, half))]


class GatherLastZ:
    def __init__(self, shard):
        self.whole = lax.axis_size("fsdp") != 8
        self.shard = shard
        self.from_x = swap(shard, "tx", 1)
        self.from_y = self.last = (self.from_x,)

    def middle(self, *after):
        if self.whole:
            return
        self.pair = jnp.stack([self.shard, tie(self.from_x, *after)])
        self.from_y = (swap(self.pair, "fsdp", 1),)

    def finish(self, *after):
        if self.whole:
            shards = (tie(self.shard, *after), self.from_x)
            self.own, self.other = [
                [(lax.all_gather(part, "fsdp", axis=0, tiled=True), [])] for part in shards
            ]
            self.last = (self.own[0][0], self.other[0][0])
            return
        square = jnp.stack([self.pair, tie(self.from_y[0], *after)])
        self.last = tuple(swap(square, "fsdp", 2 * j) for j in (1, 2, 3))
        self.own, self.other = [
            [
                (array, [((yj, r), 2 * zj + yj, 0) for yj in range(2)])
                for zj, array in enumerate((square, *self.last))
            ]
            for r in range(2)
        ]


class HalvesGather:
    def __init__(self, halves):
        self.whole = lax.axis_size("fsdp") != 8
        self.halves = halves
        self.along_z, self.along_xy, self.stacked = [None, None], [None, None], [None, None]

    def start(self, n, *after):
        half = tie(self.halves[n], *after)
        if self.whole:
            self.along_z[n] = (half,)
            return
        self.along_z[n] = tuple(swap(half, "fsdp", 2 * j) for j in (1, 2, 3))

    def middle(self, n, *after):
        if self.whole:
            self.along_xy[n] = self.along_z[n]
            return
        self.stacked[n] = jnp.stack((self.halves[n], tie(self.along_z[n][0], *after), *self.along_z[n][1:]))
        self.along_xy[n] = (swap(self.stacked[n], "fsdp", 1), swap(self.stacked[n], "tx", 1))

    def finish(self, *after):
        if self.whole:
            shard = tie(jnp.concatenate(self.halves), *after)
            gathered = lax.all_gather(shard, "fsdp", axis=0, tiled=True)
            self.own, self.other = [(gathered, [])], [(swap(gathered, "tx", 1), [])]
            self.last = (self.other[0][0],)
            return
        (first_y, first_x), (second_y, second_x) = self.along_xy
        half = self.halves[0].shape[0]
        self.last = (swap(tie(first_y, *after), "tx", 1), swap(tie(second_x, *after), "fsdp", 1))
        self.own = [
            (self.stacked[0], along_z(0)), (first_y, along_z(1)), (self.stacked[1], along_z(0, half)), (second_y, along_z(1, half)),
        ]
        self.other = [
            (first_x, along_z(0)), (self.last[0], along_z(1)), (second_x, along_z(0, half)), (self.last[1], along_z(1, half)),
        ]


class Reduction:
    def __init__(self):
        self.whole = lax.axis_size("fsdp") != 8

    def send_far(self, other):
        self.other = other
        if self.whole:
            self.sent_far = other
            return
        self.sent_far = (swap(other[0], "tx", 1), swap(other[1], "fsdp", 1))

    def split(self, count):
        parts = [Reduction() for _ in range(count)]
        for c, p in enumerate(parts):
            if self.whole:
                p.other = p.sent_far = (self.other[c],)
            else:
                p.sent_far = tuple(r[c] for r in self.sent_far)
                p.other = (None, None, self.other[2 + c])
        return parts

    def send_xy(self, own, *after):
        self.own = own
        if self.whole:
            self.from_x, self.from_y = swap(self.other[0], "tx", 1), own[0]
            self.ready = (own[0],)
            return
        self.ready = add_halves(self.other[2], own[0], self.sent_far, after)
        self.from_x, self.from_y = swap(self.ready[0], "tx", 1), swap(self.ready[1], "fsdp", 1)

    def send_z(self, *after):
        if self.whole:
            total = self.own[0] + tie(self.from_x, *after)
            self.ready = (total,)
            self.parts = (lax.psum_scatter(total, "fsdp", scatter_dimension=0, tiled=True),)
            return
        self.ready = sum_pieces(tie(self.own[1], *after), self.from_x, self.from_y)
        self.parts = (self.ready[0], *(swap(self.ready[j], "fsdp", 2 * j) for j in (1, 2, 3)))

    def total(self):
        return sum(piece.astype(F32) for piece in self.parts)


def relay(done, going, own, *after):
    if done.whole:
        done.send_z(*after)
        going.send_xy(own, *after)
        return
    _, rows, cols = done.own[1].shape

    def kernel(near, from_x, from_y, next_near, far, next_x, next_y, *outs):
        *sums, along_x, along_y = outs
        for j, out in enumerate(sums):
            total = near[j].astype(F32) + from_x[j].astype(F32) + from_y[j].astype(F32)
            out[...] = total.astype(out.dtype)
        half = far.shape[1] // 2
        along_x[:, :half] = next_near[:, :half]
        along_x[:, half:] = (next_near[:, half:].astype(F32) + next_y[...].astype(F32)).astype(BF16)
        along_y[:, :half] = (far[:, :half].astype(F32) + next_x[...].astype(F32)).astype(BF16)
        along_y[:, half:] = far[:, half:]

    out_shape = [jax.ShapeDtypeStruct((rows, cols), BF16 if j else F32) for j in range(4)]
    out_shape += [jax.ShapeDtypeStruct(own[0].shape, BF16)] * 2
    args = (tie(done.own[1], *after), done.from_x, done.from_y, going.other[2], own[0], *going.sent_far)
    outs = call(kernel, "relay", [VMEM] * 7, tuple(out_shape), [], 0.01, *args, near=True)
    going.own, going.ready, done.ready = own, outs[4:], outs[:4]
    done.parts = (outs[0], *(swap(outs[j], "fsdp", 2 * j) for j in (1, 2, 3)))
    going.from_x, going.from_y = swap(outs[4], "tx", 1), swap(outs[5], "fsdp", 1)


class ReductionFirstZ:
    def __init__(self, squares):
        self.whole = lax.axis_size("fsdp") != 8
        self.squares = squares

    def send_z(self, *after):
        if self.whole:
            total = self.squares[0] + swap(tie(self.squares, *after)[1], "tx", 1)
            self.from_z = (lax.psum_scatter(total, "fsdp", scatter_dimension=0, tiled=True),)
            return
        squares = tie(self.squares, *after)
        self.from_z = tuple(swap(squares[j], "fsdp", 2 * j) for j in (1, 2, 3))

    def send_y(self, *after):
        if self.whole:
            self.from_y = self.from_z[0]
            return
        self.square = sum_squares(tie(self.squares, *after), self.from_z)
        self.from_y = swap(self.square[1], "fsdp", 1)

    def send_x(self, *after):
        if self.whole:
            self.from_x = self.from_z[0]
            return
        self.pair = add(self.square[0], tie(self.from_y, *after))
        self.from_x = swap(self.pair[1], "tx", 1)

    def total(self):
        if self.whole:
            return self.from_x.astype(F32)
        return self.pair[0].astype(F32) + self.from_x.astype(F32)


def add(a, b):
    return (a.astype(F32) + b.astype(F32)).astype(BF16)


def sum_squares(squares, from_z):
    def kernel(squares, *refs):
        *from_z, near, far = refs
        for n, out in enumerate((near, far)):
            for r in range(2):
                total = squares[0, 2 * n + r].astype(F32)
                for piece in from_z:
                    total = total + piece[2 * n + r].astype(F32)
                out[r] = total.astype(BF16)

    out_shape = (jax.ShapeDtypeStruct((2, *squares.shape[2:]), BF16),) * 2
    return call(kernel, "sum_squares", [VMEM] * 4, out_shape, [], 0.01, squares, *from_z)


def sum_pieces(near, from_x, from_y):
    def kernel(near, from_x, from_y, *outs):
        for j, out in enumerate(outs):
            total = near[j].astype(F32) + from_x[j].astype(F32) + from_y[j].astype(F32)
            out[...] = total.astype(out.dtype)

    _, rows, cols = near.shape
    out_shape = tuple(jax.ShapeDtypeStruct((rows, cols), BF16 if j else F32) for j in range(4))
    return call(kernel, "sum_pieces", [VMEM] * 3, out_shape, [], 0.01, near, from_x, from_y)


def add_halves(near, far, sent_far, after):
    def kernel(near, far, from_x, from_y, along_x, along_y):
        half = near.shape[1] // 2
        along_x[:, :half] = near[:, :half]
        along_x[:, half:] = (near[:, half:].astype(F32) + from_y[...].astype(F32)).astype(BF16)
        along_y[:, :half] = (far[:, :half].astype(F32) + from_x[...].astype(F32)).astype(BF16)
        along_y[:, half:] = far[:, half:]

    out_shape = (jax.ShapeDtypeStruct(near.shape, BF16), jax.ShapeDtypeStruct(far.shape, BF16))
    return call(kernel, "add_halves", [VMEM] * 4, out_shape, [], 0.01, tie(near, *after), far, *sent_far, near=True)


VMEM = pl.BlockSpec(memory_space=pltpu.VMEM)
ANY = pl.BlockSpec(memory_space=pl.ANY)
SMEM = pl.BlockSpec(memory_space=pltpu.SMEM)


def call(kernel, name, in_specs, out_shape, scratch_shapes, micros, *args, near=False, away=(), away_out=()):
    out_specs = jax.tree.map(lambda _: VMEM, out_shape)
    if near:
        spaces = [pltpu.HBM if n in away or s is ANY else pltpu.VMEM for n, s in enumerate(in_specs)]
        args = [
            a if s is SMEM else pltpu.with_memory_space_constraint(a, space)
            for a, s, space in zip(args, in_specs, spaces)
        ]
        out_shape = jax.tree.map(lambda o: pltpu.VMEM(o.shape, o.dtype), out_shape)
        if away_out:
            out_shape = [pltpu.HBM(o.shape, o.dtype) if n in away_out else o for n, o in enumerate(out_shape)]
            out_specs = [ANY if n in away_out else VMEM for n in range(len(out_shape))]
    return pl.pallas_call(
        kernel,
        in_specs=in_specs,
        out_specs=out_specs,
        out_shape=out_shape,
        scratch_shapes=scratch_shapes,
        compiler_params=pltpu.CompilerParams(vmem_limit_bytes=VMEM_BYTES),
        cost_estimate=pl.CostEstimate(flops=int(micros * 1e9), bytes_accessed=1 << 10, transcendentals=0),
        name=name,
    )(*args)


def place_pieces(refs, entries, weight, rank, cols=slice(None), width=None, first_col=0):
    if len(refs) == 1 and not entries[0]:
        weight[:, first_col : first_col + width] = refs[0][:, cols]
        return
    shard = weight.shape[0] // 8
    for ref, places in zip(refs, entries):
        for index, j, first in places:
            piece = ref[(*index, slice(None), cols)]
            start = pl.multiple_of((rank ^ j) * shard + first, 16)
            weight[pl.ds(start, piece.shape[0]), first_col : first_col + width] = piece


def far_shapes(depth, cols, size, own, parts=1):
    if size != 8:
        return (jax.ShapeDtypeStruct((depth, cols // parts), BF16),) * parts
    rows = depth // 8
    near = (jax.ShapeDtypeStruct((4, rows, cols // parts), BF16),) * parts
    if own:
        return (*near, *near)
    lead = (parts,) if parts > 1 else ()
    return (jax.ShapeDtypeStruct((*lead, 4, rows // 2, cols // parts), BF16),) * 2 + near


def put_pieces(refs, block, start, rank, own, part=None):
    if len(refs[0].shape) == 2:
        refs[part or 0][start : start + block.shape[0], :] = block
        return
    near = refs[len(refs) // 2 + (part or 0)] if own else refs[2 + (part or 0)]
    rows = near.shape[1]
    for n in range(block.shape[0] // rows):
        j = (start // rows + n) ^ rank
        yj, zj = j & 1, j >> 1
        piece = block[n * rows : (n + 1) * rows]

        @pl.when(yj == 0)
        def _():
            near[zj] = piece

        @pl.when(yj == 1)
        def _():
            if own:
                refs[part or 0][zj] = piece
            elif part is None:
                refs[0][zj] = piece[: rows // 2]
                refs[1][zj] = piece[rows // 2 :]
            else:
                refs[0][part, zj] = piece[: rows // 2]
                refs[1][part, zj] = piece[rows // 2 :]


def assemble(place, gathers, depth, width):
    lists = [pieces for g in gathers for pieces in (g.own, g.other)]
    entries = [[p[1] for p in pieces] for pieces in lists]
    arrays = [p[0] for pieces in lists for p in pieces]
    counts = [pieces[0][0].shape[-1] for pieces in lists[::2]]
    parts = sum(counts) // width

    def kernel(place, *refs):
        pieces, outs = refs[: len(arrays)], refs[len(arrays) :]
        at, first = 0, 0
        for n, places in enumerate(entries):
            refs_n = pieces[at : at + len(places)]
            at += len(places)
            for i in range(counts[n // 2] // width):
                cols = slice(i * width, (i + 1) * width)
                place_pieces(refs_n, places, outs[first + i], place[1], cols, width, n % 2 * width)
            if n % 2:
                first += counts[n // 2] // width

    out_shape = tuple(jax.ShapeDtypeStruct((depth, 2 * width), BF16) for _ in range(parts))
    return call(kernel, "assemble", [SMEM] + [VMEM] * len(arrays), out_shape, [], 3, place, *arrays, near=True)


def pack_qkv(weights, vectors, chunks):
    _, shard, width = weights.shape
    part = width // chunks
    cols = -(-(3 * width + 8) // 128) * 128

    def kernel(weights, vectors, *outs):
        blocks = [weights[i, :, c * part : (c + 1) * part] for c in range(chunks) for i in range(3)]
        blocks += [vectors[...].T, jnp.zeros((shard, cols - 3 * width - 8), F32)]
        packed = jnp.concatenate(blocks, axis=1).astype(BF16)
        for n, out in enumerate(outs):
            out[...] = packed[n * shard // 2 : (n + 1) * shard // 2]

    out_shape = (jax.ShapeDtypeStruct((shard // 2, cols), BF16),) * 2
    return call(kernel, "pack_qkv", [VMEM] * 2, out_shape, [], 1, weights, vectors)


BIAS_ROWS = sum((i + 1) * BQ for i in range(LEN // BQ))


def bias_rows(i):
    start = i * (i + 1) // 2 * BQ
    return slice(start, start + (i + 1) * BQ)


def mask_bias(doc_col, doc_row, bias):
    for i in range(LEN // BQ):
        lo, hi = i * BQ, (i + 1) * BQ
        same = doc_col[:hi, :] == doc_row[:, lo:hi]
        keys = lax.broadcasted_iota(jnp.int32, (hi, BQ), 0)
        queries = lax.broadcasted_iota(jnp.int32, (hi, BQ), 1) + lo
        bias[bias_rows(i), :] = jnp.where(same & (keys <= queries), 0.0, NEG_FILL)


def outer_rows(lo, rows, core):
    half = LEN // 2
    return pl.ds(pl.multiple_of(((lo // half) ^ core) * half + lo % half, rows), rows)


def head_rows(ref, block, columns, rows):
    for h in range(ref.shape[0]):
        ref[h, rows, :] = block[:, columns[h] : columns[h] + HD].astype(ref.dtype)


def join_heads(ref, heads):
    return jnp.concatenate([ref[h] for h in heads], axis=1)


def attn_forward(place, pieces, rows_in, scale, doc_col, doc_row, chunks, depth):
    arrays, places = [p[0] for p in pieces], [p[1] for p in pieces]
    cols = arrays[0].shape[-1]
    fresh = len(rows_in) == 2
    part = scale.shape[1] // 3
    per_chunk = part // HD
    heads = per_chunk * chunks
    starts = [[c * 3 * part + n * part + h * HD for c in range(chunks) for h in range(per_chunk)] for n in range(3)]

    def kernel(place, *refs):
        pieces, refs = refs[: len(arrays)], refs[len(arrays) :]
        sources, (scale, doc_col, doc_row) = refs[: len(rows_in)], refs[len(rows_in) : len(rows_in) + 3]
        outs = refs[len(rows_in) + 3 :]
        attns, (*away, lse) = outs[:chunks], outs[chunks : chunks + 5]
        if fresh:
            x, gains, *outs = outs[chunks + 5 :]
        else:
            x, outs = sources[0], outs[chunks + 5 :]
        bias, out_heads, query, key, value, weight, sems = outs
        copies = [
            pltpu.make_async_copy(source, target, sems.at[n])
            for n, (source, target) in enumerate(zip((query, key, value, weight), away))
        ]
        core, rank = place[0], place[1]
        half = LEN // 2
        place_pieces(pieces, places, weight, rank, slice(None), cols)
        mask_bias(doc_col, doc_row, bias)
        if fresh:
            gains[...] = weight[:, cols - 128 :].astype(F32).T
            gain = gains[64:65, :]
            for n, source in enumerate(sources):

                def norm(i, _, source=source, n=n):
                    block = pl.ds(pl.multiple_of(i * 128, 128), 128)
                    values = source[block, :].astype(F32)
                    target = pl.ds(pl.multiple_of(i * 128 + n * half, 128), 128)
                    x[target, :] = (values * rms_scale(values) * gain).astype(BF16)
                    return 0

                lax.fori_loop(0, half // 128, norm, 0)

        def project(i, _):
            lo = i * BQ
            block = dot(x[outer_rows(lo, BQ, core), :], weight[...])
            rows = pl.ds(pl.multiple_of(lo, BQ), BQ)
            scaled = jnp.concatenate(
                [block[:, c * 3 * part : c * 3 * part + part] * scale[:, :part] for c in range(chunks)], axis=1
            )
            head_rows(query, scaled, [h * HD for h in range(heads)], rows)
            head_rows(key, block, starts[1], rows)
            head_rows(value, block, starts[2], rows)
            return 0

        lax.fori_loop(0, LEN // BQ, project, 0)
        for copy in copies:
            copy.start()

        def attend(h, _):
            keys = key[h]
            value_t = value[h].T
            blocks = []
            for i in range(LEN // BQ):
                lo, hi = i * BQ, (i + 1) * BQ
                scores = dot(keys[:hi], query[h, lo:hi, :], NT) + bias[bias_rows(i), :]
                top = jnp.max(scores, axis=0, keepdims=True)
                probs = jnp.exp(scores - top)
                total = jnp.sum(probs, axis=0, keepdims=True)
                blocks.append(dot(value_t[:, :hi], probs.astype(BF16)) / total)
                lse[h, :, lo:hi] = top + jnp.log(total)
            out_heads[h] = jnp.concatenate(blocks, axis=1).T.astype(BF16)
            return 0

        def attend_two(n, _):
            attend(2 * n, 0)
            return attend(2 * n + 1, 0)

        lax.fori_loop(0, heads // 2, attend_two, 0)
        for c in range(chunks):
            joined = join_heads(out_heads, range(c * per_chunk, (c + 1) * per_chunk))
            for a in range(2):
                attns[c][outer_rows(a * half, half, core), :] = joined[a * half : (a + 1) * half]
        for copy in copies:
            copy.wait()

    per_head = jax.ShapeDtypeStruct((heads, LEN, HD), BF16)
    out_shape = (
        *(jax.ShapeDtypeStruct((LEN, part), BF16),) * chunks,
        per_head,
        per_head,
        per_head,
        jax.ShapeDtypeStruct((depth, cols), BF16),
        jax.ShapeDtypeStruct((heads, 1, LEN), F32),
    )
    scratch = [pltpu.VMEM((BIAS_ROWS, BQ), F32)] + [pltpu.VMEM((heads, LEN, HD), BF16)] * 4
    scratch += [pltpu.VMEM((depth, cols), BF16), pltpu.SemaphoreType.DMA((4,))]
    if fresh:
        out_shape += (jax.ShapeDtypeStruct((LEN, depth), BF16), jax.ShapeDtypeStruct((128, depth), F32))
    specs = [SMEM] + [VMEM] * (len(arrays) + len(rows_in) + 3)
    args = (place, *arrays, *rows_in, scale, doc_col, doc_row)
    outs = call(
        kernel, "attn_forward", specs, out_shape, scratch, 8, *args, near=True, away_out=range(chunks, chunks + 4)
    )
    saved = (*outs[chunks : chunks + 3], outs[chunks + 4])
    return outs[:chunks], saved, (outs[chunks + 3], *outs[chunks + 5 :])


SIDE = 32
SCALE_COLUMN = 4


def attn_backward(place, attns, saved, dout, x, doc_col, doc_row, scale, first, own, riders, other_sums):
    part = attns[0].shape[1]
    per_chunk = part // HD
    count = len(attns)
    heads = per_chunk * count
    depth = x.shape[1]
    size = lax.axis_size("fsdp")
    pieces_shape = far_shapes(depth, (3 * part + SIDE) * count, size, own, count)

    def kernel(place, *refs):
        attns, refs = refs[:count], refs[count:]
        *saved, lse, dout, x, doc_col, doc_row, scale, riders, other_sums = refs[:11]
        refs = refs[11:]
        grads_out, sums_out, refs = refs[:count], refs[count], refs[count + 1 :]
        pieces, refs = refs[:-10], refs[-10:]
        dkey, dvalue, bias, douts, deltas, grads, query, key, value, sems = refs
        copies = [
            pltpu.make_async_copy(source, target, sems.at[n])
            for n, (source, target) in enumerate(zip(saved, (query, key, value)))
        ]
        for copy in copies:
            copy.start()
        core, rank = place[0], place[1]
        half = LEN // 2
        lanes = lax.broadcasted_iota(jnp.int32, (8, part), 1) // HD
        selector = jnp.where(lanes == lax.broadcasted_iota(jnp.int32, (8, part), 0), 1.0, 0.0)
        mask_bias(doc_col, doc_row, bias)
        for c in range(count):
            for i in range(LEN // BQ):
                lo, hi = i * BQ, (i + 1) * BQ
                rows = outer_rows(lo, BQ, core)
                dout_block = dout[rows, first + c * part : first + (c + 1) * part]
                products = attns[c][rows, :].astype(F32) * dout_block.astype(F32)
                delta = lax.dot_general(
                    selector, products, NT, precision=lax.Precision.HIGHEST, preferred_element_type=F32
                )
                for h in range(per_chunk):
                    deltas[c * per_chunk + h, :, lo:hi] = delta[h : h + 1, :]
                    douts[c * per_chunk + h, lo:hi, :] = dout_block[:, h * HD : (h + 1) * HD]

        for copy in copies:
            copy.wait()

        def attend(h, sums):
            keys = key[h]
            key_t = keys.T
            dquery_parts = []
            for i in range(LEN // BQ):
                lo, hi = i * BQ, (i + 1) * BQ
                queries = query[h, lo:hi, :]
                dout_head = douts[h, lo:hi, :]
                scores = dot(keys[:hi], queries, NT) + bias[bias_rows(i), :]
                probs = jnp.exp(scores - lse[h, :, lo:hi])
                dprobs = dot(value[h, :hi, :], dout_head, NT)
                dscores = (probs * (dprobs - deltas[h, :, lo:hi])).astype(BF16)
                dv = dot(probs.astype(BF16), dout_head)
                dk = dot(dscores, queries)
                dquery_parts.append(dot(key_t[:, :hi], dscores))
                if i:
                    dkey[:lo] += dk[:lo]
                    dvalue[:lo] += dv[:lo]
                dkey[lo:hi] = dk[lo:]
                dvalue[lo:hi] = dv[lo:]
            dquery = jnp.concatenate(dquery_parts, axis=1).T
            grads[0, h] = (dquery * scale[...]).astype(BF16)
            grads[1, h] = dkey[...].astype(BF16)
            grads[2, h] = dvalue[...].astype(BF16)
            return sums + jnp.sum(dquery * query[h].astype(F32), axis=0, keepdims=True)

        def attend_two(n, sums):
            return attend(2 * n + 1, attend(2 * n, sums))

        sums = lax.fori_loop(0, heads // 2, attend_two, jnp.zeros((1, HD), F32))
        sums = sums / scale[...]
        sums_out[...] = sums
        side = [jnp.zeros((depth, SIDE), BF16)] * count
        if size == 8:
            columns = riders[...].T
            if own:
                scales = jnp.broadcast_to(sums + other_sums[...], (128, HD)).T[:, :8]
                block = jnp.concatenate([scales, jnp.zeros((depth // size - HD, 8), F32)])
                column = lax.broadcasted_iota(jnp.int32, (depth, 8), 1) == SCALE_COLUMN
                columns = jnp.where(column, jnp.concatenate([block] * size), columns)
            side[-1] = jnp.concatenate([columns, jnp.zeros((depth, SIDE - 8), F32)], axis=1).astype(BF16)
        for c in range(count):
            mine = range(c * per_chunk, (c + 1) * per_chunk)
            joined = jnp.concatenate([grads[n, h] for n in range(3) for h in mine], axis=1)
            for a in range(2):
                grads_out[c][outer_rows(a * half, half, core), :] = joined[a * half : (a + 1) * half]
            for g in range(2):
                start = g * depth // 2
                block = dot(x[:, start : start + depth // 2], grads_out[c][...], TN).astype(BF16)
                block = jnp.concatenate([block, side[c][start : start + depth // 2]], axis=1)
                put_pieces(pieces, block, start, rank, own, c if count > 1 else None)

    out_shape = (
        *(jax.ShapeDtypeStruct((LEN, 3 * part), BF16),) * count,
        jax.ShapeDtypeStruct((1, HD), F32),
        *pieces_shape,
    )
    scratch = [
        pltpu.VMEM((LEN, HD), F32),
        pltpu.VMEM((LEN, HD), F32),
        pltpu.VMEM((BIAS_ROWS, BQ), F32),
        pltpu.VMEM((heads, LEN, HD), BF16),
        pltpu.VMEM((heads, 1, LEN), F32),
        pltpu.VMEM((3, heads, LEN, HD), BF16),
        *(pltpu.VMEM((heads, LEN, HD), BF16),) * 3,
        pltpu.SemaphoreType.DMA((3,)),
    ]
    args = (place, *attns, *saved, dout, x, doc_col, doc_row, scale, riders, other_sums)
    specs = [SMEM] + [VMEM] * count + [ANY] * 3 + [VMEM] * (len(args) - 4 - count)
    outs = call(kernel, "attn_backward", specs, out_shape, scratch, 10, *args, near=True)
    return outs[:count], outs[count], outs[count + 1 :]


def put_both(outs, block, start, rank, size):
    width = block.shape[1] // 2
    count = len(outs) // 2 if size != 8 else 2
    put_pieces(outs[:count], block[:, :width], start, rank, True)
    put_pieces(outs[count:], block[:, width:], start, rank, False)


def weight_grads(place, pairs, name):
    rows, depth = pairs[0][0][0].shape
    width = pairs[0][1].shape[1] // 2
    size = lax.axis_size("fsdp")
    shapes = [far_shapes(depth, width * len(pairs), size, own) for own in (True, False)]

    def kernel(place, *refs):
        ins, outs = refs[: 3 * len(pairs)], refs[3 * len(pairs) :]
        for g in range(2):
            cols = slice(g * depth // 2, (g + 1) * depth // 2)
            blocks = []
            for n in range(len(pairs)):
                near, far, right = ins[3 * n : 3 * n + 3]
                block = dot(near[:, cols], right[:rows, :], TN) + dot(far[:, cols], right[rows:, :], TN)
                blocks.append(block.astype(BF16))
            joined = [b[:, r * width : (r + 1) * width] for r in range(2) for b in blocks]
            put_both(outs, jnp.concatenate(joined, axis=1), g * depth // 2, place[1], size)

    args = [a for halves, right in pairs for a in (*halves, right)]
    outs = call(
        kernel, name, [SMEM] + [VMEM] * len(args), (*shapes[0], *shapes[1]), [], 4 * len(pairs), place, *args, near=True
    )
    return outs[: len(shapes[0])], outs[len(shapes[0]) :]


def out_forward(attns, out_t, inputs):
    rows, depth = inputs.shape

    def kernel(*refs):
        attns, (out_t, inputs, sent, kept) = refs[:-4], refs[-4:]
        heads = jnp.concatenate([a[...] for a in attns], axis=1)
        for i in range(rows // BQ):
            lo, hi = i * BQ, (i + 1) * BQ
            sent[lo:hi, :] = dot(heads[rows + lo : rows + hi], out_t[...], NT).astype(BF16)
            kept[lo:hi, :] = inputs[lo:hi, :].astype(F32) + dot(heads[lo:hi], out_t[...], NT)

    out_shape = (jax.ShapeDtypeStruct((rows, depth), BF16), jax.ShapeDtypeStruct((rows, depth), F32))
    return call(kernel, "out_forward", [VMEM] * (len(attns) + 2), out_shape, [], 3, *attns, out_t, inputs, near=True)


def second_norm(kept, received, gain):
    def kernel(kept, received, gain, resid_out, normed_out):
        resid = kept[...] + received[...].astype(F32)
        resid_out[...] = resid
        normed_out[...] = (resid * rms_scale(resid) * gain[...]).astype(BF16)

    out_shape = (jax.ShapeDtypeStruct(kept.shape, F32), jax.ShapeDtypeStruct(kept.shape, BF16))
    return call(kernel, "second_norm", [VMEM] * 3, out_shape, [], 1, kept, received, gain, near=True)


def mlp(normed, cot, up, down_t, bias_up):
    rows, depth = normed[0].shape
    units = up.shape[1]

    def kernel(n_near, n_far, c_near, c_far, up, down_t, bias, hidden, grad_pre, bias_sum, *outs):
        sums = jnp.zeros((1, units), F32)
        for side, (n, c) in enumerate(((n_near, c_near), (n_far, c_far))):
            out_mlp, out_grad = outs[2 * side : 2 * side + 2]

            def step(i, sums, n=n, c=c, side=side, out_mlp=out_mlp, out_grad=out_grad):
                block = pl.ds(pl.multiple_of(i * BQ, BQ), BQ)
                target = pl.ds(pl.multiple_of(i * BQ + side * rows, BQ), BQ)
                pre = dot(n[block, :], up[...]) + bias[...]
                sig = 1.0 / (1.0 + jnp.exp(-pre))
                units_low = (pre * sig).astype(BF16)
                grad = dot(c[block, :], down_t[...])
                grad_low = (grad * (sig + pre * sig * (1.0 - sig))).astype(BF16)
                hidden[target, :] = units_low
                grad_pre[target, :] = grad_low
                out_mlp[block, :] = dot(units_low, down_t[...], NT).astype(BF16)
                out_grad[block, :] = dot(grad_low, up[...], NT).astype(BF16)
                return sums + jnp.sum(grad_low.astype(F32), axis=0, keepdims=True)

            sums = lax.fori_loop(0, rows // BQ, step, sums)
        bias_sum[...] = sums

    low = jax.ShapeDtypeStruct((rows, depth), BF16)
    out_shape = (
        jax.ShapeDtypeStruct((2 * rows, units), BF16),
        jax.ShapeDtypeStruct((2 * rows, units), BF16),
        jax.ShapeDtypeStruct((1, units), F32),
        low,
        low,
        low,
        low,
    )
    return call(kernel, "mlp", [VMEM] * 7, out_shape, [], 10, *normed, *cot, up, down_t, bias_up, near=True)


def resid_grads(grads, mlps, resid, cot, gain, bias):
    def kernel(grad_near, grad_far, mlp_near, mlp_far, resid, cot, gain, bias, low_out, sum_out, layer):
        for i in range(resid.shape[0] // BQ):
            block = slice(i * BQ, (i + 1) * BQ)
            held = resid[block, :]
            grad = grad_near[block, :].astype(F32) + grad_far[block, :].astype(F32)
            recip = rms_scale(held)
            unit = held * recip
            part = jnp.sum(grad * unit, axis=0, keepdims=True)
            sum_out[...] = part if i == 0 else sum_out[...] + part
            scaled = grad * gain[...]
            mean = jnp.mean(scaled * unit, axis=-1, keepdims=True)
            total = cot[block, :].astype(F32) + recip * (scaled - unit * mean)
            low_out[block, :] = total.astype(BF16)
            mlp = mlp_near[block, :].astype(F32) + mlp_far[block, :].astype(F32)
            layer[block, :] = (held + mlp + bias[...]).astype(BF16)

    out_shape = (
        jax.ShapeDtypeStruct(resid.shape, BF16),
        jax.ShapeDtypeStruct((1, resid.shape[1]), F32),
        jax.ShapeDtypeStruct(resid.shape, BF16),
    )
    return call(kernel, "resid_grads", [VMEM] * 8, out_shape, [], 2, *grads, *mlps, resid, cot, gain, bias, near=True)


def head_grads(place, grads, out_t, attns):
    rows, depth = grads[0].shape
    width = out_t.shape[1] // 2
    size = lax.axis_size("fsdp")
    shard = depth // size

    def kernel(place, near, far, out_t, *refs):
        attns, (heads_out, squares) = refs[:-2], refs[-2:]
        for i in range(2 * rows // BQ):
            source = near if i < rows // BQ else far
            block = slice(i * BQ % rows, i * BQ % rows + BQ)
            heads_out[i * BQ : (i + 1) * BQ, :] = dot(source[block, :], out_t[...]).astype(BF16)
        heads = jnp.concatenate([a[...] for a in attns], axis=1)
        for g in range(2):
            start = g * depth // 2
            cols = slice(start, start + depth // 2)
            block = (dot(near[:, cols], heads[:rows], TN) + dot(far[:, cols], heads[rows:], TN)).astype(BF16)
            for r in range(2):
                side = block[:, r * width : (r + 1) * width]
                if size != 8:
                    squares[r, start : start + depth // 2, :] = side
                    continue
                for n in range(side.shape[0] // shard):
                    j = (start // shard + n) ^ place[1]
                    squares[j >> 1, 2 * (j & 1) + r] = side[n * shard : (n + 1) * shard]

    squares_shape = (4, 4, shard, width) if size == 8 else (2, depth, width)
    out_shape = (jax.ShapeDtypeStruct((2 * rows, 2 * width), BF16), jax.ShapeDtypeStruct(squares_shape, BF16))
    args = (place, *grads, out_t, *attns)
    specs = [SMEM] + [VMEM] * (len(args) - 1)
    return call(kernel, "head_grads", specs, out_shape, [], 6, *args, near=True, away=range(3, len(args)))


def input_grads(grads, weights, rows):
    depth = weights[0].shape[0]
    counts = [len(g) for g in grads]

    def kernel(*refs):
        ins, weights, (sent, kept) = refs[: sum(counts)], refs[sum(counts) : -2], refs[-2:]
        for side, out in enumerate((kept, sent)):

            def step(i, _, side=side, out=out):
                total, at = None, 0
                block = pl.ds(pl.multiple_of(i * BQ + side * rows, BQ), BQ)
                for count, weight in zip(counts, weights):
                    left = jnp.concatenate([g[block, :] for g in ins[at : at + count]], axis=1)
                    at += count
                    partial = dot(left, weight[:, : left.shape[1]], NT)
                    total = partial if total is None else total + partial
                out[pl.ds(pl.multiple_of(i * BQ, BQ), BQ), :] = total.astype(BF16)
                return 0

            lax.fori_loop(0, rows // BQ, step, 0)

    out_shape = (jax.ShapeDtypeStruct((rows, depth), BF16),) * 2
    flat = [g for pair in grads for g in pair]
    return call(
        kernel, "input_grads", [VMEM] * (len(flat) + len(weights)), out_shape, [], 10, *flat, *weights, near=True
    )


def first_norm_grads(kept, received, inputs, resid_grad, gain):
    def kernel(kept, received, inputs, resid_grad, gain, grad_out):
        for i in range(inputs.shape[0] // BQ):
            block = slice(i * BQ, (i + 1) * BQ)
            values = inputs[block, :].astype(F32)
            recip = rms_scale(values)
            unit = values * recip
            scaled = (kept[block, :].astype(F32) + received[block, :].astype(F32)) * gain[...]
            mean = jnp.mean(scaled * unit, axis=-1, keepdims=True)
            grad_out[block, :] = (resid_grad[block, :].astype(F32) + recip * (scaled - unit * mean)).astype(BF16)

    out_shape = jax.ShapeDtypeStruct(inputs.shape, BF16)
    args = (kept, received, inputs, resid_grad, gain)
    return call(kernel, "first_norm_grads", [VMEM] * 5, out_shape, [], 0.01, *args)


def join_chunks(parts, weights):
    counts = [len(p) for p in parts]
    _, shard, width = weights.shape
    part = width // len(parts)

    def kernel(*refs):
        *refs, weights, out, rows = refs
        at = 0
        sums = []
        for count in counts:
            sums.append(sum(ref[...].astype(F32) for ref in refs[at : at + count]))
            at += count
        total = jnp.zeros((shard, 1), F32)
        for i in range(3):
            joined = jnp.concatenate([s[:, i * part : (i + 1) * part] for s in sums], axis=1)
            out[i] = joined
            total = total + jnp.sum(joined * weights[i].astype(BF16).astype(F32), axis=1, keepdims=True)
        side = jnp.concatenate([sums[-1][:, 3 * part : 3 * part + SIDE], jnp.zeros((shard, 128 - SIDE), F32)], axis=1)
        lane = lax.broadcasted_iota(jnp.int32, (shard, 128), 1)
        rows[...] = jnp.where(lane == SCALE_COLUMN + 1, total, side).T[:8, :]

    flat = [p for pieces in parts for p in pieces]
    out_shape = (jax.ShapeDtypeStruct((3, shard, width), F32), jax.ShapeDtypeStruct((8, shard), F32))
    return call(kernel, "join_chunks", [VMEM] * (len(flat) + 1), out_shape, [], 1, *flat, weights)


def local(
    inputs,
    doc_ids,
    w_qkv,
    w_out,
    w_up,
    up_bias,
    w_down,
    down_bias,
    attn_gain,
    mlp_gain,
    dim_scale,
    cotangent,
):
    shard, _, width = w_qkv.shape
    size = lax.axis_size("fsdp")
    depth = shard * size
    rows = inputs.shape[0]
    core, tx, rank = lax.axis_index("core"), lax.axis_index("tx"), lax.axis_index("fsdp")
    place = jnp.stack([core, rank]).astype(jnp.int32)

    chunks = 2
    heads = width // HD
    part = width // chunks
    vectors = jnp.concatenate([jnp.stack([attn_gain, mlp_gain, down_bias]), jnp.zeros((5, shard), F32)])
    qkv = HalvesGather(pack_qkv(jnp.transpose(w_qkv, (1, 0, 2)), vectors, chunks))
    rest = Gather(jnp.concatenate([w_out.T, w_up, w_down.T], axis=1).astype(BF16))
    qkv.start(0)

    input_rows = (inputs, swap(inputs, "core", 1))
    cots = (cotangent, swap(cotangent, "core", 1))
    docs = lax.dynamic_slice_in_dim(doc_ids, tx * LEN, LEN, 0)
    doc_col, doc_row = docs[:, None], docs[None, :]
    scale_base = PERDIM_BASE / math.sqrt(HD)
    query_scale = scale_base * jax.nn.softplus(dim_scale)
    colscale = jnp.concatenate([jnp.tile(query_scale, heads // chunks), jnp.ones((2 * part,), F32)])[None]

    now = (*qkv.along_z[0], input_rows[1], cots[1])
    qkv.middle(0, *now)
    qkv.start(1, *now)
    now = (*qkv.along_xy[0], *qkv.along_z[1])
    qkv.middle(1, *now)
    rest.start(*now)
    now = qkv.along_xy[1]
    qkv.finish(*now)
    own_attns, own_saved, (weight_own, normed_first, gains) = attn_forward(
        place, qkv.own, (tie(inputs, *now), input_rows[1]), colscale, doc_col, doc_row, chunks, depth
    )
    now = (own_saved[3], *rest.along_z, *qkv.last)
    rest.middle(*now)
    other_attns, other_saved, (weight_other,) = attn_forward(
        place, qkv.other, (tie(normed_first, *now, *rest.ready, *qkv.last),), colscale, doc_col, doc_row, chunks, depth
    )
    now = (other_saved[3], *rest.along_xy)
    rest.finish(*now)
    bias_far = swap(tie(up_bias, *now), "tx", 1)
    rest.other[-1] = (tie(rest.other[-1][0], bias_far), rest.other[-1][1])
    bias_up = jnp.concatenate([up_bias, bias_far])[None]
    attns = [*own_attns, *other_attns]
    gain_first, gain_second, bias_second = [gains[64 + i : 65 + i] for i in range(3)]
    out_t, up, down_t = assemble(place, (rest,), depth, width)
    sent, kept = out_forward(attns, out_t, inputs)
    resid_first, normed_own = second_norm(kept, swap(sent, "core", 1), gain_second)
    normeds = (normed_own, swap(normed_own, "core", 1))
    hidden, grad_pre, upbias_sum, mlp_kept, grad_kept, mlp_sent, grad_sent = mlp(normeds, cots, up, down_t, bias_up)
    grads = (grad_kept, swap(grad_sent, "core", 1))
    mlps = (mlp_kept, swap(mlp_sent, "core", 1))
    updown_own, updown_other = weight_grads(place, [(normeds, grad_pre), (cots, hidden)], "updown_grads")
    updown, both = Reduction(), Reduction()
    now = (updown_own[-1], grads[1], mlps[1])
    updown.send_far([tie(p, *now) for p in updown_other[:2]] + list(updown_other[2:]))
    grad_own, mlpgain_sum, layer_out = resid_grads(
        (tie(grad_kept, *now), grads[1]), mlps, resid_first, cotangent, gain_second, bias_second
    )
    grad_attn = (grad_own, swap(grad_own, "core", 1))
    grad_heads, out_grads = head_grads(place, grad_attn, out_t, attns)
    out = ReductionFirstZ(out_grads)
    out.send_z(grad_heads)
    now = (grad_heads, *updown.sent_far)
    updown.send_xy(updown_own, *now)

    downbias_sum = jnp.sum(cotangent.astype(F32), axis=0)[None]
    own_riders = other_riders = nothing = jnp.zeros((8, depth), F32)
    if size == 8:
        units = jnp.tile(upbias_sum.reshape(2, 2, shard), (1, 1, size))
        own_riders = jnp.concatenate([mlpgain_sum, downbias_sum, units[0], nothing[:4]])
        other_riders = jnp.concatenate([nothing[:2], units[1], nothing[:4]])

    def back(attns, saved, first_col, own, riders, other_sums, *now):
        dout = tie(grad_heads, *now)
        return attn_backward(
            place, attns, saved, dout, normed_first, doc_col, doc_row, query_scale[None], first_col, own, riders, other_sums
        )

    grad_other, sums_other, pieces_other = back(
        other_attns, other_saved, width, False, other_riders, query_scale[None], *now, *updown.ready
    )
    now = (sums_other, updown.from_x, updown.from_y)
    both.send_far([tie(p, *now) for p in pieces_other[:2]] + list(pieces_other[2:]))
    grad_first, sums_first, pieces_first = back(own_attns, own_saved, 0, True, own_riders, sums_other, *now)
    now = (sums_first, *both.sent_far, *out.from_z)
    first, second = both.split(chunks)
    near_far = [pieces_first[c::chunks] for c in range(chunks)]
    relay(updown, first, near_far[0], *now)
    sent, kept = input_grads(
        [[tie(grad_first[0], *first.ready, *updown.ready), grad_first[1]], list(grad_other)],
        [weight_own, weight_other], rows,
    )
    now = (sent, first.from_x, first.from_y, *updown.parts[1:])
    relay(first, second, near_far[1], *now)
    now = (second.from_x, second.from_y, *first.parts[1:])
    second.send_z(*now)
    out.send_y(*now)
    received = swap(tie(sent, *now), "core", 1)

    out.send_x()
    input_grad = first_norm_grads(kept, received, inputs, grad_own, gain_first)
    updown_grad, out_grad = updown.total(), out.total()
    second_parts = (tie(second.parts[0], out.from_x, input_grad), *second.parts[1:])
    qkv_grad, small = join_chunks([first.parts, second_parts], jnp.transpose(w_qkv, (1, 0, 2)))
    summed = small + swap(small, "core", 1)
    summed = summed + swap(summed, "tx", 1)
    if size == 8:
        upbias_grad = small[2:4].reshape(-1)
        downbias_grad, mlpgain_grad, scale_sum = summed[1], summed[0], summed[SCALE_COLUMN, :HD]
    else:
        everything = ("fsdp", "tx", "core")
        upbias_grad = lax.psum(upbias_sum[0, :width] + swap(upbias_sum[0, width:], "tx", 1), "fsdp")
        vectors = lax.psum(jnp.concatenate([downbias_sum, mlpgain_sum]), everything)
        downbias_grad, mlpgain_grad = lax.dynamic_slice_in_dim(vectors, rank * shard, shard, 1)
        scale_sum = lax.psum(sums_other + sums_first, everything)[0]
    return (
        layer_out,
        input_grad,
        jnp.transpose(qkv_grad, (1, 0, 2)),
        out_grad.T,
        updown_grad[:, :width],
        upbias_grad,
        updown_grad[:, width:].T,
        downbias_grad,
        summed[SCALE_COLUMN + 1] / attn_gain.astype(BF16).astype(F32),
        mlpgain_grad,
        scale_base * jax.nn.sigmoid(dim_scale) * scale_sum,
    )


def solution(mesh):
    size, tensor = mesh.shape["fsdp"], mesh.shape["tensor"]
    split = Mesh(mesh.devices.reshape(size, tensor // 2, 2), ("fsdp", "tx", "core"))
    tokens = P(("fsdp", "tx", "core"), None)
    tensor_axes = ("tx", "core")
    in_specs = (
        tokens,
        P("fsdp"),
        P("fsdp", None, tensor_axes),
        P(tensor_axes, "fsdp"),
        P("fsdp", tensor_axes),
        P(tensor_axes),
        P(tensor_axes, "fsdp"),
        P("fsdp"),
        P("fsdp"),
        P("fsdp"),
        P(),
        tokens,
    )
    out_specs = (
        tokens,
        tokens,
        P("fsdp", None, tensor_axes),
        P(tensor_axes, "fsdp"),
        P("fsdp", tensor_axes),
        P(tensor_axes),
        P(tensor_axes, "fsdp"),
        P("fsdp"),
        P("fsdp"),
        P("fsdp"),
        P(),
    )
    return jax.shard_map(local, mesh=split, in_specs=in_specs, out_specs=out_specs, check_vma=False)
```

```python
import math

import jax
import jax.numpy as jnp
from jax import lax
from jax.experimental import pallas as pl
from jax.experimental.pallas import tpu as pltpu
from jax.sharding import Mesh
from jax.sharding import PartitionSpec as P

HD = 80
LEN = 1024
BQ = 256
NORM_EPS = 1e-06
PERDIM_BASE = 1.442695041
NEG_FILL = -1e30
VMEM_BYTES = 16 << 20
BF16 = jnp.bfloat16
F32 = jnp.float32
NT = (((1,), (1,)), ((), ()))
NN = (((1,), (0,)), ((), ()))
TN = (((0,), (0,)), ((), ()))


def dot(a, b, dims=NN):
    return lax.dot_general(a, b, dims, preferred_element_type=F32)


def swap(value, axis, bit):
    size = lax.axis_size(axis)
    return lax.ppermute(value, axis, [(i, i ^ bit) for i in range(size)])


def tie(value, *others):
    return lax.optimization_barrier((value, *others))[0] if others else value


def rms_scale(values):
    return lax.rsqrt(jnp.mean(values * values, axis=-1, keepdims=True) + NORM_EPS)


def along_z(yj, first=0):
    return [((zj,), 2 * zj + yj, first) for zj in range(4)]


class Gather:
    def __init__(self, shard):
        self.whole = lax.axis_size("fsdp") != 8
        self.shard = shard

    def start(self, *after):
        shard = tie(self.shard, *after)
        if self.whole:
            gathered = lax.all_gather(shard, "fsdp", axis=0, tiled=True)
            self.own, self.other = [(gathered, [])], [(swap(gathered, "tx", 1), [])]
            self.along_z = self.along_xy = self.last = self.ready = (gathered,)
            return
        self.along_z = tuple(swap(shard, "fsdp", 2 * j) for j in (1, 2, 3))

    def middle(self, *after):
        if self.whole:
            return
        stacked = jnp.stack((self.shard, tie(self.along_z[0], *after), *self.along_z[1:]))
        self.ready = (stacked,)
        self.along_xy = (swap(stacked, "fsdp", 1), swap(stacked, "tx", 1))
        self.own = [(stacked, along_z(0)), (self.along_xy[0], along_z(1))]

    def finish(self, *after):
        if self.whole:
            return
        half = self.shard.shape[0] // 2
        from_y, from_x = tie(self.along_xy[0], *after), tie(self.along_xy[1], *after)
        self.last = (swap(from_y[:, :half], "tx", 1), swap(from_x[:, half:], "fsdp", 1))
        self.other = [(self.along_xy[1], along_z(0)), (self.last[0], along_z(1)), (self.last[1], along_z(1, half))]


class Columns:
    def __init__(self, gather, columns):
        self.gather, self.columns, self.whole = gather, columns, gather.whole

    def middle(self, *after):
        if self.whole:
            self.along_xy = self.ready = ()
            return
        parts = (self.gather.shard, *(tie(piece, *after) for piece in self.gather.along_z))
        stacked = jnp.stack([p[:, self.columns] for p in parts])
        self.ready = (stacked,)
        self.along_xy = (swap(stacked, "fsdp", 1), swap(stacked, "tx", 1))
        self.own = [(stacked, along_z(0)), (self.along_xy[0], along_z(1))]

    def finish(self, *after):
        if self.whole:
            self.own, self.other = [
                [(tie(side[0][0], *after)[:, self.columns], [])] for side in (self.gather.own, self.gather.other)
            ]
            self.last = ()
            return
        half = self.gather.shard.shape[0] // 2
        from_y, from_x = tie(self.along_xy[0], *after), tie(self.along_xy[1], *after)
        self.last = (swap(from_y[:, :half], "tx", 1), swap(from_x[:, half:], "fsdp", 1))
        self.other = [(self.along_xy[1], along_z(0)), (self.last[0], along_z(1)), (self.last[1], along_z(1, half))]


class HalvesGather:
    def __init__(self, halves):
        self.whole = lax.axis_size("fsdp") != 8
        self.halves = halves
        self.along_z, self.along_xy, self.stacked = [None, None], [None, None], [None, None]

    def start(self, n, *after):
        half = tie(self.halves[n], *after)
        if self.whole:
            self.along_z[n] = (half,)
            return
        self.along_z[n] = tuple(swap(half, "fsdp", 2 * j) for j in (1, 2, 3))

    def middle(self, n, *after):
        if self.whole:
            self.along_xy[n] = self.along_z[n]
            return
        self.stacked[n] = jnp.stack((self.halves[n], tie(self.along_z[n][0], *after), *self.along_z[n][1:]))
        self.along_xy[n] = (swap(self.stacked[n], "fsdp", 1), swap(self.stacked[n], "tx", 1))

    def finish(self, *after):
        if self.whole:
            shard = tie(jnp.concatenate(self.halves), *after)
            gathered = lax.all_gather(shard, "fsdp", axis=0, tiled=True)
            self.own, self.other = [(gathered, [])], [(swap(gathered, "tx", 1), [])]
            self.last = (self.other[0][0],)
            return
        (first_y, first_x), (second_y, second_x) = self.along_xy
        half = self.halves[0].shape[0]
        self.last = (swap(tie(first_y, *after), "tx", 1), swap(tie(second_x, *after), "fsdp", 1))
        self.own = [
            (self.stacked[0], along_z(0)), (first_y, along_z(1)), (self.stacked[1], along_z(0, half)), (second_y, along_z(1, half)),
        ]
        self.other = [
            (first_x, along_z(0)), (self.last[0], along_z(1)), (second_x, along_z(0, half)), (self.last[1], along_z(1, half)),
        ]


class Reduction:
    def __init__(self):
        self.whole = lax.axis_size("fsdp") != 8

    def send_far(self, other):
        self.other = other
        if self.whole:
            self.sent_far = other
            return
        self.sent_far = (swap(other[0], "tx", 1), swap(other[1], "fsdp", 1))

    def split(self, count):
        parts = [Reduction() for _ in range(count)]
        for c, p in enumerate(parts):
            if self.whole:
                p.other = p.sent_far = (self.other[c],)
            else:
                p.sent_far = tuple(r[c] for r in self.sent_far)
                p.other = (None, None, self.other[2 + c])
        return parts

    def send_xy(self, own, *after):
        self.own = own
        if self.whole:
            self.from_x, self.from_y = swap(self.other[0], "tx", 1), own[0]
            self.ready = (own[0],)
            return
        self.ready = add_halves(self.other[2], own[0], self.sent_far, after)
        self.from_x, self.from_y = swap(self.ready[0], "tx", 1), swap(self.ready[1], "fsdp", 1)

    def send_z(self, *after):
        if self.whole:
            total = self.own[0] + tie(self.from_x, *after)
            self.ready = (total,)
            self.parts = (lax.psum_scatter(total, "fsdp", scatter_dimension=0, tiled=True),)
            return
        self.ready = sum_pieces(tie(self.own[1], *after), self.from_x, self.from_y)
        self.parts = (self.ready[0], *(swap(self.ready[j], "fsdp", 2 * j) for j in (1, 2, 3)))

    def total(self):
        return sum(piece.astype(F32) for piece in self.parts)


def relay(done, going, own, *after):
    if done.whole:
        done.send_z(*after)
        going.send_xy(own, *after)
        return
    _, rows, cols = done.own[1].shape

    def kernel(near, from_x, from_y, next_near, far, next_x, next_y, *outs):
        *sums, along_x, along_y = outs
        for j, out in enumerate(sums):
            total = near[j].astype(F32) + from_x[j].astype(F32) + from_y[j].astype(F32)
            out[...] = total.astype(out.dtype)
        half = far.shape[1] // 2
        along_x[:, :half] = next_near[:, :half]
        along_x[:, half:] = (next_near[:, half:].astype(F32) + next_y[...].astype(F32)).astype(BF16)
        along_y[:, :half] = (far[:, :half].astype(F32) + next_x[...].astype(F32)).astype(BF16)
        along_y[:, half:] = far[:, half:]

    out_shape = [jax.ShapeDtypeStruct((rows, cols), BF16 if j else F32) for j in range(4)]
    out_shape += [jax.ShapeDtypeStruct(own[0].shape, BF16)] * 2
    args = (tie(done.own[1], *after), done.from_x, done.from_y, going.other[2], own[0], *going.sent_far)
    outs = call(kernel, "relay", [VMEM] * 7, tuple(out_shape), [], 0.01, *args, near=True)
    going.own, going.ready, done.ready = own, outs[4:], outs[:4]
    done.parts = (outs[0], *(swap(outs[j], "fsdp", 2 * j) for j in (1, 2, 3)))
    going.from_x, going.from_y = swap(outs[4], "tx", 1), swap(outs[5], "fsdp", 1)


class ReductionFirstZ:
    def __init__(self, squares):
        self.whole = lax.axis_size("fsdp") != 8
        self.squares = squares

    def send_z(self, *after):
        if self.whole:
            total = self.squares[0] + swap(tie(self.squares, *after)[1], "tx", 1)
            self.from_z = (lax.psum_scatter(total, "fsdp", scatter_dimension=0, tiled=True),)
            return
        squares = tie(self.squares, *after)
        self.from_z = tuple(swap(squares[j], "fsdp", 2 * j) for j in (1, 2, 3))

    def send_y(self, *after):
        if self.whole:
            self.from_y = self.from_z[0]
            return
        self.square = sum_squares(tie(self.squares, *after), self.from_z)
        self.from_y = swap(self.square[1], "fsdp", 1)

    def send_x(self, *after):
        if self.whole:
            self.from_x = self.from_z[0]
            return
        self.pair = add(self.square[0], tie(self.from_y, *after))
        self.from_x = swap(self.pair[1], "tx", 1)

    def total(self):
        if self.whole:
            return self.from_x.astype(F32)
        return self.pair[0].astype(F32) + self.from_x.astype(F32)


def add(a, b):
    return (a.astype(F32) + b.astype(F32)).astype(BF16)


def sum_squares(squares, from_z):
    def kernel(squares, *refs):
        *from_z, near, far = refs
        for n, out in enumerate((near, far)):
            for r in range(2):
                total = squares[0, 2 * n + r].astype(F32)
                for piece in from_z:
                    total = total + piece[2 * n + r].astype(F32)
                out[r] = total.astype(BF16)

    out_shape = (jax.ShapeDtypeStruct((2, *squares.shape[2:]), BF16),) * 2
    return call(kernel, "sum_squares", [VMEM] * 4, out_shape, [], 0.01, squares, *from_z)


def sum_pieces(near, from_x, from_y):
    def kernel(near, from_x, from_y, *outs):
        for j, out in enumerate(outs):
            total = near[j].astype(F32) + from_x[j].astype(F32) + from_y[j].astype(F32)
            out[...] = total.astype(out.dtype)

    _, rows, cols = near.shape
    out_shape = tuple(jax.ShapeDtypeStruct((rows, cols), BF16 if j else F32) for j in range(4))
    return call(kernel, "sum_pieces", [VMEM] * 3, out_shape, [], 0.01, near, from_x, from_y)


def add_halves(near, far, sent_far, after):
    def kernel(near, far, from_x, from_y, along_x, along_y):
        half = near.shape[1] // 2
        along_x[:, :half] = near[:, :half]
        along_x[:, half:] = (near[:, half:].astype(F32) + from_y[...].astype(F32)).astype(BF16)
        along_y[:, :half] = (far[:, :half].astype(F32) + from_x[...].astype(F32)).astype(BF16)
        along_y[:, half:] = far[:, half:]

    out_shape = (jax.ShapeDtypeStruct(near.shape, BF16), jax.ShapeDtypeStruct(far.shape, BF16))
    return call(kernel, "add_halves", [VMEM] * 4, out_shape, [], 0.01, tie(near, *after), far, *sent_far, near=True)


VMEM = pl.BlockSpec(memory_space=pltpu.VMEM)
ANY = pl.BlockSpec(memory_space=pl.ANY)
SMEM = pl.BlockSpec(memory_space=pltpu.SMEM)


def call(kernel, name, in_specs, out_shape, scratch_shapes, micros, *args, near=False, away=(), away_out=()):
    out_specs = jax.tree.map(lambda _: VMEM, out_shape)
    if near:
        spaces = [pltpu.HBM if n in away or s is ANY else pltpu.VMEM for n, s in enumerate(in_specs)]
        args = [
            a if s is SMEM else pltpu.with_memory_space_constraint(a, space)
            for a, s, space in zip(args, in_specs, spaces)
        ]
        out_shape = jax.tree.map(lambda o: pltpu.VMEM(o.shape, o.dtype), out_shape)
        if away_out:
            out_shape = [pltpu.HBM(o.shape, o.dtype) if n in away_out else o for n, o in enumerate(out_shape)]
            out_specs = [ANY if n in away_out else VMEM for n in range(len(out_shape))]
    return pl.pallas_call(
        kernel,
        in_specs=in_specs,
        out_specs=out_specs,
        out_shape=out_shape,
        scratch_shapes=scratch_shapes,
        compiler_params=pltpu.CompilerParams(vmem_limit_bytes=VMEM_BYTES),
        cost_estimate=pl.CostEstimate(flops=int(micros * 1e9), bytes_accessed=1 << 10, transcendentals=0),
        name=name,
    )(*args)


def place_pieces(refs, entries, weight, rank, cols=slice(None), width=None, first_col=0):
    if len(refs) == 1 and not entries[0]:
        weight[:, first_col : first_col + width] = refs[0][:, cols]
        return
    shard = weight.shape[0] // 8
    for ref, places in zip(refs, entries):
        for index, j, first in places:
            piece = ref[(*index, slice(None), cols)]
            start = pl.multiple_of((rank ^ j) * shard + first, 16)
            weight[pl.ds(start, piece.shape[0]), first_col : first_col + width] = piece


def far_shapes(depth, cols, size, own, parts=1):
    if size != 8:
        return (jax.ShapeDtypeStruct((depth, cols // parts), BF16),) * parts
    rows = depth // 8
    near = (jax.ShapeDtypeStruct((4, rows, cols // parts), BF16),) * parts
    if own:
        return (*near, *near)
    lead = (parts,) if parts > 1 else ()
    return (jax.ShapeDtypeStruct((*lead, 4, rows // 2, cols // parts), BF16),) * 2 + near


def put_pieces(refs, block, start, rank, own, part=None):
    if len(refs[0].shape) == 2:
        refs[part or 0][start : start + block.shape[0], :] = block
        return
    near = refs[len(refs) // 2 + (part or 0)] if own else refs[2 + (part or 0)]
    rows = near.shape[1]
    for n in range(block.shape[0] // rows):
        j = (start // rows + n) ^ rank
        yj, zj = j & 1, j >> 1
        piece = block[n * rows : (n + 1) * rows]

        @pl.when(yj == 0)
        def _():
            near[zj] = piece

        @pl.when(yj == 1)
        def _():
            if own:
                refs[part or 0][zj] = piece
            elif part is None:
                refs[0][zj] = piece[: rows // 2]
                refs[1][zj] = piece[rows // 2 :]
            else:
                refs[0][part, zj] = piece[: rows // 2]
                refs[1][part, zj] = piece[rows // 2 :]


def assemble(place, gathers, depth, width):
    lists = [pieces for g in gathers for pieces in (g.own, g.other)]
    entries = [[p[1] for p in pieces] for pieces in lists]
    arrays = [p[0] for pieces in lists for p in pieces]
    counts = [pieces[0][0].shape[-1] for pieces in lists[::2]]
    parts = sum(counts) // width

    def kernel(place, *refs):
        pieces, outs = refs[: len(arrays)], refs[len(arrays) :]
        at, first = 0, 0
        for n, places in enumerate(entries):
            refs_n = pieces[at : at + len(places)]
            at += len(places)
            for i in range(counts[n // 2] // width):
                cols = slice(i * width, (i + 1) * width)
                place_pieces(refs_n, places, outs[first + i], place[1], cols, width, n % 2 * width)
            if n % 2:
                first += counts[n // 2] // width

    out_shape = tuple(jax.ShapeDtypeStruct((depth, 2 * width), BF16) for _ in range(parts))
    return call(kernel, "assemble", [SMEM] + [VMEM] * len(arrays), out_shape, [], 3, place, *arrays, near=True)


def pack_qkv(weights, vectors, chunks):
    _, shard, width = weights.shape
    part = width // chunks
    first = shard // 2
    cols = -(-(3 * width + 8) // 128) * 128

    def kernel(weights, vectors, *outs):
        blocks = [weights[i, :, c * part : (c + 1) * part] for c in range(chunks) for i in range(3)]
        blocks += [vectors[...].T, jnp.zeros((shard, cols - 3 * width - 8), F32)]
        packed = jnp.concatenate(blocks, axis=1).astype(BF16)
        outs[0][...] = packed[:first]
        outs[1][...] = packed[first:]

    out_shape = (jax.ShapeDtypeStruct((first, cols), BF16), jax.ShapeDtypeStruct((shard - first, cols), BF16))
    return call(kernel, "pack_qkv", [VMEM] * 2, out_shape, [], 1, weights, vectors)


BIAS_ROWS = sum((i + 1) * BQ for i in range(LEN // BQ))


def bias_rows(i):
    start = i * (i + 1) // 2 * BQ
    return slice(start, start + (i + 1) * BQ)


def mask_bias(doc_col, doc_row, bias):
    for i in range(LEN // BQ):
        lo, hi = i * BQ, (i + 1) * BQ
        same = doc_col[:hi, :] == doc_row[:, lo:hi]
        keys = lax.broadcasted_iota(jnp.int32, (hi, BQ), 0)
        queries = lax.broadcasted_iota(jnp.int32, (hi, BQ), 1) + lo
        bias[bias_rows(i), :] = jnp.where(same & (keys <= queries), 0.0, NEG_FILL)


def outer_rows(lo, rows, core):
    half = LEN // 2
    return pl.ds(pl.multiple_of(((lo // half) ^ core) * half + lo % half, rows), rows)


def head_rows(ref, block, columns, rows):
    for h in range(ref.shape[0]):
        ref[h, rows, :] = block[:, columns[h] : columns[h] + HD].astype(ref.dtype)


def join_heads(ref, heads):
    return jnp.concatenate([ref[h] for h in heads], axis=1)


def attn_forward(place, pieces, rows_in, scale, doc_col, doc_row, chunks, depth):
    arrays, places = [p[0] for p in pieces], [p[1] for p in pieces]
    cols = arrays[0].shape[-1]
    fresh = len(rows_in) == 2
    part = scale.shape[1] // 3
    per_chunk = part // HD
    heads = per_chunk * chunks
    starts = [[c * 3 * part + n * part + h * HD for c in range(chunks) for h in range(per_chunk)] for n in range(3)]

    def kernel(place, *refs):
        pieces, refs = refs[: len(arrays)], refs[len(arrays) :]
        sources, (scale, doc_col, doc_row) = refs[: len(rows_in)], refs[len(rows_in) : len(rows_in) + 3]
        outs = refs[len(rows_in) + 3 :]
        attns, (*away, lse) = outs[:chunks], outs[chunks : chunks + 5]
        if fresh:
            x, gains, *outs = outs[chunks + 5 :]
        else:
            x, outs = sources[0], outs[chunks + 5 :]
        bias, out_heads, query, key, value, weight, sems = outs
        copies = [
            pltpu.make_async_copy(source, target, sems.at[n])
            for n, (source, target) in enumerate(zip((query, key, value, weight), away))
        ]
        core, rank = place[0], place[1]
        half = LEN // 2
        place_pieces(pieces, places, weight, rank, slice(None), cols)
        mask_bias(doc_col, doc_row, bias)
        if fresh:
            gains[...] = weight[:, cols - 128 :].astype(F32).T
            gain = gains[64:65, :]
            for n, source in enumerate(sources):

                def norm(i, _, source=source, n=n):
                    block = pl.ds(pl.multiple_of(i * 128, 128), 128)
                    values = source[block, :].astype(F32)
                    target = pl.ds(pl.multiple_of(i * 128 + n * half, 128), 128)
                    x[target, :] = (values * rms_scale(values) * gain).astype(BF16)
                    return 0

                lax.fori_loop(0, half // 128, norm, 0)

        def project(i, _):
            lo = i * BQ
            block = dot(x[outer_rows(lo, BQ, core), :], weight[...])
            rows = pl.ds(pl.multiple_of(lo, BQ), BQ)
            scaled = jnp.concatenate(
                [block[:, c * 3 * part : c * 3 * part + part] * scale[:, :part] for c in range(chunks)], axis=1
            )
            head_rows(query, scaled, [h * HD for h in range(heads)], rows)
            head_rows(key, block, starts[1], rows)
            head_rows(value, block, starts[2], rows)
            return 0

        lax.fori_loop(0, LEN // BQ, project, 0)
        for copy in copies:
            copy.start()

        def attend(h, _):
            keys = key[h]
            value_t = value[h].T
            blocks = []
            for i in range(LEN // BQ):
                lo, hi = i * BQ, (i + 1) * BQ
                scores = dot(keys[:hi], query[h, lo:hi, :], NT) + bias[bias_rows(i), :]
                top = jnp.max(scores, axis=0, keepdims=True)
                probs = jnp.exp(scores - top)
                total = jnp.sum(probs, axis=0, keepdims=True)
                blocks.append(dot(value_t[:, :hi], probs.astype(BF16)) / total)
                lse[h, :, lo:hi] = top + jnp.log(total)
            out_heads[h] = jnp.concatenate(blocks, axis=1).T.astype(BF16)
            return 0

        def attend_two(n, _):
            attend(2 * n, 0)
            return attend(2 * n + 1, 0)

        lax.fori_loop(0, heads // 2, attend_two, 0)
        for c in range(chunks):
            joined = join_heads(out_heads, range(c * per_chunk, (c + 1) * per_chunk))
            for a in range(2):
                attns[c][outer_rows(a * half, half, core), :] = joined[a * half : (a + 1) * half]
        for copy in copies:
            copy.wait()

    per_head = jax.ShapeDtypeStruct((heads, LEN, HD), BF16)
    out_shape = (
        *(jax.ShapeDtypeStruct((LEN, part), BF16),) * chunks,
        per_head,
        per_head,
        per_head,
        jax.ShapeDtypeStruct((depth, cols), BF16),
        jax.ShapeDtypeStruct((heads, 1, LEN), F32),
    )
    scratch = [pltpu.VMEM((BIAS_ROWS, BQ), F32)] + [pltpu.VMEM((heads, LEN, HD), BF16)] * 4
    scratch += [pltpu.VMEM((depth, cols), BF16), pltpu.SemaphoreType.DMA((4,))]
    if fresh:
        out_shape += (jax.ShapeDtypeStruct((LEN, depth), BF16), jax.ShapeDtypeStruct((128, depth), F32))
    specs = [SMEM] + [VMEM] * (len(arrays) + len(rows_in) + 3)
    args = (place, *arrays, *rows_in, scale, doc_col, doc_row)
    outs = call(
        kernel, "attn_forward", specs, out_shape, scratch, 8, *args, near=True, away_out=range(chunks, chunks + 4)
    )
    saved = (*outs[chunks : chunks + 3], outs[chunks + 4])
    return outs[:chunks], saved, (outs[chunks + 3], *outs[chunks + 5 :])


SIDE = 32
SCALE_COLUMN = 4


def attn_backward(place, attns, saved, dout, x, doc_col, doc_row, scale, first, own, riders, other_sums):
    part = attns[0].shape[1]
    per_chunk = part // HD
    count = len(attns)
    heads = per_chunk * count
    depth = x.shape[1]
    size = lax.axis_size("fsdp")
    pieces_shape = far_shapes(depth, (3 * part + SIDE) * count, size, own, count)

    def kernel(place, *refs):
        attns, refs = refs[:count], refs[count:]
        *saved, lse, dout, x, doc_col, doc_row, scale, riders, other_sums = refs[:11]
        refs = refs[11:]
        grads_out, sums_out, refs = refs[:count], refs[count], refs[count + 1 :]
        pieces, refs = refs[:-10], refs[-10:]
        dkey, dvalue, bias, douts, deltas, grads, query, key, value, sems = refs
        copies = [
            pltpu.make_async_copy(source, target, sems.at[n])
            for n, (source, target) in enumerate(zip(saved, (query, key, value)))
        ]
        for copy in copies:
            copy.start()
        core, rank = place[0], place[1]
        half = LEN // 2
        lanes = lax.broadcasted_iota(jnp.int32, (8, part), 1) // HD
        selector = jnp.where(lanes == lax.broadcasted_iota(jnp.int32, (8, part), 0), 1.0, 0.0)
        mask_bias(doc_col, doc_row, bias)
        for c in range(count):
            for i in range(LEN // BQ):
                lo, hi = i * BQ, (i + 1) * BQ
                rows = outer_rows(lo, BQ, core)
                dout_block = dout[rows, first + c * part : first + (c + 1) * part]
                products = attns[c][rows, :].astype(F32) * dout_block.astype(F32)
                delta = lax.dot_general(
                    selector, products, NT, precision=lax.Precision.HIGHEST, preferred_element_type=F32
                )
                for h in range(per_chunk):
                    deltas[c * per_chunk + h, :, lo:hi] = delta[h : h + 1, :]
                    douts[c * per_chunk + h, lo:hi, :] = dout_block[:, h * HD : (h + 1) * HD]

        for copy in copies:
            copy.wait()

        def attend(h, sums):
            keys = key[h]
            key_t = keys.T
            dquery_parts = []
            for i in range(LEN // BQ):
                lo, hi = i * BQ, (i + 1) * BQ
                queries = query[h, lo:hi, :]
                dout_head = douts[h, lo:hi, :]
                scores = dot(keys[:hi], queries, NT) + bias[bias_rows(i), :]
                probs = jnp.exp(scores - lse[h, :, lo:hi])
                dprobs = dot(value[h, :hi, :], dout_head, NT)
                dscores = (probs * (dprobs - deltas[h, :, lo:hi])).astype(BF16)
                dv = dot(probs.astype(BF16), dout_head)
                dk = dot(dscores, queries)
                dquery_parts.append(dot(key_t[:, :hi], dscores))
                if i:
                    dkey[:lo] += dk[:lo]
                    dvalue[:lo] += dv[:lo]
                dkey[lo:hi] = dk[lo:]
                dvalue[lo:hi] = dv[lo:]
            dquery = jnp.concatenate(dquery_parts, axis=1).T
            grads[0, h] = (dquery * scale[...]).astype(BF16)
            grads[1, h] = dkey[...].astype(BF16)
            grads[2, h] = dvalue[...].astype(BF16)
            return sums + jnp.sum(dquery * query[h].astype(F32), axis=0, keepdims=True)

        def attend_two(n, sums):
            return attend(2 * n + 1, attend(2 * n, sums))

        sums = lax.fori_loop(0, heads // 2, attend_two, jnp.zeros((1, HD), F32))
        sums = sums / scale[...]
        sums_out[...] = sums
        side = [jnp.zeros((depth, SIDE), BF16)] * count
        if size == 8:
            columns = riders[...].T
            if own:
                scales = jnp.broadcast_to(sums + other_sums[...], (128, HD)).T[:, :8]
                block = jnp.concatenate([scales, jnp.zeros((depth // size - HD, 8), F32)])
                column = lax.broadcasted_iota(jnp.int32, (depth, 8), 1) == SCALE_COLUMN
                columns = jnp.where(column, jnp.concatenate([block] * size), columns)
            side[-1] = jnp.concatenate([columns, jnp.zeros((depth, SIDE - 8), F32)], axis=1).astype(BF16)
        for c in range(count):
            mine = range(c * per_chunk, (c + 1) * per_chunk)
            joined = jnp.concatenate([grads[n, h] for n in range(3) for h in mine], axis=1)
            for a in range(2):
                grads_out[c][outer_rows(a * half, half, core), :] = joined[a * half : (a + 1) * half]
            for g in range(2):
                start = g * depth // 2
                block = dot(x[:, start : start + depth // 2], grads_out[c][...], TN).astype(BF16)
                block = jnp.concatenate([block, side[c][start : start + depth // 2]], axis=1)
                put_pieces(pieces, block, start, rank, own, c if count > 1 else None)

    out_shape = (
        *(jax.ShapeDtypeStruct((LEN, 3 * part), BF16),) * count,
        jax.ShapeDtypeStruct((1, HD), F32),
        *pieces_shape,
    )
    scratch = [
        pltpu.VMEM((LEN, HD), F32),
        pltpu.VMEM((LEN, HD), F32),
        pltpu.VMEM((BIAS_ROWS, BQ), F32),
        pltpu.VMEM((heads, LEN, HD), BF16),
        pltpu.VMEM((heads, 1, LEN), F32),
        pltpu.VMEM((3, heads, LEN, HD), BF16),
        *(pltpu.VMEM((heads, LEN, HD), BF16),) * 3,
        pltpu.SemaphoreType.DMA((3,)),
    ]
    args = (place, *attns, *saved, dout, x, doc_col, doc_row, scale, riders, other_sums)
    specs = [SMEM] + [VMEM] * count + [ANY] * 3 + [VMEM] * (len(args) - 4 - count)
    outs = call(kernel, "attn_backward", specs, out_shape, scratch, 10, *args, near=True)
    return outs[:count], outs[count], outs[count + 1 :]


def put_both(outs, block, start, rank, size):
    width = block.shape[1] // 2
    count = len(outs) // 2 if size != 8 else 2
    put_pieces(outs[:count], block[:, :width], start, rank, True)
    put_pieces(outs[count:], block[:, width:], start, rank, False)


def weight_grads(place, pairs, name):
    rows, depth = pairs[0][0][0].shape
    width = pairs[0][1].shape[1] // 2
    size = lax.axis_size("fsdp")
    shapes = [far_shapes(depth, width * len(pairs), size, own) for own in (True, False)]

    def kernel(place, *refs):
        ins, outs = refs[: 3 * len(pairs)], refs[3 * len(pairs) :]
        for g in range(2):
            cols = slice(g * depth // 2, (g + 1) * depth // 2)
            blocks = []
            for n in range(len(pairs)):
                near, far, right = ins[3 * n : 3 * n + 3]
                block = dot(near[:, cols], right[:rows, :], TN) + dot(far[:, cols], right[rows:, :], TN)
                blocks.append(block.astype(BF16))
            joined = [b[:, r * width : (r + 1) * width] for r in range(2) for b in blocks]
            put_both(outs, jnp.concatenate(joined, axis=1), g * depth // 2, place[1], size)

    args = [a for halves, right in pairs for a in (*halves, right)]
    outs = call(
        kernel, name, [SMEM] + [VMEM] * len(args), (*shapes[0], *shapes[1]), [], 4 * len(pairs), place, *args, near=True
    )
    return outs[: len(shapes[0])], outs[len(shapes[0]) :]


def out_forward(attns, out_t, inputs):
    rows, depth = inputs.shape

    def kernel(*refs):
        attns, (out_t, inputs, sent, kept) = refs[:-4], refs[-4:]
        heads = jnp.concatenate([a[...] for a in attns], axis=1)
        for i in range(rows // BQ):
            lo, hi = i * BQ, (i + 1) * BQ
            sent[lo:hi, :] = dot(heads[rows + lo : rows + hi], out_t[...], NT).astype(BF16)
            kept[lo:hi, :] = inputs[lo:hi, :].astype(F32) + dot(heads[lo:hi], out_t[...], NT)

    out_shape = (jax.ShapeDtypeStruct((rows, depth), BF16), jax.ShapeDtypeStruct((rows, depth), F32))
    return call(kernel, "out_forward", [VMEM] * (len(attns) + 2), out_shape, [], 3, *attns, out_t, inputs, near=True)


def second_norm(kept, received, gain):
    def kernel(kept, received, gain, resid_out, normed_out):
        resid = kept[...] + received[...].astype(F32)
        resid_out[...] = resid
        normed_out[...] = (resid * rms_scale(resid) * gain[...]).astype(BF16)

    out_shape = (jax.ShapeDtypeStruct(kept.shape, F32), jax.ShapeDtypeStruct(kept.shape, BF16))
    return call(kernel, "second_norm", [VMEM] * 3, out_shape, [], 1, kept, received, gain, near=True)


def mlp(normed, cot, up, down_t, bias_up):
    rows, depth = normed[0].shape
    units = up.shape[1]

    def kernel(n_near, n_far, c_near, c_far, up, down_t, bias, hidden, grad_pre, bias_sum, *outs):
        sums = jnp.zeros((1, units), F32)
        for side, (n, c) in enumerate(((n_near, c_near), (n_far, c_far))):
            out_mlp, out_grad = outs[2 * side : 2 * side + 2]

            def step(i, sums, n=n, c=c, side=side, out_mlp=out_mlp, out_grad=out_grad):
                block = pl.ds(pl.multiple_of(i * BQ, BQ), BQ)
                target = pl.ds(pl.multiple_of(i * BQ + side * rows, BQ), BQ)
                pre = dot(n[block, :], up[...]) + bias[...]
                sig = 1.0 / (1.0 + jnp.exp(-pre))
                units_low = (pre * sig).astype(BF16)
                grad = dot(c[block, :], down_t[...])
                grad_low = (grad * (sig + pre * sig * (1.0 - sig))).astype(BF16)
                hidden[target, :] = units_low
                grad_pre[target, :] = grad_low
                out_mlp[block, :] = dot(units_low, down_t[...], NT).astype(BF16)
                out_grad[block, :] = dot(grad_low, up[...], NT).astype(BF16)
                return sums + jnp.sum(grad_low.astype(F32), axis=0, keepdims=True)

            sums = lax.fori_loop(0, rows // BQ, step, sums)
        bias_sum[...] = sums

    low = jax.ShapeDtypeStruct((rows, depth), BF16)
    out_shape = (
        jax.ShapeDtypeStruct((2 * rows, units), BF16),
        jax.ShapeDtypeStruct((2 * rows, units), BF16),
        jax.ShapeDtypeStruct((1, units), F32),
        low,
        low,
        low,
        low,
    )
    return call(kernel, "mlp", [VMEM] * 7, out_shape, [], 10, *normed, *cot, up, down_t, bias_up, near=True)


def resid_grads(grads, mlps, resid, cot, gain, bias):
    def kernel(grad_near, grad_far, mlp_near, mlp_far, resid, cot, gain, bias, low_out, sum_out, layer):
        for i in range(resid.shape[0] // BQ):
            block = slice(i * BQ, (i + 1) * BQ)
            held = resid[block, :]
            grad = grad_near[block, :].astype(F32) + grad_far[block, :].astype(F32)
            recip = rms_scale(held)
            unit = held * recip
            part = jnp.sum(grad * unit, axis=0, keepdims=True)
            sum_out[...] = part if i == 0 else sum_out[...] + part
            scaled = grad * gain[...]
            mean = jnp.mean(scaled * unit, axis=-1, keepdims=True)
            total = cot[block, :].astype(F32) + recip * (scaled - unit * mean)
            low_out[block, :] = total.astype(BF16)
            mlp = mlp_near[block, :].astype(F32) + mlp_far[block, :].astype(F32)
            layer[block, :] = (held + mlp + bias[...]).astype(BF16)

    out_shape = (
        jax.ShapeDtypeStruct(resid.shape, BF16),
        jax.ShapeDtypeStruct((1, resid.shape[1]), F32),
        jax.ShapeDtypeStruct(resid.shape, BF16),
    )
    return call(kernel, "resid_grads", [VMEM] * 8, out_shape, [], 2, *grads, *mlps, resid, cot, gain, bias, near=True)


def head_grads(place, grads, out_t, attns):
    rows, depth = grads[0].shape
    width = out_t.shape[1] // 2
    size = lax.axis_size("fsdp")
    shard = depth // size

    def kernel(place, near, far, out_t, *refs):
        attns, (heads_out, squares) = refs[:-2], refs[-2:]
        for i in range(2 * rows // BQ):
            source = near if i < rows // BQ else far
            block = slice(i * BQ % rows, i * BQ % rows + BQ)
            heads_out[i * BQ : (i + 1) * BQ, :] = dot(source[block, :], out_t[...]).astype(BF16)
        heads = jnp.concatenate([a[...] for a in attns], axis=1)
        for g in range(2):
            start = g * depth // 2
            cols = slice(start, start + depth // 2)
            block = (dot(near[:, cols], heads[:rows], TN) + dot(far[:, cols], heads[rows:], TN)).astype(BF16)
            for r in range(2):
                side = block[:, r * width : (r + 1) * width]
                if size != 8:
                    squares[r, start : start + depth // 2, :] = side
                    continue
                for n in range(side.shape[0] // shard):
                    j = (start // shard + n) ^ place[1]
                    squares[j >> 1, 2 * (j & 1) + r] = side[n * shard : (n + 1) * shard]

    squares_shape = (4, 4, shard, width) if size == 8 else (2, depth, width)
    out_shape = (jax.ShapeDtypeStruct((2 * rows, 2 * width), BF16), jax.ShapeDtypeStruct(squares_shape, BF16))
    args = (place, *grads, out_t, *attns)
    specs = [SMEM] + [VMEM] * (len(args) - 1)
    return call(kernel, "head_grads", specs, out_shape, [], 6, *args, near=True, away=range(3, len(args)))


def input_grads(grads, weights, rows):
    depth = weights[0].shape[0]
    counts = [len(g) for g in grads]

    def kernel(*refs):
        ins, weights, (sent, kept) = refs[: sum(counts)], refs[sum(counts) : -2], refs[-2:]
        for side, out in enumerate((kept, sent)):

            def step(i, _, side=side, out=out):
                total, at = None, 0
                block = pl.ds(pl.multiple_of(i * BQ + side * rows, BQ), BQ)
                for count, weight in zip(counts, weights):
                    left = jnp.concatenate([g[block, :] for g in ins[at : at + count]], axis=1)
                    at += count
                    partial = dot(left, weight[:, : left.shape[1]], NT)
                    total = partial if total is None else total + partial
                out[pl.ds(pl.multiple_of(i * BQ, BQ), BQ), :] = total.astype(BF16)
                return 0

            lax.fori_loop(0, rows // BQ, step, 0)

    out_shape = (jax.ShapeDtypeStruct((rows, depth), BF16),) * 2
    flat = [g for pair in grads for g in pair]
    return call(
        kernel, "input_grads", [VMEM] * (len(flat) + len(weights)), out_shape, [], 10, *flat, *weights, near=True
    )


def first_norm_grads(kept, received, inputs, resid_grad, gain):
    def kernel(kept, received, inputs, resid_grad, gain, grad_out):
        for i in range(inputs.shape[0] // BQ):
            block = slice(i * BQ, (i + 1) * BQ)
            values = inputs[block, :].astype(F32)
            recip = rms_scale(values)
            unit = values * recip
            scaled = (kept[block, :].astype(F32) + received[block, :].astype(F32)) * gain[...]
            mean = jnp.mean(scaled * unit, axis=-1, keepdims=True)
            grad_out[block, :] = (resid_grad[block, :].astype(F32) + recip * (scaled - unit * mean)).astype(BF16)

    out_shape = jax.ShapeDtypeStruct(inputs.shape, BF16)
    args = (kept, received, inputs, resid_grad, gain)
    return call(kernel, "first_norm_grads", [VMEM] * 5, out_shape, [], 0.01, *args)


def join_chunks(parts, weights):
    counts = [len(p) for p in parts]
    _, shard, width = weights.shape
    part = width // len(parts)

    def kernel(*refs):
        *refs, weights, out, rows = refs
        at = 0
        sums = []
        for count in counts:
            sums.append(sum(ref[...].astype(F32) for ref in refs[at : at + count]))
            at += count
        total = jnp.zeros((shard, 1), F32)
        for i in range(3):
            joined = jnp.concatenate([s[:, i * part : (i + 1) * part] for s in sums], axis=1)
            out[i] = joined
            total = total + jnp.sum(joined * weights[i].astype(BF16).astype(F32), axis=1, keepdims=True)
        side = jnp.concatenate([sums[-1][:, 3 * part : 3 * part + SIDE], jnp.zeros((shard, 128 - SIDE), F32)], axis=1)
        lane = lax.broadcasted_iota(jnp.int32, (shard, 128), 1)
        rows[...] = jnp.where(lane == SCALE_COLUMN + 1, total, side).T[:8, :]

    flat = [p for pieces in parts for p in pieces]
    out_shape = (jax.ShapeDtypeStruct((3, shard, width), F32), jax.ShapeDtypeStruct((8, shard), F32))
    return call(kernel, "join_chunks", [VMEM] * (len(flat) + 1), out_shape, [], 1, *flat, weights)


def local(
    inputs,
    doc_ids,
    w_qkv,
    w_out,
    w_up,
    up_bias,
    w_down,
    down_bias,
    attn_gain,
    mlp_gain,
    dim_scale,
    cotangent,
):
    shard, _, width = w_qkv.shape
    size = lax.axis_size("fsdp")
    depth = shard * size
    rows = inputs.shape[0]
    core, tx, rank = lax.axis_index("core"), lax.axis_index("tx"), lax.axis_index("fsdp")
    place = jnp.stack([core, rank]).astype(jnp.int32)

    chunks = 2
    heads = width // HD
    part = width // chunks
    vectors = jnp.concatenate([jnp.stack([attn_gain, mlp_gain, down_bias]), jnp.zeros((5, shard), F32)])
    qkv = HalvesGather(pack_qkv(jnp.transpose(w_qkv, (1, 0, 2)), vectors, chunks))
    rest = Gather(jnp.concatenate([w_out.T, w_up, w_down.T], axis=1).astype(BF16))
    qkv.start(0)

    input_rows = (inputs, swap(inputs, "core", 1))
    cots = (cotangent, swap(cotangent, "core", 1))
    docs = lax.dynamic_slice_in_dim(doc_ids, tx * LEN, LEN, 0)
    doc_col, doc_row = docs[:, None], docs[None, :]
    scale_base = PERDIM_BASE / math.sqrt(HD)
    query_scale = scale_base * jax.nn.softplus(dim_scale)
    colscale = jnp.concatenate([jnp.tile(query_scale, heads // chunks), jnp.ones((2 * part,), F32)])[None]

    bias_far = swap(tie(up_bias, input_rows[1], cots[1]), "tx", 1)
    now = (*qkv.along_z[0], input_rows[1], cots[1], bias_far)
    qkv.middle(0, *now)
    qkv.start(1, *now)
    now = (*qkv.along_xy[0], *qkv.along_z[1])
    qkv.middle(1, *now)
    rest.start(*now)
    now = qkv.along_xy[1]
    qkv.finish(*now)
    own_attns, own_saved, (weight_own, normed_first, gains) = attn_forward(
        place, qkv.own, (tie(inputs, *now), input_rows[1]), colscale, doc_col, doc_row, chunks, depth
    )
    now = (own_saved[3], *rest.along_z, *qkv.last)
    out_columns, mlp_columns = Columns(rest, slice(0, 2 * width)), Columns(rest, slice(2 * width, 3 * width))
    out_columns.middle(*now)
    mlp_columns.middle(*now, *out_columns.ready)
    other_attns, other_saved, (weight_other,) = attn_forward(
        place, qkv.other, (tie(normed_first, *now, *mlp_columns.ready),), colscale, doc_col, doc_row, chunks, depth
    )
    now = (other_saved[3], *out_columns.along_xy)
    out_columns.finish(*now)
    mlp_columns.finish(*now, *mlp_columns.along_xy)
    bias_up = jnp.concatenate([up_bias, bias_far])[None]
    attns = [*own_attns, *other_attns]
    gain_first, gain_second, bias_second = [gains[64 + i : 65 + i] for i in range(3)]
    if size == 8:
        out_columns.other[-1] = (tie(out_columns.other[-1][0], *mlp_columns.along_xy), out_columns.other[-1][1])
    out_t, up = assemble(place, (out_columns,), depth, width)
    sent, kept = out_forward(attns, out_t, inputs)
    sent = tie(sent, *mlp_columns.last)
    resid_first, normed_own = second_norm(kept, swap(sent, "core", 1), gain_second)
    normeds = (normed_own, swap(normed_own, "core", 1))
    (down_t,) = assemble(place, (mlp_columns,), depth, width)
    hidden, grad_pre, upbias_sum, mlp_kept, grad_kept, mlp_sent, grad_sent = mlp(normeds, cots, up, down_t, bias_up)
    grads = (grad_kept, swap(grad_sent, "core", 1))
    mlps = (mlp_kept, swap(mlp_sent, "core", 1))
    updown_own, updown_other = weight_grads(place, [(normeds, grad_pre), (cots, hidden)], "updown_grads")
    updown, both = Reduction(), Reduction()
    now = (updown_own[-1], grads[1], mlps[1])
    updown.send_far([tie(p, *now) for p in updown_other[:2]] + list(updown_other[2:]))
    grad_own, mlpgain_sum, layer_out = resid_grads(
        (tie(grad_kept, *now), grads[1]), mlps, resid_first, cotangent, gain_second, bias_second
    )
    grad_attn = (grad_own, swap(grad_own, "core", 1))
    grad_heads, out_grads = head_grads(place, grad_attn, out_t, attns)
    out = ReductionFirstZ(out_grads)
    out.send_z(grad_heads)
    now = (grad_heads, *updown.sent_far)
    updown.send_xy(updown_own, *now)

    downbias_sum = jnp.sum(cotangent.astype(F32), axis=0)[None]
    own_riders = other_riders = nothing = jnp.zeros((8, depth), F32)
    if size == 8:
        units = jnp.tile(upbias_sum.reshape(2, 2, shard), (1, 1, size))
        own_riders = jnp.concatenate([mlpgain_sum, downbias_sum, units[0], nothing[:4]])
        other_riders = jnp.concatenate([nothing[:2], units[1], nothing[:4]])

    def back(attns, saved, first_col, own, riders, other_sums, *now):
        dout = tie(grad_heads, *now)
        return attn_backward(
            place, attns, saved, dout, normed_first, doc_col, doc_row, query_scale[None], first_col, own, riders, other_sums
        )

    grad_other, sums_other, pieces_other = back(
        other_attns, other_saved, width, False, other_riders, query_scale[None], *now, *updown.ready
    )
    now = (sums_other, updown.from_x, updown.from_y)
    both.send_far([tie(p, *now) for p in pieces_other[:2]] + list(pieces_other[2:]))
    grad_first, sums_first, pieces_first = back(own_attns, own_saved, 0, True, own_riders, sums_other, *now)
    now = (sums_first, *both.sent_far, *out.from_z)
    first, second = both.split(chunks)
    near_far = [pieces_first[c::chunks] for c in range(chunks)]
    relay(updown, first, near_far[0], *now)
    sent, kept = input_grads(
        [[tie(grad_first[0], *first.ready, *updown.ready), grad_first[1]], list(grad_other)],
        [weight_own, weight_other], rows,
    )
    now = (sent, first.from_x, first.from_y, *updown.parts[1:])
    relay(first, second, near_far[1], *now)
    now = (second.from_x, second.from_y, *first.parts[1:])
    second.send_z(*now)
    out.send_y(*now)
    received = swap(tie(sent, *now), "core", 1)

    out.send_x()
    input_grad = first_norm_grads(kept, received, inputs, grad_own, gain_first)
    updown_grad, out_grad = updown.total(), out.total()
    second_parts = (tie(second.parts[0], out.from_x, input_grad), *second.parts[1:])
    qkv_grad, small = join_chunks([first.parts, second_parts], jnp.transpose(w_qkv, (1, 0, 2)))
    summed = small + swap(small, "core", 1)
    summed = summed + swap(summed, "tx", 1)
    if size == 8:
        upbias_grad = small[2:4].reshape(-1)
        downbias_grad, mlpgain_grad, scale_sum = summed[1], summed[0], summed[SCALE_COLUMN, :HD]
    else:
        everything = ("fsdp", "tx", "core")
        upbias_grad = lax.psum(upbias_sum[0, :width] + swap(upbias_sum[0, width:], "tx", 1), "fsdp")
        vectors = lax.psum(jnp.concatenate([downbias_sum, mlpgain_sum]), everything)
        downbias_grad, mlpgain_grad = lax.dynamic_slice_in_dim(vectors, rank * shard, shard, 1)
        scale_sum = lax.psum(sums_other + sums_first, everything)[0]
    return (
        layer_out,
        input_grad,
        jnp.transpose(qkv_grad, (1, 0, 2)),
        out_grad.T,
        updown_grad[:, :width],
        upbias_grad,
        updown_grad[:, width:].T,
        downbias_grad,
        summed[SCALE_COLUMN + 1] / attn_gain.astype(BF16).astype(F32),
        mlpgain_grad,
        scale_base * jax.nn.sigmoid(dim_scale) * scale_sum,
    )


def solution(mesh):
    size, tensor = mesh.shape["fsdp"], mesh.shape["tensor"]
    split = Mesh(mesh.devices.reshape(size, tensor // 2, 2), ("fsdp", "tx", "core"))
    tokens = P(("fsdp", "tx", "core"), None)
    tensor_axes = ("tx", "core")
    in_specs = (
        tokens,
        P("fsdp"),
        P("fsdp", None, tensor_axes),
        P(tensor_axes, "fsdp"),
        P("fsdp", tensor_axes),
        P(tensor_axes),
        P(tensor_axes, "fsdp"),
        P("fsdp"),
        P("fsdp"),
        P("fsdp"),
        P(),
        tokens,
    )
    out_specs = (
        tokens,
        tokens,
        P("fsdp", None, tensor_axes),
        P(tensor_axes, "fsdp"),
        P("fsdp", tensor_axes),
        P(tensor_axes),
        P(tensor_axes, "fsdp"),
        P("fsdp"),
        P("fsdp"),
        P("fsdp"),
        P(),
    )
    return jax.shard_map(local, mesh=split, in_specs=in_specs, out_specs=out_specs, check_vma=False)
```

```python
import math

import jax
import jax.numpy as jnp
from jax import lax
from jax.experimental import pallas as pl
from jax.experimental.pallas import tpu as pltpu
from jax.sharding import Mesh
from jax.sharding import PartitionSpec as P

HD = 80
LEN = 1024
BQ = 256
NORM_EPS = 1e-06
PERDIM_BASE = 1.442695041
NEG_FILL = -1e30
VMEM_BYTES = 16 << 20
BF16 = jnp.bfloat16
F32 = jnp.float32
NT = (((1,), (1,)), ((), ()))
NN = (((1,), (0,)), ((), ()))
TN = (((0,), (0,)), ((), ()))


def dot(a, b, dims=NN):
    return lax.dot_general(a, b, dims, preferred_element_type=F32)


def swap(value, axis, bit):
    size = lax.axis_size(axis)
    return lax.ppermute(value, axis, [(i, i ^ bit) for i in range(size)])


def tie(value, *others):
    return lax.optimization_barrier((value, *others))[0] if others else value


def rms_scale(values):
    return lax.rsqrt(jnp.mean(values * values, axis=-1, keepdims=True) + NORM_EPS)


def along_z(yj, first=0):
    return [((zj,), 2 * zj + yj, first) for zj in range(4)]


class Gather:
    def __init__(self, shard):
        self.whole = lax.axis_size("fsdp") != 8
        self.shard = shard

    def start(self, *after):
        shard = tie(self.shard, *after)
        if self.whole:
            gathered = lax.all_gather(shard, "fsdp", axis=0, tiled=True)
            self.own, self.other = [(gathered, [])], [(swap(gathered, "tx", 1), [])]
            self.along_z = self.along_xy = self.last = self.ready = (gathered,)
            return
        self.along_z = tuple(swap(shard, "fsdp", 2 * j) for j in (1, 2, 3))

    def middle(self, *after):
        if self.whole:
            return
        stacked = jnp.stack((self.shard, tie(self.along_z[0], *after), *self.along_z[1:]))
        self.ready = (stacked,)
        self.along_xy = (swap(stacked, "fsdp", 1), swap(stacked, "tx", 1))
        self.own = [(stacked, along_z(0)), (self.along_xy[0], along_z(1))]

    def finish(self, *after):
        if self.whole:
            return
        half = self.shard.shape[0] // 2
        from_y, from_x = tie(self.along_xy[0], *after), tie(self.along_xy[1], *after)
        self.last = (swap(from_y[:, :half], "tx", 1), swap(from_x[:, half:], "fsdp", 1))
        self.other = [(self.along_xy[1], along_z(0)), (self.last[0], along_z(1)), (self.last[1], along_z(1, half))]


class Columns:
    def __init__(self, gather, columns):
        self.gather, self.columns, self.whole = gather, columns, gather.whole

    def middle(self, *after):
        if self.whole:
            self.along_xy = self.ready = ()
            return
        parts = (self.gather.shard, *(tie(piece, *after) for piece in self.gather.along_z))
        stacked = jnp.stack([p[:, self.columns] for p in parts])
        self.ready = (stacked,)
        self.along_xy = (swap(stacked, "fsdp", 1), swap(stacked, "tx", 1))
        self.own = [(stacked, along_z(0)), (self.along_xy[0], along_z(1))]

    def finish(self, *after):
        if self.whole:
            self.own, self.other = [
                [(tie(side[0][0], *after)[:, self.columns], [])] for side in (self.gather.own, self.gather.other)
            ]
            self.last = ()
            return
        half = self.gather.shard.shape[0] // 2
        from_y, from_x = tie(self.along_xy[0], *after), tie(self.along_xy[1], *after)
        self.last = (swap(from_y[:, :half], "tx", 1), swap(from_x[:, half:], "fsdp", 1))
        self.other = [(self.along_xy[1], along_z(0)), (self.last[0], along_z(1)), (self.last[1], along_z(1, half))]


class HalvesGather:
    def __init__(self, halves):
        self.whole = lax.axis_size("fsdp") != 8
        self.halves = halves
        self.along_z, self.along_xy, self.stacked = [None, None], [None, None], [None, None]

    def start(self, n, *after):
        half = tie(self.halves[n], *after)
        if self.whole:
            self.along_z[n] = (half,)
            return
        self.along_z[n] = tuple(swap(half, "fsdp", 2 * j) for j in (1, 2, 3))

    def middle(self, n, *after):
        if self.whole:
            self.along_xy[n] = self.along_z[n]
            return
        self.stacked[n] = jnp.stack((self.halves[n], tie(self.along_z[n][0], *after), *self.along_z[n][1:]))
        self.along_xy[n] = (swap(self.stacked[n], "fsdp", 1), swap(self.stacked[n], "tx", 1))

    def finish(self, *after):
        if self.whole:
            shard = tie(jnp.concatenate(self.halves), *after)
            gathered = lax.all_gather(shard, "fsdp", axis=0, tiled=True)
            self.own, self.other = [(gathered, [])], [(swap(gathered, "tx", 1), [])]
            self.last = (self.other[0][0],)
            return
        (first_y, first_x), (second_y, second_x) = self.along_xy
        half = self.halves[0].shape[0]
        self.last = (swap(tie(first_y, *after), "tx", 1), swap(tie(second_x, *after), "fsdp", 1))
        self.own = [
            (self.stacked[0], along_z(0)), (first_y, along_z(1)), (self.stacked[1], along_z(0, half)), (second_y, along_z(1, half)),
        ]
        self.other = [
            (first_x, along_z(0)), (self.last[0], along_z(1)), (second_x, along_z(0, half)), (self.last[1], along_z(1, half)),
        ]


class Reduction:
    def __init__(self):
        self.whole = lax.axis_size("fsdp") != 8

    def send_far(self, other):
        self.other = other
        if self.whole:
            self.sent_far = other
            return
        self.sent_far = (swap(other[0], "tx", 1), swap(other[1], "fsdp", 1))

    def split(self, count):
        parts = [Reduction() for _ in range(count)]
        for c, p in enumerate(parts):
            if self.whole:
                p.other = p.sent_far = (self.other[c],)
            else:
                p.sent_far = tuple(r[c] for r in self.sent_far)
                p.other = (None, None, self.other[2 + c])
        return parts

    def send_xy(self, own, *after):
        self.own = own
        if self.whole:
            self.from_x, self.from_y = swap(self.other[0], "tx", 1), own[0]
            self.ready = (own[0],)
            return
        self.ready = add_halves(self.other[2], own[0], self.sent_far, after)
        self.from_x, self.from_y = swap(self.ready[0], "tx", 1), swap(self.ready[1], "fsdp", 1)

    def send_z(self, *after):
        if self.whole:
            total = self.own[0] + tie(self.from_x, *after)
            self.ready = (total,)
            self.parts = (lax.psum_scatter(total, "fsdp", scatter_dimension=0, tiled=True),)
            return
        self.ready = sum_pieces(tie(self.own[1], *after), self.from_x, self.from_y)
        self.parts = (self.ready[0], *(swap(self.ready[j], "fsdp", 2 * j) for j in (1, 2, 3)))

    def total(self):
        return sum(piece.astype(F32) for piece in self.parts)


def relay(done, going, own, *after):
    if done.whole:
        done.send_z(*after)
        going.send_xy(own, *after)
        return
    _, rows, cols = done.own[1].shape

    def kernel(near, from_x, from_y, next_near, far, next_x, next_y, *outs):
        *sums, along_x, along_y = outs
        for j, out in enumerate(sums):
            total = near[j].astype(F32) + from_x[j].astype(F32) + from_y[j].astype(F32)
            out[...] = total.astype(out.dtype)
        half = far.shape[1] // 2
        along_x[:, :half] = next_near[:, :half]
        along_x[:, half:] = (next_near[:, half:].astype(F32) + next_y[...].astype(F32)).astype(BF16)
        along_y[:, :half] = (far[:, :half].astype(F32) + next_x[...].astype(F32)).astype(BF16)
        along_y[:, half:] = far[:, half:]

    out_shape = [jax.ShapeDtypeStruct((rows, cols), BF16 if j else F32) for j in range(4)]
    out_shape += [jax.ShapeDtypeStruct(own[0].shape, BF16)] * 2
    args = (tie(done.own[1], *after), done.from_x, done.from_y, going.other[2], own[0], *going.sent_far)
    outs = call(kernel, "relay", [VMEM] * 7, tuple(out_shape), [], 0.01, *args, near=True)
    going.own, going.ready, done.ready = own, outs[4:], outs[:4]
    done.parts = (outs[0], *(swap(outs[j], "fsdp", 2 * j) for j in (1, 2, 3)))
    going.from_x, going.from_y = swap(outs[4], "tx", 1), swap(outs[5], "fsdp", 1)


class ReductionFirstZ:
    def __init__(self, squares):
        self.whole = lax.axis_size("fsdp") != 8
        self.squares = squares

    def send_z(self, *after):
        if self.whole:
            total = self.squares[0] + swap(tie(self.squares, *after)[1], "tx", 1)
            self.from_z = (lax.psum_scatter(total, "fsdp", scatter_dimension=0, tiled=True),)
            return
        squares = tie(self.squares, *after)
        self.from_z = tuple(swap(squares[j], "fsdp", 2 * j) for j in (1, 2, 3))

    def sum_z(self, *after):
        self.square = (self.squares,)
        if not self.whole:
            self.square = sum_squares(tie(self.squares, *after), self.from_z)

    def send_y(self, *after):
        if self.whole:
            self.from_y = self.from_z[0]
            return
        self.from_y = swap(tie(self.square[1], *after), "fsdp", 1)

    def send_x(self, *after):
        if self.whole:
            self.from_x = self.from_z[0]
            return
        self.pair = add(self.square[0], tie(self.from_y, *after))
        self.from_x = swap(self.pair[1], "tx", 1)

    def total(self):
        if self.whole:
            return self.from_x.astype(F32)
        return self.pair[0].astype(F32) + self.from_x.astype(F32)


def add(a, b):
    return (a.astype(F32) + b.astype(F32)).astype(BF16)


def sum_squares(squares, from_z):
    def kernel(squares, *refs):
        *from_z, near, far = refs
        for n, out in enumerate((near, far)):
            for r in range(2):
                total = squares[0, 2 * n + r].astype(F32)
                for piece in from_z:
                    total = total + piece[2 * n + r].astype(F32)
                out[r] = total.astype(BF16)

    out_shape = (jax.ShapeDtypeStruct((2, *squares.shape[2:]), BF16),) * 2
    return call(kernel, "sum_squares", [VMEM] * 4, out_shape, [], 0.01, squares, *from_z)


def sum_pieces(near, from_x, from_y):
    def kernel(near, from_x, from_y, *outs):
        for j, out in enumerate(outs):
            total = near[j].astype(F32) + from_x[j].astype(F32) + from_y[j].astype(F32)
            out[...] = total.astype(out.dtype)

    _, rows, cols = near.shape
    out_shape = tuple(jax.ShapeDtypeStruct((rows, cols), BF16 if j else F32) for j in range(4))
    return call(kernel, "sum_pieces", [VMEM] * 3, out_shape, [], 0.01, near, from_x, from_y)


def add_halves(near, far, sent_far, after):
    def kernel(near, far, from_x, from_y, along_x, along_y):
        half = near.shape[1] // 2
        along_x[:, :half] = near[:, :half]
        along_x[:, half:] = (near[:, half:].astype(F32) + from_y[...].astype(F32)).astype(BF16)
        along_y[:, :half] = (far[:, :half].astype(F32) + from_x[...].astype(F32)).astype(BF16)
        along_y[:, half:] = far[:, half:]

    out_shape = (jax.ShapeDtypeStruct(near.shape, BF16), jax.ShapeDtypeStruct(far.shape, BF16))
    return call(kernel, "add_halves", [VMEM] * 4, out_shape, [], 0.01, tie(near, *after), far, *sent_far, near=True)


VMEM = pl.BlockSpec(memory_space=pltpu.VMEM)
ANY = pl.BlockSpec(memory_space=pl.ANY)
SMEM = pl.BlockSpec(memory_space=pltpu.SMEM)


def call(kernel, name, in_specs, out_shape, scratch_shapes, micros, *args, near=False, away=(), away_out=()):
    out_specs = jax.tree.map(lambda _: VMEM, out_shape)
    if near:
        spaces = [pltpu.HBM if n in away or s is ANY else pltpu.VMEM for n, s in enumerate(in_specs)]
        args = [
            a if s is SMEM else pltpu.with_memory_space_constraint(a, space)
            for a, s, space in zip(args, in_specs, spaces)
        ]
        out_shape = jax.tree.map(lambda o: pltpu.VMEM(o.shape, o.dtype), out_shape)
        if away_out:
            out_shape = [pltpu.HBM(o.shape, o.dtype) if n in away_out else o for n, o in enumerate(out_shape)]
            out_specs = [ANY if n in away_out else VMEM for n in range(len(out_shape))]
    return pl.pallas_call(
        kernel,
        in_specs=in_specs,
        out_specs=out_specs,
        out_shape=out_shape,
        scratch_shapes=scratch_shapes,
        compiler_params=pltpu.CompilerParams(vmem_limit_bytes=VMEM_BYTES),
        cost_estimate=pl.CostEstimate(flops=int(micros * 1e9), bytes_accessed=1 << 10, transcendentals=0),
        name=name,
    )(*args)


def place_pieces(refs, entries, weight, rank, cols=slice(None), width=None, first_col=0):
    if len(refs) == 1 and not entries[0]:
        weight[:, first_col : first_col + width] = refs[0][:, cols]
        return
    shard = weight.shape[0] // 8
    for ref, places in zip(refs, entries):
        for index, j, first in places:
            piece = ref[(*index, slice(None), cols)]
            start = pl.multiple_of((rank ^ j) * shard + first, 16)
            weight[pl.ds(start, piece.shape[0]), first_col : first_col + width] = piece


def far_shapes(depth, cols, size, own, parts=1):
    if size != 8:
        return (jax.ShapeDtypeStruct((depth, cols // parts), BF16),) * parts
    rows = depth // 8
    near = (jax.ShapeDtypeStruct((4, rows, cols // parts), BF16),) * parts
    if own:
        return (*near, *near)
    lead = (parts,) if parts > 1 else ()
    return (jax.ShapeDtypeStruct((*lead, 4, rows // 2, cols // parts), BF16),) * 2 + near


def put_pieces(refs, block, start, rank, own, part=None):
    if len(refs[0].shape) == 2:
        refs[part or 0][start : start + block.shape[0], :] = block
        return
    near = refs[len(refs) // 2 + (part or 0)] if own else refs[2 + (part or 0)]
    rows = near.shape[1]
    for n in range(block.shape[0] // rows):
        j = (start // rows + n) ^ rank
        yj, zj = j & 1, j >> 1
        piece = block[n * rows : (n + 1) * rows]

        @pl.when(yj == 0)
        def _():
            near[zj] = piece

        @pl.when(yj == 1)
        def _():
            if own:
                refs[part or 0][zj] = piece
            elif part is None:
                refs[0][zj] = piece[: rows // 2]
                refs[1][zj] = piece[rows // 2 :]
            else:
                refs[0][part, zj] = piece[: rows // 2]
                refs[1][part, zj] = piece[rows // 2 :]


def assemble(place, gathers, depth, width):
    lists = [pieces for g in gathers for pieces in (g.own, g.other)]
    entries = [[p[1] for p in pieces] for pieces in lists]
    arrays = [p[0] for pieces in lists for p in pieces]
    counts = [pieces[0][0].shape[-1] for pieces in lists[::2]]
    parts = sum(counts) // width

    def kernel(place, *refs):
        pieces, outs = refs[: len(arrays)], refs[len(arrays) :]
        at, first = 0, 0
        for n, places in enumerate(entries):
            refs_n = pieces[at : at + len(places)]
            at += len(places)
            for i in range(counts[n // 2] // width):
                cols = slice(i * width, (i + 1) * width)
                place_pieces(refs_n, places, outs[first + i], place[1], cols, width, n % 2 * width)
            if n % 2:
                first += counts[n // 2] // width

    out_shape = tuple(jax.ShapeDtypeStruct((depth, 2 * width), BF16) for _ in range(parts))
    return call(kernel, "assemble", [SMEM] + [VMEM] * len(arrays), out_shape, [], 3, place, *arrays, near=True)


def pack_qkv(weights, vectors, chunks):
    _, shard, width = weights.shape
    part = width // chunks
    first = shard // 2
    cols = -(-(3 * width + 8) // 128) * 128

    def kernel(weights, vectors, *outs):
        blocks = [weights[i, :, c * part : (c + 1) * part] for c in range(chunks) for i in range(3)]
        blocks += [vectors[...].T, jnp.zeros((shard, cols - 3 * width - 8), F32)]
        packed = jnp.concatenate(blocks, axis=1).astype(BF16)
        outs[0][...] = packed[:first]
        outs[1][...] = packed[first:]

    out_shape = (jax.ShapeDtypeStruct((first, cols), BF16), jax.ShapeDtypeStruct((shard - first, cols), BF16))
    return call(kernel, "pack_qkv", [VMEM] * 2, out_shape, [], 1, weights, vectors)


BIAS_ROWS = sum((i + 1) * BQ for i in range(LEN // BQ))


def bias_rows(i):
    start = i * (i + 1) // 2 * BQ
    return slice(start, start + (i + 1) * BQ)


def mask_bias(doc_col, doc_row, bias):
    for i in range(LEN // BQ):
        lo, hi = i * BQ, (i + 1) * BQ
        same = doc_col[:hi, :] == doc_row[:, lo:hi]
        keys = lax.broadcasted_iota(jnp.int32, (hi, BQ), 0)
        queries = lax.broadcasted_iota(jnp.int32, (hi, BQ), 1) + lo
        bias[bias_rows(i), :] = jnp.where(same & (keys <= queries), 0.0, NEG_FILL)


def outer_rows(lo, rows, core):
    half = LEN // 2
    return pl.ds(pl.multiple_of(((lo // half) ^ core) * half + lo % half, rows), rows)


def head_rows(ref, block, columns, rows):
    for h in range(ref.shape[0]):
        ref[h, rows, :] = block[:, columns[h] : columns[h] + HD].astype(ref.dtype)


def join_heads(ref, heads):
    return jnp.concatenate([ref[h] for h in heads], axis=1)


def attn_forward(place, pieces, rows_in, scale, doc_col, doc_row, chunks, depth):
    arrays, places = [p[0] for p in pieces], [p[1] for p in pieces]
    cols = arrays[0].shape[-1]
    fresh = len(rows_in) == 2
    part = scale.shape[1] // 3
    per_chunk = part // HD
    heads = per_chunk * chunks
    starts = [[c * 3 * part + n * part + h * HD for c in range(chunks) for h in range(per_chunk)] for n in range(3)]

    def kernel(place, *refs):
        pieces, refs = refs[: len(arrays)], refs[len(arrays) :]
        sources, (scale, doc_col, doc_row) = refs[: len(rows_in)], refs[len(rows_in) : len(rows_in) + 3]
        outs = refs[len(rows_in) + 3 :]
        attns, (*away, lse) = outs[:chunks], outs[chunks : chunks + 5]
        if fresh:
            x, gains, *outs = outs[chunks + 5 :]
        else:
            x, outs = sources[0], outs[chunks + 5 :]
        bias, out_heads, query, key, value, weight, sems = outs
        copies = [
            pltpu.make_async_copy(source, target, sems.at[n])
            for n, (source, target) in enumerate(zip((query, key, value, weight), away))
        ]
        core, rank = place[0], place[1]
        half = LEN // 2
        place_pieces(pieces, places, weight, rank, slice(None), cols)
        mask_bias(doc_col, doc_row, bias)
        if fresh:
            gains[...] = weight[:, cols - 128 :].astype(F32).T
            gain = gains[64:65, :]
            for n, source in enumerate(sources):

                def norm(i, _, source=source, n=n):
                    block = pl.ds(pl.multiple_of(i * 128, 128), 128)
                    values = source[block, :].astype(F32)
                    target = pl.ds(pl.multiple_of(i * 128 + n * half, 128), 128)
                    x[target, :] = (values * rms_scale(values) * gain).astype(BF16)
                    return 0

                lax.fori_loop(0, half // 128, norm, 0)

        def project(i, _):
            lo = i * BQ
            block = dot(x[outer_rows(lo, BQ, core), :], weight[...])
            rows = pl.ds(pl.multiple_of(lo, BQ), BQ)
            scaled = jnp.concatenate(
                [block[:, c * 3 * part : c * 3 * part + part] * scale[:, :part] for c in range(chunks)], axis=1
            )
            head_rows(query, scaled, [h * HD for h in range(heads)], rows)
            head_rows(key, block, starts[1], rows)
            head_rows(value, block, starts[2], rows)
            return 0

        lax.fori_loop(0, LEN // BQ, project, 0)
        for copy in copies:
            copy.start()

        def attend(h, _):
            keys = key[h]
            value_t = value[h].T
            blocks = []
            for i in range(LEN // BQ):
                lo, hi = i * BQ, (i + 1) * BQ
                scores = dot(keys[:hi], query[h, lo:hi, :], NT) + bias[bias_rows(i), :]
                top = jnp.max(scores, axis=0, keepdims=True)
                probs = jnp.exp(scores - top)
                total = jnp.sum(probs, axis=0, keepdims=True)
                blocks.append(dot(value_t[:, :hi], probs.astype(BF16)) / total)
                lse[h, :, lo:hi] = top + jnp.log(total)
            out_heads[h] = jnp.concatenate(blocks, axis=1).T.astype(BF16)
            return 0

        def attend_two(n, _):
            attend(2 * n, 0)
            return attend(2 * n + 1, 0)

        lax.fori_loop(0, heads // 2, attend_two, 0)
        for c in range(chunks):
            joined = join_heads(out_heads, range(c * per_chunk, (c + 1) * per_chunk))
            for a in range(2):
                attns[c][outer_rows(a * half, half, core), :] = joined[a * half : (a + 1) * half]
        for copy in copies:
            copy.wait()

    per_head = jax.ShapeDtypeStruct((heads, LEN, HD), BF16)
    out_shape = (
        *(jax.ShapeDtypeStruct((LEN, part), BF16),) * chunks,
        per_head,
        per_head,
        per_head,
        jax.ShapeDtypeStruct((depth, cols), BF16),
        jax.ShapeDtypeStruct((heads, 1, LEN), F32),
    )
    scratch = [pltpu.VMEM((BIAS_ROWS, BQ), F32)] + [pltpu.VMEM((heads, LEN, HD), BF16)] * 4
    scratch += [pltpu.VMEM((depth, cols), BF16), pltpu.SemaphoreType.DMA((4,))]
    if fresh:
        out_shape += (jax.ShapeDtypeStruct((LEN, depth), BF16), jax.ShapeDtypeStruct((128, depth), F32))
    specs = [SMEM] + [VMEM] * (len(arrays) + len(rows_in) + 3)
    args = (place, *arrays, *rows_in, scale, doc_col, doc_row)
    outs = call(
        kernel, "attn_forward", specs, out_shape, scratch, 8, *args, near=True, away_out=range(chunks, chunks + 4)
    )
    saved = (*outs[chunks : chunks + 3], outs[chunks + 4])
    return outs[:chunks], saved, (outs[chunks + 3], *outs[chunks + 5 :])


SIDE = 32
SCALE_COLUMN = 4


def attn_backward(place, attns, saved, dout, x, doc_col, doc_row, scale, first, own, riders, other_sums):
    part = attns[0].shape[1]
    per_chunk = part // HD
    count = len(attns)
    heads = per_chunk * count
    depth = x.shape[1]
    size = lax.axis_size("fsdp")
    pieces_shape = far_shapes(depth, (3 * part + SIDE) * count, size, own, count)

    def kernel(place, *refs):
        attns, refs = refs[:count], refs[count:]
        *saved, lse, dout, x, doc_col, doc_row, scale, other_sums = refs[:10]
        riders, refs = refs[10 : 10 + len(riders_in)], refs[10 + len(riders_in) :]
        grads_out, sums_out, refs = refs[:count], refs[count], refs[count + 1 :]
        pieces, refs = refs[:-10], refs[-10:]
        dkey, dvalue, bias, douts, deltas, grads, query, key, value, sems = refs
        copies = [
            pltpu.make_async_copy(source, target, sems.at[n])
            for n, (source, target) in enumerate(zip(saved, (query, key, value)))
        ]
        for copy in copies:
            copy.start()
        core, rank = place[0], place[1]
        half = LEN // 2
        lanes = lax.broadcasted_iota(jnp.int32, (8, part), 1) // HD
        selector = jnp.where(lanes == lax.broadcasted_iota(jnp.int32, (8, part), 0), 1.0, 0.0)
        mask_bias(doc_col, doc_row, bias)
        for c in range(count):
            for i in range(LEN // BQ):
                lo, hi = i * BQ, (i + 1) * BQ
                rows = outer_rows(lo, BQ, core)
                dout_block = dout[rows, first + c * part : first + (c + 1) * part]
                products = attns[c][rows, :].astype(F32) * dout_block.astype(F32)
                delta = lax.dot_general(
                    selector, products, NT, precision=lax.Precision.HIGHEST, preferred_element_type=F32
                )
                for h in range(per_chunk):
                    deltas[c * per_chunk + h, :, lo:hi] = delta[h : h + 1, :]
                    douts[c * per_chunk + h, lo:hi, :] = dout_block[:, h * HD : (h + 1) * HD]

        for copy in copies:
            copy.wait()

        def attend(h, sums):
            keys = key[h]
            key_t = keys.T
            dquery_parts = []
            for i in range(LEN // BQ):
                lo, hi = i * BQ, (i + 1) * BQ
                queries = query[h, lo:hi, :]
                dout_head = douts[h, lo:hi, :]
                scores = dot(keys[:hi], queries, NT) + bias[bias_rows(i), :]
                probs = jnp.exp(scores - lse[h, :, lo:hi])
                dprobs = dot(value[h, :hi, :], dout_head, NT)
                dscores = (probs * (dprobs - deltas[h, :, lo:hi])).astype(BF16)
                dv = dot(probs.astype(BF16), dout_head)
                dk = dot(dscores, queries)
                dquery_parts.append(dot(key_t[:, :hi], dscores))
                if i:
                    dkey[:lo] += dk[:lo]
                    dvalue[:lo] += dv[:lo]
                dkey[lo:hi] = dk[lo:]
                dvalue[lo:hi] = dv[lo:]
            dquery = jnp.concatenate(dquery_parts, axis=1).T
            grads[0, h] = (dquery * scale[...]).astype(BF16)
            grads[1, h] = dkey[...].astype(BF16)
            grads[2, h] = dvalue[...].astype(BF16)
            return sums + jnp.sum(dquery * query[h].astype(F32), axis=0, keepdims=True)

        def attend_two(n, sums):
            return attend(2 * n + 1, attend(2 * n, sums))

        sums = lax.fori_loop(0, heads // 2, attend_two, jnp.zeros((1, HD), F32))
        sums = sums / scale[...]
        sums_out[...] = sums
        side = [jnp.zeros((depth, SIDE), BF16)] * count
        if size == 8:
            units = riders[0][:, 0 if own else units_width : units_width if own else 2 * units_width]
            units = [units[:, n * (depth // size) : (n + 1) * (depth // size)] for n in range(2)]
            nothing = jnp.zeros((1, depth), F32)
            rows = [r[...] for r in riders[1:]] if own else [nothing] * 2
            rows += [jnp.concatenate([u] * size, axis=1) for u in units] + [nothing] * 4
            columns = jnp.concatenate(rows).T
            if own:
                scales = jnp.broadcast_to(sums + other_sums[...], (128, HD)).T[:, :8]
                block = jnp.concatenate([scales, jnp.zeros((depth // size - HD, 8), F32)])
                column = lax.broadcasted_iota(jnp.int32, (depth, 8), 1) == SCALE_COLUMN
                columns = jnp.where(column, jnp.concatenate([block] * size), columns)
            side[-1] = jnp.concatenate([columns, jnp.zeros((depth, SIDE - 8), F32)], axis=1).astype(BF16)
        for c in range(count):
            mine = range(c * per_chunk, (c + 1) * per_chunk)
            joined = jnp.concatenate([grads[n, h] for n in range(3) for h in mine], axis=1)
            for a in range(2):
                grads_out[c][outer_rows(a * half, half, core), :] = joined[a * half : (a + 1) * half]
            for g in range(2):
                start = g * depth // 2
                block = dot(x[:, start : start + depth // 2], grads_out[c][...], TN).astype(BF16)
                block = jnp.concatenate([block, side[c][start : start + depth // 2]], axis=1)
                put_pieces(pieces, block, start, rank, own, c if count > 1 else None)

    out_shape = (
        *(jax.ShapeDtypeStruct((LEN, 3 * part), BF16),) * count,
        jax.ShapeDtypeStruct((1, HD), F32),
        *pieces_shape,
    )
    scratch = [
        pltpu.VMEM((LEN, HD), F32),
        pltpu.VMEM((LEN, HD), F32),
        pltpu.VMEM((BIAS_ROWS, BQ), F32),
        pltpu.VMEM((heads, LEN, HD), BF16),
        pltpu.VMEM((heads, 1, LEN), F32),
        pltpu.VMEM((3, heads, LEN, HD), BF16),
        *(pltpu.VMEM((heads, LEN, HD), BF16),) * 3,
        pltpu.SemaphoreType.DMA((3,)),
    ]
    riders_in = riders
    units_width = riders[0].shape[1] // 2
    args = (place, *attns, *saved, dout, x, doc_col, doc_row, scale, other_sums, *riders)
    specs = [SMEM] + [VMEM] * count + [ANY] * 3 + [VMEM] * (len(args) - 4 - count)
    outs = call(kernel, "attn_backward", specs, out_shape, scratch, 10, *args, near=True)
    return outs[:count], outs[count], outs[count + 1 :]


def put_both(outs, block, start, rank, size):
    width = block.shape[1] // 2
    count = len(outs) // 2 if size != 8 else 2
    put_pieces(outs[:count], block[:, :width], start, rank, True)
    put_pieces(outs[count:], block[:, width:], start, rank, False)


def weight_grads(place, pairs, name):
    rows, depth = pairs[0][0][0].shape
    width = pairs[0][1].shape[1] // 2
    size = lax.axis_size("fsdp")
    shapes = [far_shapes(depth, width * len(pairs), size, own) for own in (True, False)]

    def kernel(place, *refs):
        ins, outs = refs[: 3 * len(pairs)], refs[3 * len(pairs) :]
        for g in range(2):
            cols = slice(g * depth // 2, (g + 1) * depth // 2)
            blocks = []
            for n in range(len(pairs)):
                near, far, right = ins[3 * n : 3 * n + 3]
                block = dot(near[:, cols], right[:rows, :], TN) + dot(far[:, cols], right[rows:, :], TN)
                blocks.append(block.astype(BF16))
            joined = [b[:, r * width : (r + 1) * width] for r in range(2) for b in blocks]
            put_both(outs, jnp.concatenate(joined, axis=1), g * depth // 2, place[1], size)

    args = [a for halves, right in pairs for a in (*halves, right)]
    outs = call(
        kernel, name, [SMEM] + [VMEM] * len(args), (*shapes[0], *shapes[1]), [], 4 * len(pairs), place, *args, near=True
    )
    return outs[: len(shapes[0])], outs[len(shapes[0]) :]


def out_forward(attns, out_t, inputs):
    rows, depth = inputs.shape

    def kernel(*refs):
        attns, (out_t, inputs, sent, kept) = refs[:-4], refs[-4:]
        heads = jnp.concatenate([a[...] for a in attns], axis=1)
        for i in range(rows // BQ):
            lo, hi = i * BQ, (i + 1) * BQ
            sent[lo:hi, :] = dot(heads[rows + lo : rows + hi], out_t[...], NT).astype(BF16)
            kept[lo:hi, :] = inputs[lo:hi, :].astype(F32) + dot(heads[lo:hi], out_t[...], NT)

    out_shape = (jax.ShapeDtypeStruct((rows, depth), BF16), jax.ShapeDtypeStruct((rows, depth), F32))
    return call(kernel, "out_forward", [VMEM] * (len(attns) + 2), out_shape, [], 3, *attns, out_t, inputs, near=True)


def second_norm(kept, received, gain):
    def kernel(kept, received, gain, resid_out, normed_out):
        resid = kept[...] + received[...].astype(F32)
        resid_out[...] = resid
        normed_out[...] = (resid * rms_scale(resid) * gain[...]).astype(BF16)

    out_shape = (jax.ShapeDtypeStruct(kept.shape, F32), jax.ShapeDtypeStruct(kept.shape, BF16))
    return call(kernel, "second_norm", [VMEM] * 3, out_shape, [], 1, kept, received, gain, near=True)


def mlp(normed, cot, up, down_t, bias_up):
    rows, depth = normed[0].shape
    units = up.shape[1]

    def kernel(n_near, n_far, c_near, c_far, up, down_t, bias, hidden, grad_pre, bias_sum, *outs):
        sums = jnp.zeros((1, units), F32)
        for side, (n, c) in enumerate(((n_near, c_near), (n_far, c_far))):
            out_mlp, out_grad = outs[2 * side : 2 * side + 2]

            def step(i, sums, n=n, c=c, side=side, out_mlp=out_mlp, out_grad=out_grad):
                block = pl.ds(pl.multiple_of(i * BQ, BQ), BQ)
                target = pl.ds(pl.multiple_of(i * BQ + side * rows, BQ), BQ)
                pre = dot(n[block, :], up[...]) + bias[...]
                sig = 1.0 / (1.0 + jnp.exp(-pre))
                units_low = (pre * sig).astype(BF16)
                grad = dot(c[block, :], down_t[...])
                grad_low = (grad * (sig + pre * sig * (1.0 - sig))).astype(BF16)
                hidden[target, :] = units_low
                grad_pre[target, :] = grad_low
                out_mlp[block, :] = dot(units_low, down_t[...], NT).astype(BF16)
                out_grad[block, :] = dot(grad_low, up[...], NT).astype(BF16)
                return sums + jnp.sum(grad_low.astype(F32), axis=0, keepdims=True)

            sums = lax.fori_loop(0, rows // BQ, step, sums)
        bias_sum[...] = sums

    low = jax.ShapeDtypeStruct((rows, depth), BF16)
    out_shape = (
        jax.ShapeDtypeStruct((2 * rows, units), BF16),
        jax.ShapeDtypeStruct((2 * rows, units), BF16),
        jax.ShapeDtypeStruct((1, units), F32),
        low,
        low,
        low,
        low,
    )
    return call(kernel, "mlp", [VMEM] * 7, out_shape, [], 10, *normed, *cot, up, down_t, bias_up, near=True)


def resid_grads(grads, mlps, resid, cot, gain, bias):
    def kernel(grad_near, grad_far, mlp_near, mlp_far, resid, cot, gain, bias, low_out, sum_out, layer):
        for i in range(resid.shape[0] // BQ):
            block = slice(i * BQ, (i + 1) * BQ)
            held = resid[block, :]
            grad = grad_near[block, :].astype(F32) + grad_far[block, :].astype(F32)
            recip = rms_scale(held)
            unit = held * recip
            part = jnp.sum(grad * unit, axis=0, keepdims=True)
            sum_out[...] = part if i == 0 else sum_out[...] + part
            scaled = grad * gain[...]
            mean = jnp.mean(scaled * unit, axis=-1, keepdims=True)
            total = cot[block, :].astype(F32) + recip * (scaled - unit * mean)
            low_out[block, :] = total.astype(BF16)
            mlp = mlp_near[block, :].astype(F32) + mlp_far[block, :].astype(F32)
            layer[block, :] = (held + mlp + bias[...]).astype(BF16)

    out_shape = (
        jax.ShapeDtypeStruct(resid.shape, BF16),
        jax.ShapeDtypeStruct((1, resid.shape[1]), F32),
        jax.ShapeDtypeStruct(resid.shape, BF16),
    )
    return call(kernel, "resid_grads", [VMEM] * 8, out_shape, [], 2, *grads, *mlps, resid, cot, gain, bias, near=True)


def head_grads(place, grads, out_t, attns):
    rows, depth = grads[0].shape
    width = out_t.shape[1] // 2
    size = lax.axis_size("fsdp")
    shard = depth // size

    def kernel(place, near, far, out_t, *refs):
        attns, (heads_out, squares) = refs[:-2], refs[-2:]
        for i in range(2 * rows // BQ):
            source = near if i < rows // BQ else far
            block = slice(i * BQ % rows, i * BQ % rows + BQ)
            heads_out[i * BQ : (i + 1) * BQ, :] = dot(source[block, :], out_t[...]).astype(BF16)
        heads = jnp.concatenate([a[...] for a in attns], axis=1)
        for g in range(2):
            start = g * depth // 2
            cols = slice(start, start + depth // 2)
            block = (dot(near[:, cols], heads[:rows], TN) + dot(far[:, cols], heads[rows:], TN)).astype(BF16)
            for r in range(2):
                side = block[:, r * width : (r + 1) * width]
                if size != 8:
                    squares[r, start : start + depth // 2, :] = side
                    continue
                for n in range(side.shape[0] // shard):
                    j = (start // shard + n) ^ place[1]
                    squares[j >> 1, 2 * (j & 1) + r] = side[n * shard : (n + 1) * shard]

    squares_shape = (4, 4, shard, width) if size == 8 else (2, depth, width)
    out_shape = (jax.ShapeDtypeStruct((2 * rows, 2 * width), BF16), jax.ShapeDtypeStruct(squares_shape, BF16))
    args = (place, *grads, out_t, *attns)
    specs = [SMEM] + [VMEM] * (len(args) - 1)
    return call(kernel, "head_grads", specs, out_shape, [], 6, *args, near=True, away=range(3, len(args)))


def input_grads(grads, weights, rows):
    depth = weights[0].shape[0]
    counts = [len(g) for g in grads]

    def kernel(*refs):
        ins, weights, (sent, kept) = refs[: sum(counts)], refs[sum(counts) : -2], refs[-2:]
        for side, out in enumerate((kept, sent)):

            def step(i, _, side=side, out=out):
                total, at = None, 0
                block = pl.ds(pl.multiple_of(i * BQ + side * rows, BQ), BQ)
                for count, weight in zip(counts, weights):
                    left = jnp.concatenate([g[block, :] for g in ins[at : at + count]], axis=1)
                    at += count
                    partial = dot(left, weight[:, : left.shape[1]], NT)
                    total = partial if total is None else total + partial
                out[pl.ds(pl.multiple_of(i * BQ, BQ), BQ), :] = total.astype(BF16)
                return 0

            lax.fori_loop(0, rows // BQ, step, 0)

    out_shape = (jax.ShapeDtypeStruct((rows, depth), BF16),) * 2
    flat = [g for pair in grads for g in pair]
    return call(
        kernel, "input_grads", [VMEM] * (len(flat) + len(weights)), out_shape, [], 10, *flat, *weights, near=True
    )


def first_norm_grads(kept, received, inputs, resid_grad, gain):
    def kernel(kept, received, inputs, resid_grad, gain, grad_out):
        for i in range(inputs.shape[0] // BQ):
            block = slice(i * BQ, (i + 1) * BQ)
            values = inputs[block, :].astype(F32)
            recip = rms_scale(values)
            unit = values * recip
            scaled = (kept[block, :].astype(F32) + received[block, :].astype(F32)) * gain[...]
            mean = jnp.mean(scaled * unit, axis=-1, keepdims=True)
            grad_out[block, :] = (resid_grad[block, :].astype(F32) + recip * (scaled - unit * mean)).astype(BF16)

    out_shape = jax.ShapeDtypeStruct(inputs.shape, BF16)
    args = (kept, received, inputs, resid_grad, gain)
    return call(kernel, "first_norm_grads", [VMEM] * 5, out_shape, [], 0.01, *args)


def join_chunks(parts, weights, factors):
    counts = [len(p) for p in parts]
    _, shard, width = weights.shape
    part = width // len(parts)

    def kernel(*refs):
        *refs, weights, factors, out, rows = refs
        at = 0
        sums = []
        for count in counts:
            sums.append(sum(ref[...].astype(F32) for ref in refs[at : at + count]))
            at += count
        total = jnp.zeros((shard, 1), F32)
        for i in range(3):
            joined = jnp.concatenate([s[:, i * part : (i + 1) * part] for s in sums], axis=1)
            out[i] = joined
            total = total + jnp.sum(joined * weights[i].astype(BF16).astype(F32), axis=1, keepdims=True)
        side = jnp.concatenate([sums[-1][:, 3 * part : 3 * part + SIDE], jnp.zeros((shard, 128 - SIDE), F32)], axis=1)
        lane = lax.broadcasted_iota(jnp.int32, (shard, 128), 1)
        rows[...] = jnp.where(lane == SCALE_COLUMN + 1, total, side).T[:8, :] * factors[...]

    flat = [p for pieces in parts for p in pieces]
    out_shape = (jax.ShapeDtypeStruct((3, shard, width), F32), jax.ShapeDtypeStruct((8, shard), F32))
    return call(kernel, "join_chunks", [VMEM] * (len(flat) + 2), out_shape, [], 1, *flat, weights, factors)


def local(
    inputs,
    doc_ids,
    w_qkv,
    w_out,
    w_up,
    up_bias,
    w_down,
    down_bias,
    attn_gain,
    mlp_gain,
    dim_scale,
    cotangent,
):
    shard, _, width = w_qkv.shape
    size = lax.axis_size("fsdp")
    depth = shard * size
    rows = inputs.shape[0]
    core, tx, rank = lax.axis_index("core"), lax.axis_index("tx"), lax.axis_index("fsdp")
    place = jnp.stack([core, rank]).astype(jnp.int32)

    chunks = 2
    heads = width // HD
    part = width // chunks
    vectors = jnp.concatenate([jnp.stack([attn_gain, mlp_gain, down_bias]), jnp.zeros((5, shard), F32)])
    qkv = HalvesGather(pack_qkv(jnp.transpose(w_qkv, (1, 0, 2)), vectors, chunks))
    rest = Gather(jnp.concatenate([w_out.T, w_up, w_down.T], axis=1).astype(BF16))
    qkv.start(0)

    input_rows = (inputs, swap(inputs, "core", 1))
    cots = (cotangent, swap(cotangent, "core", 1))
    docs = lax.dynamic_slice_in_dim(doc_ids, tx * LEN, LEN, 0)
    doc_col, doc_row = docs[:, None], docs[None, :]
    scale_base = PERDIM_BASE / math.sqrt(HD)
    query_scale = scale_base * jax.nn.softplus(dim_scale)
    colscale = jnp.concatenate([jnp.tile(query_scale, heads // chunks), jnp.ones((2 * part,), F32)])[None]

    scale_factor = scale_base * jax.nn.sigmoid(dim_scale)
    factors = jnp.ones((8, shard), F32).at[SCALE_COLUMN + 1].set(1.0 / attn_gain.astype(BF16).astype(F32))
    if size == 8:
        factors = factors.at[SCALE_COLUMN, :HD].set(scale_factor)
    downbias_sum = jnp.sum(cotangent.astype(F32), axis=0)[None]

    bias_far = swap(tie(up_bias, input_rows[1], cots[1]), "tx", 1)
    now = (*qkv.along_z[0], input_rows[1], cots[1], bias_far)
    qkv.middle(0, *now)
    qkv.start(1, *now)
    now = (*qkv.along_xy[0], *qkv.along_z[1])
    qkv.middle(1, *now)
    rest.start(*now)
    now = qkv.along_xy[1]
    qkv.finish(*now)
    own_attns, own_saved, (weight_own, normed_first, gains) = attn_forward(
        place, qkv.own, (tie(inputs, *now), input_rows[1]), colscale, doc_col, doc_row, chunks, depth
    )
    now = (own_saved[3], *rest.along_z, *qkv.last)
    out_columns, mlp_columns = Columns(rest, slice(0, 2 * width)), Columns(rest, slice(2 * width, 3 * width))
    out_columns.middle(*now)
    mlp_columns.middle(*now, *out_columns.ready)
    other_attns, other_saved, (weight_other,) = attn_forward(
        place, qkv.other, (tie(normed_first, *now, *mlp_columns.ready, downbias_sum, factors),), colscale, doc_col, doc_row, chunks, depth
    )
    now = (other_saved[3], *out_columns.along_xy)
    out_columns.finish(*now)
    mlp_columns.finish(*now, *mlp_columns.along_xy)
    bias_up = jnp.concatenate([up_bias, bias_far])[None]
    attns = [*own_attns, *other_attns]
    gain_first, gain_second, bias_second = [gains[64 + i : 65 + i] for i in range(3)]
    if size == 8:
        out_columns.other[-1] = (tie(out_columns.other[-1][0], *mlp_columns.along_xy), out_columns.other[-1][1])
    out_t, up = assemble(place, (out_columns,), depth, width)
    sent, kept = out_forward(attns, out_t, inputs)
    sent = tie(sent, *mlp_columns.last)
    resid_first, normed_own = second_norm(kept, swap(sent, "core", 1), gain_second)
    normeds = (normed_own, swap(normed_own, "core", 1))
    (down_t,) = assemble(place, (mlp_columns,), depth, width)
    hidden, grad_pre, upbias_sum, mlp_kept, grad_kept, mlp_sent, grad_sent = mlp(normeds, cots, up, down_t, bias_up)
    grads = (grad_kept, swap(grad_sent, "core", 1))
    mlps = (mlp_kept, swap(mlp_sent, "core", 1))
    updown_own, updown_other = weight_grads(place, [(normeds, grad_pre), (cots, hidden)], "updown_grads")
    updown, both = Reduction(), Reduction()
    now = (updown_own[-1], grads[1], mlps[1])
    updown.send_far([tie(p, *now) for p in updown_other[:2]] + list(updown_other[2:]))
    grad_own, mlpgain_sum, layer_out = resid_grads(
        (tie(grad_kept, *now), grads[1]), mlps, resid_first, cotangent, gain_second, bias_second
    )
    grad_attn = (grad_own, swap(grad_own, "core", 1))
    grad_heads, out_grads = head_grads(place, grad_attn, out_t, attns)
    out = ReductionFirstZ(out_grads)
    out.send_z(grad_heads)
    now = (grad_heads, *updown.sent_far)
    updown.send_xy(updown_own, *now)

    def back(attns, saved, first_col, own, riders, other_sums, *now):
        dout = tie(grad_heads, *now)
        return attn_backward(
            place, attns, saved, dout, normed_first, doc_col, doc_row, query_scale[None], first_col, own, riders, other_sums
        )

    grad_other, sums_other, pieces_other = back(
        other_attns, other_saved, width, False, (upbias_sum,), query_scale[None], *now, *updown.ready
    )
    now = (sums_other, updown.from_x, updown.from_y)
    both.send_far([tie(p, *now) for p in pieces_other[:2]] + list(pieces_other[2:]))
    grad_first, sums_first, pieces_first = back(
        own_attns, own_saved, 0, True, (upbias_sum, mlpgain_sum, downbias_sum), sums_other, *now
    )
    now = (sums_first, *both.sent_far, *out.from_z)
    first, second = both.split(chunks)
    near_far = [pieces_first[c::chunks] for c in range(chunks)]
    out.sum_z(*now)
    relay(updown, first, near_far[0], *now)
    sent, kept = input_grads(
        [[tie(grad_first[0], *first.ready, *updown.ready, *out.square), grad_first[1]], list(grad_other)],
        [weight_own, weight_other], rows,
    )
    now = (sent, first.from_x, first.from_y, *updown.parts[1:])
    relay(first, second, near_far[1], *now)
    now = (second.from_x, second.from_y, *first.parts[1:], *updown.parts[1:])
    second.send_z(*now)
    out.send_y(*now, *second.ready)
    received = swap(tie(sent, *now, *second.ready), "core", 1)
    out.send_x()
    input_grad = first_norm_grads(kept, received, inputs, grad_own, gain_first)
    updown_grad, out_grad = updown.total(), out.total()
    second_parts = (tie(second.parts[0], out.from_x, input_grad), *second.parts[1:])
    qkv_grad, small = join_chunks([first.parts, second_parts], jnp.transpose(w_qkv, (1, 0, 2)), factors)
    tensor = ("tx", "core")
    others = [lax.ppermute(small, tensor, [(i, i ^ bit) for i in range(4)]) for bit in (1, 2, 3)]
    summed = small + others[0] + others[1] + others[2]
    if size == 8:
        upbias_grad = small[2:4].reshape(-1)
        downbias_grad, mlpgain_grad, scale_sum = summed[1], summed[0], summed[SCALE_COLUMN, :HD]
    else:
        everything = ("fsdp", "tx", "core")
        upbias_grad = lax.psum(upbias_sum[0, :width] + swap(upbias_sum[0, width:], "tx", 1), "fsdp")
        vectors = lax.psum(jnp.concatenate([downbias_sum, mlpgain_sum]), everything)
        downbias_grad, mlpgain_grad = lax.dynamic_slice_in_dim(vectors, rank * shard, shard, 1)
        scale_sum = scale_factor * lax.psum(sums_other + sums_first, everything)[0]
    return (
        layer_out,
        input_grad,
        jnp.transpose(qkv_grad, (1, 0, 2)),
        out_grad.T,
        updown_grad[:, :width],
        upbias_grad,
        updown_grad[:, width:].T,
        downbias_grad,
        summed[SCALE_COLUMN + 1],
        mlpgain_grad,
        scale_sum,
    )


def solution(mesh):
    size, tensor = mesh.shape["fsdp"], mesh.shape["tensor"]
    split = Mesh(mesh.devices.reshape(size, tensor // 2, 2), ("fsdp", "tx", "core"))
    tokens = P(("fsdp", "tx", "core"), None)
    tensor_axes = ("tx", "core")
    in_specs = (
        tokens,
        P("fsdp"),
        P("fsdp", None, tensor_axes),
        P(tensor_axes, "fsdp"),
        P("fsdp", tensor_axes),
        P(tensor_axes),
        P(tensor_axes, "fsdp"),
        P("fsdp"),
        P("fsdp"),
        P("fsdp"),
        P(),
        tokens,
    )
    out_specs = (
        tokens,
        tokens,
        P("fsdp", None, tensor_axes),
        P(tensor_axes, "fsdp"),
        P("fsdp", tensor_axes),
        P(tensor_axes),
        P(tensor_axes, "fsdp"),
        P("fsdp"),
        P("fsdp"),
        P("fsdp"),
        P(),
    )
    return jax.shard_map(local, mesh=split, in_specs=in_specs, out_specs=out_specs, check_vma=False)
```

```python
import math

import jax
import jax.numpy as jnp
from jax import lax
from jax.experimental import pallas as pl
from jax.experimental.pallas import tpu as pltpu
from jax.sharding import Mesh
from jax.sharding import PartitionSpec as P

HD = 80
LEN = 1024
BQ = 256
NORM_EPS = 1e-06
PERDIM_BASE = 1.442695041
NEG_FILL = -1e30
VMEM_BYTES = 16 << 20
BF16 = jnp.bfloat16
F32 = jnp.float32
NT = (((1,), (1,)), ((), ()))
NN = (((1,), (0,)), ((), ()))
TN = (((0,), (0,)), ((), ()))


def dot(a, b, dims=NN):
    return lax.dot_general(a, b, dims, preferred_element_type=F32)


def swap(value, axis, bit):
    size = lax.axis_size(axis)
    return lax.ppermute(value, axis, [(i, i ^ bit) for i in range(size)])


def tie(value, *others):
    return lax.optimization_barrier((value, *others))[0] if others else value


def rms_scale(values):
    return lax.rsqrt(jnp.mean(values * values, axis=-1, keepdims=True) + NORM_EPS)


def along_z(yj, first=0):
    return [((zj,), 2 * zj + yj, first) for zj in range(4)]


class Gather:
    def __init__(self, shard):
        self.whole = lax.axis_size("fsdp") != 8
        self.shard = shard

    def start(self, *after):
        shard = tie(self.shard, *after)
        if self.whole:
            gathered = lax.all_gather(shard, "fsdp", axis=0, tiled=True)
            self.own, self.other = [(gathered, [])], [(swap(gathered, "tx", 1), [])]
            self.along_z = self.along_xy = self.last = self.ready = (gathered,)
            return
        self.along_z = tuple(swap(shard, "fsdp", 2 * j) for j in (1, 2, 3))

    def middle(self, *after):
        if self.whole:
            return
        stacked = jnp.stack((self.shard, tie(self.along_z[0], *after), *self.along_z[1:]))
        self.ready = (stacked,)
        self.along_xy = (swap(stacked, "fsdp", 1), swap(stacked, "tx", 1))
        self.own = [(stacked, along_z(0)), (self.along_xy[0], along_z(1))]

    def finish(self, *after):
        if self.whole:
            return
        half = self.shard.shape[0] // 2
        from_y, from_x = tie(self.along_xy[0], *after), tie(self.along_xy[1], *after)
        self.last = (swap(from_y[:, :half], "tx", 1), swap(from_x[:, half:], "fsdp", 1))
        self.other = [(self.along_xy[1], along_z(0)), (self.last[0], along_z(1)), (self.last[1], along_z(1, half))]


class Columns:
    def __init__(self, gather, columns):
        self.gather, self.columns, self.whole = gather, columns, gather.whole

    def middle(self, *after):
        if self.whole:
            self.along_xy = self.ready = ()
            return
        parts = (self.gather.shard, *(tie(piece, *after) for piece in self.gather.along_z))
        stacked = jnp.stack([p[:, self.columns] for p in parts])
        self.ready = (stacked,)
        self.along_xy = (swap(stacked, "fsdp", 1), swap(stacked, "tx", 1))
        self.own = [(stacked, along_z(0)), (self.along_xy[0], along_z(1))]

    def finish(self, *after):
        if self.whole:
            self.own, self.other = [
                [(tie(side[0][0], *after)[:, self.columns], [])] for side in (self.gather.own, self.gather.other)
            ]
            self.last = ()
            return
        half = self.gather.shard.shape[0] // 2
        from_y, from_x = tie(self.along_xy[0], *after), tie(self.along_xy[1], *after)
        self.last = (swap(from_y[:, :half], "tx", 1), swap(from_x[:, half:], "fsdp", 1))
        self.other = [(self.along_xy[1], along_z(0)), (self.last[0], along_z(1)), (self.last[1], along_z(1, half))]


class HalvesGather:
    def __init__(self, halves):
        self.whole = lax.axis_size("fsdp") != 8
        self.halves = halves
        self.along_z, self.along_xy, self.stacked = [None, None], [None, None], [None, None]

    def start(self, n, *after):
        half = tie(self.halves[n], *after)
        if self.whole:
            self.along_z[n] = (half,)
            return
        self.along_z[n] = tuple(swap(half, "fsdp", 2 * j) for j in (1, 2, 3))

    def middle(self, n, *after):
        if self.whole:
            self.along_xy[n] = self.along_z[n]
            return
        self.stacked[n] = jnp.stack((self.halves[n], tie(self.along_z[n][0], *after), *self.along_z[n][1:]))
        self.along_xy[n] = (swap(self.stacked[n], "fsdp", 1), swap(self.stacked[n], "tx", 1))

    def finish(self, *after):
        if self.whole:
            shard = tie(jnp.concatenate(self.halves), *after)
            gathered = lax.all_gather(shard, "fsdp", axis=0, tiled=True)
            self.own, self.other = [(gathered, [])], [(swap(gathered, "tx", 1), [])]
            self.last = (self.other[0][0],)
            return
        (first_y, first_x), (second_y, second_x) = self.along_xy
        half = self.halves[0].shape[0]
        self.last = (swap(tie(first_y, *after), "tx", 1), swap(tie(second_x, *after), "fsdp", 1))
        self.own = [
            (self.stacked[0], along_z(0)), (first_y, along_z(1)), (self.stacked[1], along_z(0, half)), (second_y, along_z(1, half)),
        ]
        self.other = [
            (first_x, along_z(0)), (self.last[0], along_z(1)), (second_x, along_z(0, half)), (self.last[1], along_z(1, half)),
        ]


class Reduction:
    def __init__(self):
        self.whole = lax.axis_size("fsdp") != 8

    def send_far(self, other):
        self.other = other
        if self.whole:
            self.sent_far = other
            return
        self.sent_far = (swap(other[0], "tx", 1), swap(other[1], "fsdp", 1))

    def split(self, count):
        parts = [Reduction() for _ in range(count)]
        for c, p in enumerate(parts):
            if self.whole:
                p.other = p.sent_far = (self.other[c],)
            else:
                p.sent_far = tuple(r[c] for r in self.sent_far)
                p.other = (None, None, self.other[2 + c])
        return parts

    def send_xy(self, own, *after):
        self.own = own
        if self.whole:
            self.from_x, self.from_y = swap(self.other[0], "tx", 1), own[0]
            self.ready = (own[0],)
            return
        self.ready = add_halves(self.other[2], own[0], self.sent_far, after)
        self.from_x, self.from_y = swap(self.ready[0], "tx", 1), swap(self.ready[1], "fsdp", 1)

    def send_z(self, *after):
        if self.whole:
            total = self.own[0] + tie(self.from_x, *after)
            self.ready = (total,)
            self.parts = (lax.psum_scatter(total, "fsdp", scatter_dimension=0, tiled=True),)
            return
        self.ready = sum_pieces(tie(self.own[1], *after), self.from_x, self.from_y)
        self.parts = (self.ready[0], *(swap(self.ready[j], "fsdp", 2 * j) for j in (1, 2, 3)))

    def total(self):
        return sum(piece.astype(F32) for piece in self.parts)


def relay(done, going, own, *after):
    if done.whole:
        done.send_z(*after)
        going.send_xy(own, *after)
        return
    _, rows, cols = done.own[1].shape

    def kernel(near, from_x, from_y, next_near, far, next_x, next_y, *outs):
        *sums, along_x, along_y = outs
        for j, out in enumerate(sums):
            total = near[j].astype(F32) + from_x[j].astype(F32) + from_y[j].astype(F32)
            out[...] = total.astype(out.dtype)
        half = far.shape[1] // 2
        along_x[:, :half] = next_near[:, :half]
        along_x[:, half:] = (next_near[:, half:].astype(F32) + next_y[...].astype(F32)).astype(BF16)
        along_y[:, :half] = (far[:, :half].astype(F32) + next_x[...].astype(F32)).astype(BF16)
        along_y[:, half:] = far[:, half:]

    out_shape = [jax.ShapeDtypeStruct((rows, cols), BF16 if j else F32) for j in range(4)]
    out_shape += [jax.ShapeDtypeStruct(own[0].shape, BF16)] * 2
    args = (tie(done.own[1], *after), done.from_x, done.from_y, going.other[2], own[0], *going.sent_far)
    outs = call(kernel, "relay", [VMEM] * 7, tuple(out_shape), [], 0.01, *args, near=True)
    going.own, going.ready, done.ready = own, outs[4:], outs[:4]
    done.parts = (outs[0], *(swap(outs[j], "fsdp", 2 * j) for j in (1, 2, 3)))
    going.from_x, going.from_y = swap(outs[4], "tx", 1), swap(outs[5], "fsdp", 1)


class ReductionFirstZ:
    def __init__(self, squares):
        self.whole = lax.axis_size("fsdp") != 8
        self.squares = squares

    def send_z(self, *after):
        if self.whole:
            total = self.squares[0] + swap(tie(self.squares, *after)[1], "tx", 1)
            self.from_z = (lax.psum_scatter(total, "fsdp", scatter_dimension=0, tiled=True),)
            return
        squares = tie(self.squares, *after)
        self.from_z = tuple(swap(squares[j], "fsdp", 2 * j) for j in (1, 2, 3))

    def sum_z(self, *after):
        self.square = (self.squares,)
        if not self.whole:
            self.square = sum_squares(tie(self.squares, *after), self.from_z)

    def send_y(self, *after):
        if self.whole:
            self.from_y = self.from_z[0]
            return
        self.from_y = swap(tie(self.square[1], *after), "fsdp", 1)

    def send_x(self, *after):
        if self.whole:
            self.from_x = self.from_z[0]
            return
        self.pair = add(self.square[0], tie(self.from_y, *after))
        self.from_x = swap(self.pair[1], "tx", 1)

    def total(self):
        if self.whole:
            return self.from_x.astype(F32)
        return self.pair[0].astype(F32) + self.from_x.astype(F32)


def add(a, b):
    return (a.astype(F32) + b.astype(F32)).astype(BF16)


def sum_squares(squares, from_z):
    def kernel(squares, *refs):
        *from_z, near, far = refs
        for n, out in enumerate((near, far)):
            for r in range(2):
                total = squares[0, 2 * n + r].astype(F32)
                for piece in from_z:
                    total = total + piece[2 * n + r].astype(F32)
                out[r] = total.astype(BF16)

    out_shape = (jax.ShapeDtypeStruct((2, *squares.shape[2:]), BF16),) * 2
    return call(kernel, "sum_squares", [VMEM] * 4, out_shape, [], 0.01, squares, *from_z)


def sum_pieces(near, from_x, from_y):
    def kernel(near, from_x, from_y, *outs):
        for j, out in enumerate(outs):
            total = near[j].astype(F32) + from_x[j].astype(F32) + from_y[j].astype(F32)
            out[...] = total.astype(out.dtype)

    _, rows, cols = near.shape
    out_shape = tuple(jax.ShapeDtypeStruct((rows, cols), BF16 if j else F32) for j in range(4))
    return call(kernel, "sum_pieces", [VMEM] * 3, out_shape, [], 0.01, near, from_x, from_y)


def add_halves(near, far, sent_far, after):
    def kernel(near, far, from_x, from_y, along_x, along_y):
        half = near.shape[1] // 2
        along_x[:, :half] = near[:, :half]
        along_x[:, half:] = (near[:, half:].astype(F32) + from_y[...].astype(F32)).astype(BF16)
        along_y[:, :half] = (far[:, :half].astype(F32) + from_x[...].astype(F32)).astype(BF16)
        along_y[:, half:] = far[:, half:]

    out_shape = (jax.ShapeDtypeStruct(near.shape, BF16), jax.ShapeDtypeStruct(far.shape, BF16))
    return call(kernel, "add_halves", [VMEM] * 4, out_shape, [], 0.01, tie(near, *after), far, *sent_far, near=True)


VMEM = pl.BlockSpec(memory_space=pltpu.VMEM)
ANY = pl.BlockSpec(memory_space=pl.ANY)
SMEM = pl.BlockSpec(memory_space=pltpu.SMEM)


def call(kernel, name, in_specs, out_shape, scratch_shapes, micros, *args, near=False, away=(), away_out=(), by_hand=True):
    out_specs = jax.tree.map(lambda _: VMEM, out_shape)
    if near:
        spaces = [pltpu.HBM if n in away or s is ANY else pltpu.VMEM for n, s in enumerate(in_specs)]
        args = [
            a if s is SMEM else pltpu.with_memory_space_constraint(a, space)
            for a, s, space in zip(args, in_specs, spaces)
        ]
        out_shape = jax.tree.map(lambda o: pltpu.VMEM(o.shape, o.dtype), out_shape)
        if away_out:
            out_shape = [pltpu.HBM(o.shape, o.dtype) if n in away_out else o for n, o in enumerate(out_shape)]
            out_specs = [ANY if n in away_out and by_hand else VMEM for n in range(len(out_shape))]
    return pl.pallas_call(
        kernel,
        in_specs=in_specs,
        out_specs=out_specs,
        out_shape=out_shape,
        scratch_shapes=scratch_shapes,
        compiler_params=pltpu.CompilerParams(vmem_limit_bytes=VMEM_BYTES),
        cost_estimate=pl.CostEstimate(flops=int(micros * 1e9), bytes_accessed=1 << 10, transcendentals=0),
        name=name,
    )(*args)


def place_pieces(refs, entries, weight, rank, cols=slice(None), width=None, first_col=0):
    if len(refs) == 1 and not entries[0]:
        weight[:, first_col : first_col + width] = refs[0][:, cols]
        return
    shard = weight.shape[0] // 8
    for ref, places in zip(refs, entries):
        for index, j, first in places:
            piece = ref[(*index, slice(None), cols)]
            start = pl.multiple_of((rank ^ j) * shard + first, 16)
            weight[pl.ds(start, piece.shape[0]), first_col : first_col + width] = piece


def far_shapes(depth, cols, size, own, parts=1):
    if size != 8:
        return (jax.ShapeDtypeStruct((depth, cols // parts), BF16),) * parts
    rows = depth // 8
    near = (jax.ShapeDtypeStruct((4, rows, cols // parts), BF16),) * parts
    if own:
        return (*near, *near)
    lead = (parts,) if parts > 1 else ()
    return (jax.ShapeDtypeStruct((*lead, 4, rows // 2, cols // parts), BF16),) * 2 + near


def put_pieces(refs, block, start, rank, own, part=None):
    if len(refs[0].shape) == 2:
        refs[part or 0][start : start + block.shape[0], :] = block
        return
    near = refs[len(refs) // 2 + (part or 0)] if own else refs[2 + (part or 0)]
    rows = near.shape[1]
    for n in range(block.shape[0] // rows):
        j = (start // rows + n) ^ rank
        yj, zj = j & 1, j >> 1
        piece = block[n * rows : (n + 1) * rows]

        @pl.when(yj == 0)
        def _():
            near[zj] = piece

        @pl.when(yj == 1)
        def _():
            if own:
                refs[part or 0][zj] = piece
            elif part is None:
                refs[0][zj] = piece[: rows // 2]
                refs[1][zj] = piece[rows // 2 :]
            else:
                refs[0][part, zj] = piece[: rows // 2]
                refs[1][part, zj] = piece[rows // 2 :]


def assemble(place, gathers, depth, width):
    lists = [pieces for g in gathers for pieces in (g.own, g.other)]
    entries = [[p[1] for p in pieces] for pieces in lists]
    arrays = [p[0] for pieces in lists for p in pieces]
    counts = [pieces[0][0].shape[-1] for pieces in lists[::2]]
    parts = sum(counts) // width

    def kernel(place, *refs):
        pieces, outs = refs[: len(arrays)], refs[len(arrays) :]
        at, first = 0, 0
        for n, places in enumerate(entries):
            refs_n = pieces[at : at + len(places)]
            at += len(places)
            for i in range(counts[n // 2] // width):
                cols = slice(i * width, (i + 1) * width)
                place_pieces(refs_n, places, outs[first + i], place[1], cols, width, n % 2 * width)
            if n % 2:
                first += counts[n // 2] // width

    out_shape = tuple(jax.ShapeDtypeStruct((depth, 2 * width), BF16) for _ in range(parts))
    return call(kernel, "assemble", [SMEM] + [VMEM] * len(arrays), out_shape, [], 3, place, *arrays, near=True)


def pack_qkv(weights, vectors, chunks):
    _, shard, width = weights.shape
    part = width // chunks
    first = shard // 2
    cols = -(-(3 * width + 8) // 128) * 128

    def kernel(weights, vectors, *outs):
        blocks = [weights[i, :, c * part : (c + 1) * part] for c in range(chunks) for i in range(3)]
        blocks += [vectors[...].T, jnp.zeros((shard, cols - 3 * width - 8), F32)]
        packed = jnp.concatenate(blocks, axis=1).astype(BF16)
        outs[0][...] = packed[:first]
        outs[1][...] = packed[first:]

    out_shape = (jax.ShapeDtypeStruct((first, cols), BF16), jax.ShapeDtypeStruct((shard - first, cols), BF16))
    return call(kernel, "pack_qkv", [VMEM] * 2, out_shape, [], 1, weights, vectors)


BIAS_ROWS = sum((i + 1) * BQ for i in range(LEN // BQ))


def bias_rows(i):
    start = i * (i + 1) // 2 * BQ
    return slice(start, start + (i + 1) * BQ)


def mask_bias(doc_col, doc_row, bias):
    for i in range(LEN // BQ):
        lo, hi = i * BQ, (i + 1) * BQ
        same = doc_col[:hi, :] == doc_row[:, lo:hi]
        keys = lax.broadcasted_iota(jnp.int32, (hi, BQ), 0)
        queries = lax.broadcasted_iota(jnp.int32, (hi, BQ), 1) + lo
        bias[bias_rows(i), :] = jnp.where(same & (keys <= queries), 0.0, NEG_FILL)


def outer_rows(lo, rows, core):
    half = LEN // 2
    return pl.ds(pl.multiple_of(((lo // half) ^ core) * half + lo % half, rows), rows)


def head_rows(ref, block, columns, rows):
    for h in range(ref.shape[0]):
        ref[h, rows, :] = block[:, columns[h] : columns[h] + HD].astype(ref.dtype)


def join_heads(ref, heads):
    return jnp.concatenate([ref[h] for h in heads], axis=1)


def attn_forward(place, pieces, rows_in, scale, doc_col, doc_row, chunks, depth):
    arrays, places = [p[0] for p in pieces], [p[1] for p in pieces]
    cols = arrays[0].shape[-1]
    fresh = len(rows_in) == 2
    part = scale.shape[1] // 3
    per_chunk = part // HD
    heads = per_chunk * chunks
    starts = [[c * 3 * part + n * part + h * HD for c in range(chunks) for h in range(per_chunk)] for n in range(3)]

    def kernel(place, *refs):
        pieces, refs = refs[: len(arrays)], refs[len(arrays) :]
        sources, (scale, doc_col, doc_row) = refs[: len(rows_in)], refs[len(rows_in) : len(rows_in) + 3]
        outs = refs[len(rows_in) + 3 :]
        attns, (*away, lse) = outs[:chunks], outs[chunks : chunks + 5]
        if fresh:
            x, gains, *outs = outs[chunks + 5 :]
        else:
            x, outs = sources[0], outs[chunks + 5 :]
        bias, out_heads, query, key, value, weight, sems = outs
        copies = [
            pltpu.make_async_copy(source, target, sems.at[n])
            for n, (source, target) in enumerate(zip((query, key, value, weight), away))
        ]
        core, rank = place[0], place[1]
        half = LEN // 2
        place_pieces(pieces, places, weight, rank, slice(None), cols)
        mask_bias(doc_col, doc_row, bias)
        if fresh:
            gains[...] = weight[:, cols - 128 :].astype(F32).T
            gain = gains[64:65, :]
            for n, source in enumerate(sources):

                def norm(i, _, source=source, n=n):
                    block = pl.ds(pl.multiple_of(i * 128, 128), 128)
                    values = source[block, :].astype(F32)
                    target = pl.ds(pl.multiple_of(i * 128 + n * half, 128), 128)
                    x[target, :] = (values * rms_scale(values) * gain).astype(BF16)
                    return 0

                lax.fori_loop(0, half // 128, norm, 0)

        def project(i, _):
            lo = i * BQ
            block = dot(x[outer_rows(lo, BQ, core), :], weight[...])
            rows = pl.ds(pl.multiple_of(lo, BQ), BQ)
            scaled = jnp.concatenate(
                [block[:, c * 3 * part : c * 3 * part + part] * scale[:, :part] for c in range(chunks)], axis=1
            )
            head_rows(query, scaled, [h * HD for h in range(heads)], rows)
            head_rows(key, block, starts[1], rows)
            head_rows(value, block, starts[2], rows)
            return 0

        lax.fori_loop(0, LEN // BQ, project, 0)
        for copy in copies:
            copy.start()

        def attend(h, _):
            keys = key[h]
            value_t = value[h].T
            blocks = []
            for i in range(LEN // BQ):
                lo, hi = i * BQ, (i + 1) * BQ
                scores = dot(keys[:hi], query[h, lo:hi, :], NT) + bias[bias_rows(i), :]
                top = jnp.max(scores, axis=0, keepdims=True)
                probs = jnp.exp(scores - top)
                total = jnp.sum(probs, axis=0, keepdims=True)
                blocks.append(dot(value_t[:, :hi], probs.astype(BF16)) / total)
                lse[h, :, lo:hi] = top + jnp.log(total)
            out_heads[h] = jnp.concatenate(blocks, axis=1).T.astype(BF16)
            return 0

        def attend_two(n, _):
            attend(2 * n, 0)
            return attend(2 * n + 1, 0)

        lax.fori_loop(0, heads // 2, attend_two, 0)
        for c in range(chunks):
            joined = join_heads(out_heads, range(c * per_chunk, (c + 1) * per_chunk))
            for a in range(2):
                attns[c][outer_rows(a * half, half, core), :] = joined[a * half : (a + 1) * half]
        for copy in copies:
            copy.wait()

    per_head = jax.ShapeDtypeStruct((heads, LEN, HD), BF16)
    out_shape = (
        *(jax.ShapeDtypeStruct((LEN, part), BF16),) * chunks,
        per_head,
        per_head,
        per_head,
        jax.ShapeDtypeStruct((depth, cols), BF16),
        jax.ShapeDtypeStruct((heads, 1, LEN), F32),
    )
    scratch = [pltpu.VMEM((BIAS_ROWS, BQ), F32)] + [pltpu.VMEM((heads, LEN, HD), BF16)] * 4
    scratch += [pltpu.VMEM((depth, cols), BF16), pltpu.SemaphoreType.DMA((4,))]
    if fresh:
        out_shape += (jax.ShapeDtypeStruct((LEN, depth), BF16), jax.ShapeDtypeStruct((128, depth), F32))
    specs = [SMEM] + [VMEM] * (len(arrays) + len(rows_in) + 3)
    args = (place, *arrays, *rows_in, scale, doc_col, doc_row)
    outs = call(
        kernel, "attn_forward", specs, out_shape, scratch, 8, *args, near=True, away_out=range(chunks, chunks + 4)
    )
    saved = (*outs[chunks : chunks + 3], outs[chunks + 4])
    return outs[:chunks], saved, (outs[chunks + 3], *outs[chunks + 5 :])


SIDE = 32
SCALE_COLUMN = 4


def attn_backward(place, attns, saved, dout, x, doc_col, doc_row, scale, first, own, riders, other_sums):
    part = attns[0].shape[1]
    per_chunk = part // HD
    count = len(attns)
    heads = per_chunk * count
    depth = x.shape[1]
    size = lax.axis_size("fsdp")
    pieces_shape = far_shapes(depth, (3 * part + SIDE) * count, size, own, count)

    def kernel(place, *refs):
        attns, refs = refs[:count], refs[count:]
        *saved, lse, dout, x, doc_col, doc_row, scale, other_sums = refs[:10]
        riders, refs = refs[10 : 10 + len(riders_in)], refs[10 + len(riders_in) :]
        grads_out, sums_out, refs = refs[:count], refs[count], refs[count + 1 :]
        pieces, refs = refs[:-10], refs[-10:]
        dkey, dvalue, bias, douts, deltas, grads, query, key, value, sems = refs

        def copies(n):
            pair = pl.ds(2 * n, 2)
            return [
                pltpu.make_async_copy(source.at[pair], target.at[pair], sems.at[n, k])
                for k, (source, target) in enumerate(zip(saved, (query, key, value)))
            ]

        for n in range(heads // 2):
            for copy in copies(n):
                copy.start()
        core, rank = place[0], place[1]
        half = LEN // 2
        lanes = lax.broadcasted_iota(jnp.int32, (8, part), 1) // HD
        selector = jnp.where(lanes == lax.broadcasted_iota(jnp.int32, (8, part), 0), 1.0, 0.0)
        mask_bias(doc_col, doc_row, bias)
        for c in range(count):
            for i in range(LEN // BQ):
                lo, hi = i * BQ, (i + 1) * BQ
                rows = outer_rows(lo, BQ, core)
                dout_block = dout[rows, first + c * part : first + (c + 1) * part]
                products = attns[c][rows, :].astype(F32) * dout_block.astype(F32)
                delta = lax.dot_general(
                    selector, products, NT, precision=lax.Precision.HIGHEST, preferred_element_type=F32
                )
                for h in range(per_chunk):
                    deltas[c * per_chunk + h, :, lo:hi] = delta[h : h + 1, :]
                    douts[c * per_chunk + h, lo:hi, :] = dout_block[:, h * HD : (h + 1) * HD]

        def attend(h, sums):
            keys = key[h]
            key_t = keys.T
            dquery_parts = []
            for i in range(LEN // BQ):
                lo, hi = i * BQ, (i + 1) * BQ
                queries = query[h, lo:hi, :]
                dout_head = douts[h, lo:hi, :]
                scores = dot(keys[:hi], queries, NT) + bias[bias_rows(i), :]
                probs = jnp.exp(scores - lse[h, :, lo:hi])
                dprobs = dot(value[h, :hi, :], dout_head, NT)
                dscores = (probs * (dprobs - deltas[h, :, lo:hi])).astype(BF16)
                dv = dot(probs.astype(BF16), dout_head)
                dk = dot(dscores, queries)
                dquery_parts.append(dot(key_t[:, :hi], dscores))
                if i:
                    dkey[:lo] += dk[:lo]
                    dvalue[:lo] += dv[:lo]
                dkey[lo:hi] = dk[lo:]
                dvalue[lo:hi] = dv[lo:]
            dquery = jnp.concatenate(dquery_parts, axis=1).T
            grads[0, h] = (dquery * scale[...]).astype(BF16)
            grads[1, h] = dkey[...].astype(BF16)
            grads[2, h] = dvalue[...].astype(BF16)
            return sums + jnp.sum(dquery * query[h].astype(F32), axis=0, keepdims=True)

        def attend_two(n, sums):
            for copy in copies(n):
                copy.wait()
            return attend(2 * n + 1, attend(2 * n, sums))

        sums = lax.fori_loop(0, heads // 2, attend_two, jnp.zeros((1, HD), F32))
        sums = sums / scale[...]
        sums_out[...] = sums
        side = [jnp.zeros((depth, SIDE), BF16)] * count
        if size == 8:
            units = riders[0][:, 0 if own else units_width : units_width if own else 2 * units_width]
            units = [units[:, n * (depth // size) : (n + 1) * (depth // size)] for n in range(2)]
            nothing = jnp.zeros((1, depth), F32)
            rows = [r[...] for r in riders[1:]] if own else [nothing] * 2
            rows += [jnp.concatenate([u] * size, axis=1) for u in units] + [nothing] * 4
            columns = jnp.concatenate(rows).T
            if own:
                scales = jnp.broadcast_to(sums + other_sums[...], (128, HD)).T[:, :8]
                block = jnp.concatenate([scales, jnp.zeros((depth // size - HD, 8), F32)])
                column = lax.broadcasted_iota(jnp.int32, (depth, 8), 1) == SCALE_COLUMN
                columns = jnp.where(column, jnp.concatenate([block] * size), columns)
            side[-1] = jnp.concatenate([columns, jnp.zeros((depth, SIDE - 8), F32)], axis=1).astype(BF16)
        for c in range(count):
            mine = range(c * per_chunk, (c + 1) * per_chunk)
            joined = jnp.concatenate([grads[n, h] for n in range(3) for h in mine], axis=1)
            for a in range(2):
                grads_out[c][outer_rows(a * half, half, core), :] = joined[a * half : (a + 1) * half]
            for g in range(2):
                start = g * depth // 2
                block = dot(x[:, start : start + depth // 2], grads_out[c][...], TN).astype(BF16)
                block = jnp.concatenate([block, side[c][start : start + depth // 2]], axis=1)
                put_pieces(pieces, block, start, rank, own, c if count > 1 else None)

    out_shape = (
        *(jax.ShapeDtypeStruct((LEN, 3 * part), BF16),) * count,
        jax.ShapeDtypeStruct((1, HD), F32),
        *pieces_shape,
    )
    scratch = [
        pltpu.VMEM((LEN, HD), F32),
        pltpu.VMEM((LEN, HD), F32),
        pltpu.VMEM((BIAS_ROWS, BQ), F32),
        pltpu.VMEM((heads, LEN, HD), BF16),
        pltpu.VMEM((heads, 1, LEN), F32),
        pltpu.VMEM((3, heads, LEN, HD), BF16),
        *(pltpu.VMEM((heads, LEN, HD), BF16),) * 3,
        pltpu.SemaphoreType.DMA((heads // 2, 3)),
    ]
    riders_in = riders
    units_width = riders[0].shape[1] // 2
    args = (place, *attns, *saved, dout, x, doc_col, doc_row, scale, other_sums, *riders)
    specs = [SMEM] + [VMEM] * count + [ANY] * 3 + [VMEM] * (len(args) - 4 - count)
    outs = call(kernel, "attn_backward", specs, out_shape, scratch, 10, *args, near=True)
    return outs[:count], outs[count], outs[count + 1 :]


def put_both(outs, block, start, rank, size):
    width = block.shape[1] // 2
    count = len(outs) // 2 if size != 8 else 2
    put_pieces(outs[:count], block[:, :width], start, rank, True)
    put_pieces(outs[count:], block[:, width:], start, rank, False)


def weight_grads(place, pairs, name):
    rows, depth = pairs[0][0][0].shape
    width = pairs[0][1].shape[1] // 2
    size = lax.axis_size("fsdp")
    shapes = [far_shapes(depth, width * len(pairs), size, own) for own in (True, False)]

    def kernel(place, *refs):
        ins, outs = refs[: 3 * len(pairs)], refs[3 * len(pairs) :]
        for g in range(2):
            cols = slice(g * depth // 2, (g + 1) * depth // 2)
            blocks = []
            for n in range(len(pairs)):
                near, far, right = ins[3 * n : 3 * n + 3]
                block = dot(near[:, cols], right[:rows, :], TN) + dot(far[:, cols], right[rows:, :], TN)
                blocks.append(block.astype(BF16))
            joined = [b[:, r * width : (r + 1) * width] for r in range(2) for b in blocks]
            put_both(outs, jnp.concatenate(joined, axis=1), g * depth // 2, place[1], size)

    args = [a for halves, right in pairs for a in (*halves, right)]
    outs = call(
        kernel, name, [SMEM] + [VMEM] * len(args), (*shapes[0], *shapes[1]), [], 4 * len(pairs), place, *args, near=True
    )
    return outs[: len(shapes[0])], outs[len(shapes[0]) :]


def out_forward(attns, out_t, inputs):
    rows, depth = inputs.shape

    def kernel(*refs):
        attns, (out_t, inputs, sent, kept) = refs[:-4], refs[-4:]
        heads = jnp.concatenate([a[...] for a in attns], axis=1)
        for i in range(rows // BQ):
            lo, hi = i * BQ, (i + 1) * BQ
            sent[lo:hi, :] = dot(heads[rows + lo : rows + hi], out_t[...], NT).astype(BF16)
            kept[lo:hi, :] = inputs[lo:hi, :].astype(F32) + dot(heads[lo:hi], out_t[...], NT)

    out_shape = (jax.ShapeDtypeStruct((rows, depth), BF16), jax.ShapeDtypeStruct((rows, depth), F32))
    return call(kernel, "out_forward", [VMEM] * (len(attns) + 2), out_shape, [], 3, *attns, out_t, inputs, near=True)


def second_norm(kept, received, gain):
    def kernel(kept, received, gain, resid_out, normed_out):
        resid = kept[...] + received[...].astype(F32)
        resid_out[...] = resid
        normed_out[...] = (resid * rms_scale(resid) * gain[...]).astype(BF16)

    out_shape = (jax.ShapeDtypeStruct(kept.shape, F32), jax.ShapeDtypeStruct(kept.shape, BF16))
    return call(kernel, "second_norm", [VMEM] * 3, out_shape, [], 1, kept, received, gain, near=True)


def mlp(normed, cot, up, down_t, bias_up):
    rows, depth = normed[0].shape
    units = up.shape[1]

    def kernel(n_near, n_far, c_near, c_far, up, down_t, bias, hidden, grad_pre, bias_sum, *outs):
        sums = jnp.zeros((1, units), F32)
        for side, (n, c) in enumerate(((n_near, c_near), (n_far, c_far))):
            out_mlp, out_grad = outs[2 * side : 2 * side + 2]

            def step(i, sums, n=n, c=c, side=side, out_mlp=out_mlp, out_grad=out_grad):
                block = pl.ds(pl.multiple_of(i * BQ, BQ), BQ)
                target = pl.ds(pl.multiple_of(i * BQ + side * rows, BQ), BQ)
                pre = dot(n[block, :], up[...]) + bias[...]
                sig = 1.0 / (1.0 + jnp.exp(-pre))
                units_low = (pre * sig).astype(BF16)
                grad = dot(c[block, :], down_t[...])
                grad_low = (grad * (sig + pre * sig * (1.0 - sig))).astype(BF16)
                hidden[target, :] = units_low
                grad_pre[target, :] = grad_low
                out_mlp[block, :] = dot(units_low, down_t[...], NT).astype(BF16)
                out_grad[block, :] = dot(grad_low, up[...], NT).astype(BF16)
                return sums + jnp.sum(grad_low.astype(F32), axis=0, keepdims=True)

            sums = lax.fori_loop(0, rows // BQ, step, sums)
        bias_sum[...] = sums

    low = jax.ShapeDtypeStruct((rows, depth), BF16)
    out_shape = (
        jax.ShapeDtypeStruct((2 * rows, units), BF16),
        jax.ShapeDtypeStruct((2 * rows, units), BF16),
        jax.ShapeDtypeStruct((1, units), F32),
        low,
        low,
        low,
        low,
    )
    return call(kernel, "mlp", [VMEM] * 7, out_shape, [], 10, *normed, *cot, up, down_t, bias_up, near=True)


def resid_grads(grads, mlps, resid, cot, gain, bias):
    def kernel(grad_near, grad_far, mlp_near, mlp_far, resid, cot, gain, bias, low_out, sum_out, layer):
        for i in range(resid.shape[0] // BQ):
            block = slice(i * BQ, (i + 1) * BQ)
            held = resid[block, :]
            grad = grad_near[block, :].astype(F32) + grad_far[block, :].astype(F32)
            recip = rms_scale(held)
            unit = held * recip
            part = jnp.sum(grad * unit, axis=0, keepdims=True)
            sum_out[...] = part if i == 0 else sum_out[...] + part
            scaled = grad * gain[...]
            mean = jnp.mean(scaled * unit, axis=-1, keepdims=True)
            total = cot[block, :].astype(F32) + recip * (scaled - unit * mean)
            low_out[block, :] = total.astype(BF16)
            mlp = mlp_near[block, :].astype(F32) + mlp_far[block, :].astype(F32)
            layer[block, :] = (held + mlp + bias[...]).astype(BF16)

    out_shape = (
        jax.ShapeDtypeStruct(resid.shape, BF16),
        jax.ShapeDtypeStruct((1, resid.shape[1]), F32),
        jax.ShapeDtypeStruct(resid.shape, BF16),
    )
    args = (*grads, *mlps, resid, cot, gain, bias)
    return call(kernel, "resid_grads", [VMEM] * 8, out_shape, [], 2, *args, near=True)


def head_grads(place, grads, out_t, attns):
    rows, depth = grads[0].shape
    width = out_t.shape[1] // 2
    size = lax.axis_size("fsdp")
    shard = depth // size

    def kernel(place, near, far, out_t, *refs):
        attns, (heads_out, squares) = refs[:-2], refs[-2:]
        for i in range(2 * rows // BQ):
            source = near if i < rows // BQ else far
            block = slice(i * BQ % rows, i * BQ % rows + BQ)
            heads_out[i * BQ : (i + 1) * BQ, :] = dot(source[block, :], out_t[...]).astype(BF16)
        heads = jnp.concatenate([a[...] for a in attns], axis=1)
        for g in range(2):
            start = g * depth // 2
            cols = slice(start, start + depth // 2)
            block = (dot(near[:, cols], heads[:rows], TN) + dot(far[:, cols], heads[rows:], TN)).astype(BF16)
            for r in range(2):
                side = block[:, r * width : (r + 1) * width]
                if size != 8:
                    squares[r, start : start + depth // 2, :] = side
                    continue
                for n in range(side.shape[0] // shard):
                    j = (start // shard + n) ^ place[1]
                    squares[j >> 1, 2 * (j & 1) + r] = side[n * shard : (n + 1) * shard]

    squares_shape = (4, 4, shard, width) if size == 8 else (2, depth, width)
    out_shape = (jax.ShapeDtypeStruct((2 * rows, 2 * width), BF16), jax.ShapeDtypeStruct(squares_shape, BF16))
    args = (place, *grads, out_t, *attns)
    specs = [SMEM] + [VMEM] * (len(args) - 1)
    return call(kernel, "head_grads", specs, out_shape, [], 6, *args, near=True, away=range(3, len(args)))


def input_grads(grads, weights, rows):
    depth = weights[0].shape[0]
    counts = [len(g) for g in grads]

    def kernel(*refs):
        ins, weights, (sent, kept) = refs[: sum(counts)], refs[sum(counts) : -2], refs[-2:]
        for side, out in enumerate((kept, sent)):

            def step(i, _, side=side, out=out):
                total, at = None, 0
                block = pl.ds(pl.multiple_of(i * BQ + side * rows, BQ), BQ)
                for count, weight in zip(counts, weights):
                    left = jnp.concatenate([g[block, :] for g in ins[at : at + count]], axis=1)
                    at += count
                    partial = dot(left, weight[:, : left.shape[1]], NT)
                    total = partial if total is None else total + partial
                out[pl.ds(pl.multiple_of(i * BQ, BQ), BQ), :] = total.astype(BF16)
                return 0

            lax.fori_loop(0, rows // BQ, step, 0)

    out_shape = (jax.ShapeDtypeStruct((rows, depth), BF16),) * 2
    flat = [g for pair in grads for g in pair]
    return call(
        kernel, "input_grads", [VMEM] * (len(flat) + len(weights)), out_shape, [], 10, *flat, *weights, near=True
    )


def first_norm_grads(kept, received, inputs, resid_grad, gain):
    def kernel(kept, received, inputs, resid_grad, gain, grad_out):
        for i in range(inputs.shape[0] // BQ):
            block = slice(i * BQ, (i + 1) * BQ)
            values = inputs[block, :].astype(F32)
            recip = rms_scale(values)
            unit = values * recip
            scaled = (kept[block, :].astype(F32) + received[block, :].astype(F32)) * gain[...]
            mean = jnp.mean(scaled * unit, axis=-1, keepdims=True)
            grad_out[block, :] = (resid_grad[block, :].astype(F32) + recip * (scaled - unit * mean)).astype(BF16)

    out_shape = jax.ShapeDtypeStruct(inputs.shape, BF16)
    args = (kept, received, inputs, resid_grad, gain)
    return call(kernel, "first_norm_grads", [VMEM] * 5, out_shape, [], 0.01, *args)


def join_chunks(parts, weights, factors):
    counts = [len(p) for p in parts]
    _, shard, width = weights.shape
    part = width // len(parts)

    def kernel(*refs):
        *refs, weights, factors, out, rows = refs
        at = 0
        sums = []
        for count in counts:
            sums.append(sum(ref[...].astype(F32) for ref in refs[at : at + count]))
            at += count
        total = jnp.zeros((shard, 1), F32)
        for i in range(3):
            joined = jnp.concatenate([s[:, i * part : (i + 1) * part] for s in sums], axis=1)
            out[i] = joined
            total = total + jnp.sum(joined * weights[i].astype(BF16).astype(F32), axis=1, keepdims=True)
        side = jnp.concatenate([sums[-1][:, 3 * part : 3 * part + SIDE], jnp.zeros((shard, 128 - SIDE), F32)], axis=1)
        lane = lax.broadcasted_iota(jnp.int32, (shard, 128), 1)
        rows[...] = jnp.where(lane == SCALE_COLUMN + 1, total, side).T[:8, :] * factors[...]

    flat = [p for pieces in parts for p in pieces]
    out_shape = (jax.ShapeDtypeStruct((3, shard, width), F32), jax.ShapeDtypeStruct((8, shard), F32))
    return call(kernel, "join_chunks", [VMEM] * (len(flat) + 2), out_shape, [], 1, *flat, weights, factors)


def local(
    inputs,
    doc_ids,
    w_qkv,
    w_out,
    w_up,
    up_bias,
    w_down,
    down_bias,
    attn_gain,
    mlp_gain,
    dim_scale,
    cotangent,
):
    shard, _, width = w_qkv.shape
    size = lax.axis_size("fsdp")
    depth = shard * size
    rows = inputs.shape[0]
    core, tx, rank = lax.axis_index("core"), lax.axis_index("tx"), lax.axis_index("fsdp")
    place = jnp.stack([core, rank]).astype(jnp.int32)

    chunks = 2
    heads = width // HD
    part = width // chunks
    vectors = jnp.concatenate([jnp.stack([attn_gain, mlp_gain, down_bias]), jnp.zeros((5, shard), F32)])
    qkv = HalvesGather(pack_qkv(jnp.transpose(w_qkv, (1, 0, 2)), vectors, chunks))
    rest = Gather(jnp.concatenate([w_out.T, w_up, w_down.T], axis=1).astype(BF16))
    qkv.start(0)

    input_rows = (inputs, swap(inputs, "core", 1))
    cots = (cotangent, swap(cotangent, "core", 1))
    docs = lax.dynamic_slice_in_dim(doc_ids, tx * LEN, LEN, 0)
    doc_col, doc_row = docs[:, None], docs[None, :]
    scale_base = PERDIM_BASE / math.sqrt(HD)
    query_scale = scale_base * jax.nn.softplus(dim_scale)
    colscale = jnp.concatenate([jnp.tile(query_scale, heads // chunks), jnp.ones((2 * part,), F32)])[None]

    scale_factor = scale_base * jax.nn.sigmoid(dim_scale)
    factors = jnp.ones((8, shard), F32).at[SCALE_COLUMN + 1].set(1.0 / attn_gain.astype(BF16).astype(F32))
    if size == 8:
        factors = factors.at[SCALE_COLUMN, :HD].set(scale_factor)
    downbias_sum = jnp.sum(cotangent.astype(F32), axis=0)[None]

    bias_far = swap(tie(up_bias, input_rows[1], cots[1]), "tx", 1)
    now = (*qkv.along_z[0], input_rows[1], cots[1], bias_far)
    qkv.middle(0, *now)
    qkv.start(1, *now)
    now = (*qkv.along_xy[0], *qkv.along_z[1])
    qkv.middle(1, *now)
    rest.start(*now)
    now = qkv.along_xy[1]
    qkv.finish(*now)
    own_attns, own_saved, (weight_own, normed_first, gains) = attn_forward(
        place, qkv.own, (tie(inputs, *now), input_rows[1]), colscale, doc_col, doc_row, chunks, depth
    )
    now = (own_saved[3], *rest.along_z, *qkv.last)
    out_columns, mlp_columns = Columns(rest, slice(0, 2 * width)), Columns(rest, slice(2 * width, 3 * width))
    out_columns.middle(*now)
    mlp_columns.middle(*now, *out_columns.ready)
    other_attns, other_saved, (weight_other,) = attn_forward(
        place, qkv.other, (tie(normed_first, *now, *mlp_columns.ready, downbias_sum, factors),), colscale, doc_col, doc_row, chunks, depth
    )
    now = (other_saved[3], *out_columns.along_xy)
    out_columns.finish(*now)
    mlp_columns.finish(*now, *mlp_columns.along_xy)
    bias_up = jnp.concatenate([up_bias, bias_far])[None]
    attns = [*own_attns, *other_attns]
    gain_first, gain_second, bias_second = [gains[64 + i : 65 + i] for i in range(3)]
    if size == 8:
        out_columns.other[-1] = (tie(out_columns.other[-1][0], *mlp_columns.along_xy), out_columns.other[-1][1])
    out_t, up = assemble(place, (out_columns,), depth, width)
    sent, kept = out_forward(attns, out_t, inputs)
    sent = tie(sent, *mlp_columns.last)
    resid_first, normed_own = second_norm(kept, swap(sent, "core", 1), gain_second)
    normeds = (normed_own, swap(normed_own, "core", 1))
    (down_t,) = assemble(place, (mlp_columns,), depth, width)
    hidden, grad_pre, upbias_sum, mlp_kept, grad_kept, mlp_sent, grad_sent = mlp(normeds, cots, up, down_t, bias_up)
    grads = (grad_kept, swap(grad_sent, "core", 1))
    mlps = (mlp_kept, swap(mlp_sent, "core", 1))
    updown_own, updown_other = weight_grads(place, [(normeds, grad_pre), (cots, hidden)], "updown_grads")
    updown, both = Reduction(), Reduction()
    now = (updown_own[-1], grads[1], mlps[1])
    updown.send_far([tie(p, *now) for p in updown_other[:2]] + list(updown_other[2:]))
    grad_own, mlpgain_sum, layer_out = resid_grads(
        (tie(grad_kept, *now), grads[1]), mlps, resid_first, cotangent, gain_second, bias_second
    )
    grad_attn = (grad_own, swap(grad_own, "core", 1))
    grad_heads, out_grads = head_grads(place, grad_attn, out_t, attns)
    out = ReductionFirstZ(out_grads)
    out.send_z(grad_heads)
    now = (grad_heads, *updown.sent_far)
    updown.send_xy(updown_own, *now)

    def back(attns, saved, first_col, own, riders, other_sums, *now):
        dout = tie(grad_heads, *now)
        return attn_backward(
            place, attns, saved, dout, normed_first, doc_col, doc_row, query_scale[None], first_col, own, riders, other_sums
        )

    grad_other, sums_other, pieces_other = back(
        other_attns, other_saved, width, False, (upbias_sum,), query_scale[None], *now, *updown.ready
    )
    now = (sums_other, updown.from_x, updown.from_y)
    both.send_far([tie(p, *now) for p in pieces_other[:2]] + list(pieces_other[2:]))
    grad_first, sums_first, pieces_first = back(
        own_attns, own_saved, 0, True, (upbias_sum, mlpgain_sum, downbias_sum), sums_other, *now
    )
    now = (sums_first, *both.sent_far, *out.from_z)
    first, second = both.split(chunks)
    near_far = [pieces_first[c::chunks] for c in range(chunks)]
    out.sum_z(*now)
    relay(updown, first, near_far[0], *now)
    sent, kept = input_grads(
        [[tie(grad_first[0], *first.ready, *updown.ready, *out.square), grad_first[1]], list(grad_other)],
        [weight_own, weight_other], rows,
    )
    now = (sent, first.from_x, first.from_y, *updown.parts[1:])
    relay(first, second, near_far[1], *now)
    now = (second.from_x, second.from_y, *first.parts[1:], *updown.parts[1:])
    second.send_z(*now)
    out.send_y(*now, *second.ready)
    received = swap(tie(sent, *now, *second.ready), "core", 1)
    out.send_x()
    input_grad = first_norm_grads(kept, received, inputs, grad_own, gain_first)
    updown_grad, out_grad = updown.total(), out.total()
    second_parts = (tie(second.parts[0], out.from_x, input_grad), *second.parts[1:])
    qkv_grad, small = join_chunks([first.parts, second_parts], jnp.transpose(w_qkv, (1, 0, 2)), factors)
    tensor = ("tx", "core")
    others = [lax.ppermute(small, tensor, [(i, i ^ bit) for i in range(4)]) for bit in (1, 2, 3)]
    summed = small + others[0] + others[1] + others[2]
    if size == 8:
        upbias_grad = small[2:4].reshape(-1)
        downbias_grad, mlpgain_grad, scale_sum = summed[1], summed[0], summed[SCALE_COLUMN, :HD]
    else:
        everything = ("fsdp", "tx", "core")
        upbias_grad = lax.psum(upbias_sum[0, :width] + swap(upbias_sum[0, width:], "tx", 1), "fsdp")
        vectors = lax.psum(jnp.concatenate([downbias_sum, mlpgain_sum]), everything)
        downbias_grad, mlpgain_grad = lax.dynamic_slice_in_dim(vectors, rank * shard, shard, 1)
        scale_sum = scale_factor * lax.psum(sums_other + sums_first, everything)[0]
    return (
        layer_out,
        input_grad,
        jnp.transpose(qkv_grad, (1, 0, 2)),
        out_grad.T,
        updown_grad[:, :width],
        upbias_grad,
        updown_grad[:, width:].T,
        downbias_grad,
        summed[SCALE_COLUMN + 1],
        mlpgain_grad,
        scale_sum,
    )


def solution(mesh):
    size, tensor = mesh.shape["fsdp"], mesh.shape["tensor"]
    split = Mesh(mesh.devices.reshape(size, tensor // 2, 2), ("fsdp", "tx", "core"))
    tokens = P(("fsdp", "tx", "core"), None)
    tensor_axes = ("tx", "core")
    in_specs = (
        tokens,
        P("fsdp"),
        P("fsdp", None, tensor_axes),
        P(tensor_axes, "fsdp"),
        P("fsdp", tensor_axes),
        P(tensor_axes),
        P(tensor_axes, "fsdp"),
        P("fsdp"),
        P("fsdp"),
        P("fsdp"),
        P(),
        tokens,
    )
    out_specs = (
        tokens,
        tokens,
        P("fsdp", None, tensor_axes),
        P(tensor_axes, "fsdp"),
        P("fsdp", tensor_axes),
        P(tensor_axes),
        P(tensor_axes, "fsdp"),
        P("fsdp"),
        P("fsdp"),
        P("fsdp"),
        P(),
    )
    return jax.shard_map(local, mesh=split, in_specs=in_specs, out_specs=out_specs, check_vma=False)
```

```python
import math

import jax
import jax.numpy as jnp
from jax import lax
from jax.experimental import pallas as pl
from jax.experimental.pallas import tpu as pltpu
from jax.sharding import Mesh
from jax.sharding import PartitionSpec as P

HD = 80
LEN = 1024
BQ = 256
NORM_EPS = 1e-06
PERDIM_BASE = 1.442695041
NEG_FILL = -1e30
VMEM_BYTES = 16 << 20
BF16 = jnp.bfloat16
F32 = jnp.float32
NT = (((1,), (1,)), ((), ()))
NN = (((1,), (0,)), ((), ()))
TN = (((0,), (0,)), ((), ()))


def dot(a, b, dims=NN):
    return lax.dot_general(a, b, dims, preferred_element_type=F32)


def swap(value, axis, bit):
    size = lax.axis_size(axis)
    return lax.ppermute(value, axis, [(i, i ^ bit) for i in range(size)])


def tie(value, *others):
    return lax.optimization_barrier((value, *others))[0] if others else value


def rms_scale(values):
    return lax.rsqrt(jnp.mean(values * values, axis=-1, keepdims=True) + NORM_EPS)


def along_z(yj, first=0):
    return [((zj,), 2 * zj + yj, first) for zj in range(4)]


class Gather:
    def __init__(self, shard):
        self.whole = lax.axis_size("fsdp") != 8
        self.shard = shard

    def start(self, *after):
        shard = tie(self.shard, *after)
        if self.whole:
            gathered = lax.all_gather(shard, "fsdp", axis=0, tiled=True)
            self.own, self.other = [(gathered, [])], [(swap(gathered, "tx", 1), [])]
            self.along_z = self.along_xy = self.last = self.ready = (gathered,)
            return
        self.along_z = tuple(swap(shard, "fsdp", 2 * j) for j in (1, 2, 3))

    def middle(self, *after):
        if self.whole:
            return
        stacked = jnp.stack((self.shard, tie(self.along_z[0], *after), *self.along_z[1:]))
        self.ready = (stacked,)
        self.along_xy = (swap(stacked, "fsdp", 1), swap(stacked, "tx", 1))
        self.own = [(stacked, along_z(0)), (self.along_xy[0], along_z(1))]

    def finish(self, *after):
        if self.whole:
            return
        half = self.shard.shape[0] // 2
        from_y, from_x = tie(self.along_xy[0], *after), tie(self.along_xy[1], *after)
        self.last = (swap(from_y[:, :half], "tx", 1), swap(from_x[:, half:], "fsdp", 1))
        self.other = [(self.along_xy[1], along_z(0)), (self.last[0], along_z(1)), (self.last[1], along_z(1, half))]


class Columns:
    def __init__(self, gather, columns):
        self.gather, self.columns, self.whole = gather, columns, gather.whole

    def middle(self, *after):
        if self.whole:
            self.along_xy = self.ready = ()
            return
        parts = (self.gather.shard, *(tie(piece, *after) for piece in self.gather.along_z))
        stacked = jnp.stack([p[:, self.columns] for p in parts])
        self.ready = (stacked,)
        self.along_xy = (swap(stacked, "fsdp", 1), swap(stacked, "tx", 1))
        self.own = [(stacked, along_z(0)), (self.along_xy[0], along_z(1))]

    def finish(self, *after):
        if self.whole:
            self.own, self.other = [
                [(tie(side[0][0], *after)[:, self.columns], [])] for side in (self.gather.own, self.gather.other)
            ]
            self.last = ()
            return
        half = self.gather.shard.shape[0] // 2
        from_y, from_x = tie(self.along_xy[0], *after), tie(self.along_xy[1], *after)
        self.last = (swap(from_y[:, :half], "tx", 1), swap(from_x[:, half:], "fsdp", 1))
        self.other = [(self.along_xy[1], along_z(0)), (self.last[0], along_z(1)), (self.last[1], along_z(1, half))]


class HalvesGather:
    def __init__(self, halves):
        self.whole = lax.axis_size("fsdp") != 8
        self.halves = halves
        self.along_z, self.along_xy, self.stacked = [None, None], [None, None], [None, None]

    def start(self, n, *after):
        half = tie(self.halves[n], *after)
        if self.whole:
            self.along_z[n] = (half,)
            return
        self.along_z[n] = tuple(swap(half, "fsdp", 2 * j) for j in (1, 2, 3))

    def middle(self, n, *after):
        if self.whole:
            self.along_xy[n] = self.along_z[n]
            return
        self.stacked[n] = jnp.stack((self.halves[n], tie(self.along_z[n][0], *after), *self.along_z[n][1:]))
        self.along_xy[n] = (swap(self.stacked[n], "fsdp", 1), swap(self.stacked[n], "tx", 1))

    def finish(self, *after):
        if self.whole:
            shard = tie(jnp.concatenate(self.halves), *after)
            gathered = lax.all_gather(shard, "fsdp", axis=0, tiled=True)
            self.own, self.other = [(gathered, [])], [(swap(gathered, "tx", 1), [])]
            self.last = (self.other[0][0],)
            return
        (first_y, first_x), (second_y, second_x) = self.along_xy
        half = self.halves[0].shape[0]
        self.last = (swap(tie(first_y, *after), "tx", 1), swap(tie(second_x, *after), "fsdp", 1))
        self.own = [
            (self.stacked[0], along_z(0)), (first_y, along_z(1)), (self.stacked[1], along_z(0, half)), (second_y, along_z(1, half)),
        ]
        self.other = [
            (first_x, along_z(0)), (self.last[0], along_z(1)), (second_x, along_z(0, half)), (self.last[1], along_z(1, half)),
        ]


class Reduction:
    def __init__(self):
        self.whole = lax.axis_size("fsdp") != 8

    def send_far(self, other):
        self.other = other
        if self.whole:
            self.sent_far = other
            return
        self.sent_far = (swap(other[0], "tx", 1), swap(other[1], "fsdp", 1))

    def split(self, count):
        parts = [Reduction() for _ in range(count)]
        for c, p in enumerate(parts):
            if self.whole:
                p.other = p.sent_far = (self.other[c],)
            else:
                p.sent_far = tuple(r[c] for r in self.sent_far)
                p.other = (None, None, self.other[2 + c])
        return parts

    def send_xy(self, own, *after):
        self.own = own
        if self.whole:
            self.from_x, self.from_y = swap(self.other[0], "tx", 1), own[0]
            self.ready = (own[0],)
            return
        self.ready = add_halves(self.other[2], own[0], self.sent_far, after)
        self.from_x, self.from_y = swap(self.ready[0], "tx", 1), swap(self.ready[1], "fsdp", 1)

    def send_z(self, *after):
        if self.whole:
            total = self.own[0] + tie(self.from_x, *after)
            self.ready = (total,)
            self.parts = (lax.psum_scatter(total, "fsdp", scatter_dimension=0, tiled=True),)
            return
        self.ready = sum_pieces(tie(self.own[1], *after), self.from_x, self.from_y)
        self.parts = (self.ready[0], *(swap(self.ready[j], "fsdp", 2 * j) for j in (1, 2, 3)))

    def total(self):
        return sum(piece.astype(F32) for piece in self.parts)


def relay(done, going, own, *after):
    if done.whole:
        done.send_z(*after)
        going.send_xy(own, *after)
        return
    _, rows, cols = done.own[1].shape

    def kernel(near, from_x, from_y, next_near, far, next_x, next_y, *outs):
        *sums, along_x, along_y = outs
        for j, out in enumerate(sums):
            total = near[j].astype(F32) + from_x[j].astype(F32) + from_y[j].astype(F32)
            out[...] = total.astype(out.dtype)
        half = far.shape[1] // 2
        along_x[:, :half] = next_near[:, :half]
        along_x[:, half:] = (next_near[:, half:].astype(F32) + next_y[...].astype(F32)).astype(BF16)
        along_y[:, :half] = (far[:, :half].astype(F32) + next_x[...].astype(F32)).astype(BF16)
        along_y[:, half:] = far[:, half:]

    out_shape = [jax.ShapeDtypeStruct((rows, cols), BF16 if j else F32) for j in range(4)]
    out_shape += [jax.ShapeDtypeStruct(own[0].shape, BF16)] * 2
    args = (tie(done.own[1], *after), done.from_x, done.from_y, going.other[2], own[0], *going.sent_far)
    outs = call(kernel, "relay", [VMEM] * 7, tuple(out_shape), [], 0.01, *args, near=True)
    going.own, going.ready, done.ready = own, outs[4:], outs[:4]
    done.parts = (outs[0], *(swap(outs[j], "fsdp", 2 * j) for j in (1, 2, 3)))
    going.from_x, going.from_y = swap(outs[4], "tx", 1), swap(outs[5], "fsdp", 1)


class ReductionFirstZ:
    def __init__(self, squares):
        self.whole = lax.axis_size("fsdp") != 8
        self.squares = squares

    def send_z(self, *after):
        if self.whole:
            total = self.squares[0] + swap(tie(self.squares, *after)[1], "tx", 1)
            self.from_z = (lax.psum_scatter(total, "fsdp", scatter_dimension=0, tiled=True),)
            return
        squares = tie(self.squares, *after)
        self.from_z = tuple(swap(squares[j], "fsdp", 2 * j) for j in (1, 2, 3))

    def sum_z(self, *after):
        self.square = (self.squares,)
        if not self.whole:
            self.square = sum_squares(tie(self.squares, *after), self.from_z)

    def send_y(self, *after):
        if self.whole:
            self.from_y = self.from_z[0]
            return
        self.from_y = swap(tie(self.square[1], *after), "fsdp", 1)

    def send_x(self, *after):
        if self.whole:
            self.from_x = self.from_z[0]
            return
        self.pair = add(self.square[0], tie(self.from_y, *after))
        self.from_x = swap(self.pair[1], "tx", 1)

    def total(self):
        if self.whole:
            return self.from_x.astype(F32)
        return self.pair[0].astype(F32) + self.from_x.astype(F32)


def add(a, b):
    return (a.astype(F32) + b.astype(F32)).astype(BF16)


def sum_squares(squares, from_z):
    def kernel(squares, *refs):
        *from_z, near, far = refs
        for n, out in enumerate((near, far)):
            for r in range(2):
                total = squares[0, 2 * n + r].astype(F32)
                for piece in from_z:
                    total = total + piece[2 * n + r].astype(F32)
                out[r] = total.astype(BF16)

    out_shape = (jax.ShapeDtypeStruct((2, *squares.shape[2:]), BF16),) * 2
    return call(kernel, "sum_squares", [VMEM] * 4, out_shape, [], 0.01, squares, *from_z)


def sum_pieces(near, from_x, from_y):
    def kernel(near, from_x, from_y, *outs):
        for j, out in enumerate(outs):
            total = near[j].astype(F32) + from_x[j].astype(F32) + from_y[j].astype(F32)
            out[...] = total.astype(out.dtype)

    _, rows, cols = near.shape
    out_shape = tuple(jax.ShapeDtypeStruct((rows, cols), BF16 if j else F32) for j in range(4))
    return call(kernel, "sum_pieces", [VMEM] * 3, out_shape, [], 0.01, near, from_x, from_y)


def add_halves(near, far, sent_far, after):
    def kernel(near, far, from_x, from_y, along_x, along_y):
        half = near.shape[1] // 2
        along_x[:, :half] = near[:, :half]
        along_x[:, half:] = (near[:, half:].astype(F32) + from_y[...].astype(F32)).astype(BF16)
        along_y[:, :half] = (far[:, :half].astype(F32) + from_x[...].astype(F32)).astype(BF16)
        along_y[:, half:] = far[:, half:]

    out_shape = (jax.ShapeDtypeStruct(near.shape, BF16), jax.ShapeDtypeStruct(far.shape, BF16))
    return call(kernel, "add_halves", [VMEM] * 4, out_shape, [], 0.01, tie(near, *after), far, *sent_far, near=True)


VMEM = pl.BlockSpec(memory_space=pltpu.VMEM)
ANY = pl.BlockSpec(memory_space=pl.ANY)
SMEM = pl.BlockSpec(memory_space=pltpu.SMEM)


def call(kernel, name, in_specs, out_shape, scratch_shapes, micros, *args, near=False, away=(), away_out=(), by_hand=True):
    out_specs = jax.tree.map(lambda _: VMEM, out_shape)
    if near:
        spaces = [pltpu.HBM if n in away or s is ANY else pltpu.VMEM for n, s in enumerate(in_specs)]
        args = [
            a if s is SMEM else pltpu.with_memory_space_constraint(a, space)
            for a, s, space in zip(args, in_specs, spaces)
        ]
        out_shape = jax.tree.map(lambda o: pltpu.VMEM(o.shape, o.dtype), out_shape)
        if away_out:
            out_shape = [pltpu.HBM(o.shape, o.dtype) if n in away_out else o for n, o in enumerate(out_shape)]
            out_specs = [ANY if n in away_out and by_hand else VMEM for n in range(len(out_shape))]
    return pl.pallas_call(
        kernel,
        in_specs=in_specs,
        out_specs=out_specs,
        out_shape=out_shape,
        scratch_shapes=scratch_shapes,
        compiler_params=pltpu.CompilerParams(vmem_limit_bytes=VMEM_BYTES),
        cost_estimate=pl.CostEstimate(flops=int(micros * 1e9), bytes_accessed=1 << 10, transcendentals=0),
        name=name,
    )(*args)


def place_pieces(refs, entries, weight, rank, cols=slice(None), width=None, first_col=0):
    if len(refs) == 1 and not entries[0]:
        weight[:, first_col : first_col + width] = refs[0][:, cols]
        return
    shard = weight.shape[0] // 8
    for ref, places in zip(refs, entries):
        for index, j, first in places:
            piece = ref[(*index, slice(None), cols)]
            start = pl.multiple_of((rank ^ j) * shard + first, 16)
            weight[pl.ds(start, piece.shape[0]), first_col : first_col + width] = piece


def far_shapes(depth, cols, size, own, parts=1):
    if size != 8:
        return (jax.ShapeDtypeStruct((depth, cols // parts), BF16),) * parts
    rows = depth // 8
    near = (jax.ShapeDtypeStruct((4, rows, cols // parts), BF16),) * parts
    if own:
        return (*near, *near)
    lead = (parts,) if parts > 1 else ()
    return (jax.ShapeDtypeStruct((*lead, 4, rows // 2, cols // parts), BF16),) * 2 + near


def put_pieces(refs, block, start, rank, own, part=None):
    if len(refs[0].shape) == 2:
        refs[part or 0][start : start + block.shape[0], :] = block
        return
    near = refs[len(refs) // 2 + (part or 0)] if own else refs[2 + (part or 0)]
    rows = near.shape[1]
    for n in range(block.shape[0] // rows):
        j = (start // rows + n) ^ rank
        yj, zj = j & 1, j >> 1
        piece = block[n * rows : (n + 1) * rows]

        @pl.when(yj == 0)
        def _():
            near[zj] = piece

        @pl.when(yj == 1)
        def _():
            if own:
                refs[part or 0][zj] = piece
            elif part is None:
                refs[0][zj] = piece[: rows // 2]
                refs[1][zj] = piece[rows // 2 :]
            else:
                refs[0][part, zj] = piece[: rows // 2]
                refs[1][part, zj] = piece[rows // 2 :]


def assemble(place, gathers, depth, width):
    lists = [pieces for g in gathers for pieces in (g.own, g.other)]
    entries = [[p[1] for p in pieces] for pieces in lists]
    arrays = [p[0] for pieces in lists for p in pieces]
    counts = [pieces[0][0].shape[-1] for pieces in lists[::2]]
    parts = sum(counts) // width

    def kernel(place, *refs):
        pieces, outs = refs[: len(arrays)], refs[len(arrays) :]
        at, first = 0, 0
        for n, places in enumerate(entries):
            refs_n = pieces[at : at + len(places)]
            at += len(places)
            for i in range(counts[n // 2] // width):
                cols = slice(i * width, (i + 1) * width)
                place_pieces(refs_n, places, outs[first + i], place[1], cols, width, n % 2 * width)
            if n % 2:
                first += counts[n // 2] // width

    out_shape = tuple(jax.ShapeDtypeStruct((depth, 2 * width), BF16) for _ in range(parts))
    return call(kernel, "assemble", [SMEM] + [VMEM] * len(arrays), out_shape, [], 3, place, *arrays, near=True)


def pack_qkv(weights, vectors, chunks):
    _, shard, width = weights.shape
    part = width // chunks
    first = shard // 2
    cols = -(-(3 * width + 8) // 128) * 128

    def kernel(weights, vectors, *outs):
        blocks = [weights[i, :, c * part : (c + 1) * part] for c in range(chunks) for i in range(3)]
        blocks += [vectors[...].T, jnp.zeros((shard, cols - 3 * width - 8), F32)]
        packed = jnp.concatenate(blocks, axis=1).astype(BF16)
        outs[0][...] = packed[:first]
        outs[1][...] = packed[first:]

    out_shape = (jax.ShapeDtypeStruct((first, cols), BF16), jax.ShapeDtypeStruct((shard - first, cols), BF16))
    return call(kernel, "pack_qkv", [VMEM] * 2, out_shape, [], 1, weights, vectors)


BIAS_ROWS = sum((i + 1) * BQ for i in range(LEN // BQ))


def bias_rows(i):
    start = i * (i + 1) // 2 * BQ
    return slice(start, start + (i + 1) * BQ)


def mask_bias(doc_col, doc_row, bias):
    for i in range(LEN // BQ):
        lo, hi = i * BQ, (i + 1) * BQ
        same = doc_col[:hi, :] == doc_row[:, lo:hi]
        keys = lax.broadcasted_iota(jnp.int32, (hi, BQ), 0)
        queries = lax.broadcasted_iota(jnp.int32, (hi, BQ), 1) + lo
        bias[bias_rows(i), :] = jnp.where(same & (keys <= queries), 0.0, NEG_FILL)


def outer_rows(lo, rows, core):
    half = LEN // 2
    return pl.ds(pl.multiple_of(((lo // half) ^ core) * half + lo % half, rows), rows)


def head_rows(ref, block, columns, rows):
    for h in range(ref.shape[0]):
        ref[h, rows, :] = block[:, columns[h] : columns[h] + HD].astype(ref.dtype)


def join_heads(ref, heads):
    return jnp.concatenate([ref[h] for h in heads], axis=1)


def attn_forward(place, pieces, rows_in, scale, doc_col, doc_row, chunks, depth):
    arrays, places = [p[0] for p in pieces], [p[1] for p in pieces]
    cols = arrays[0].shape[-1]
    fresh = len(rows_in) == 2
    part = scale.shape[1] // 3
    per_chunk = part // HD
    heads = per_chunk * chunks
    starts = [[c * 3 * part + n * part + h * HD for c in range(chunks) for h in range(per_chunk)] for n in range(3)]

    def kernel(place, *refs):
        pieces, refs = refs[: len(arrays)], refs[len(arrays) :]
        sources, (scale, doc_col, doc_row) = refs[: len(rows_in)], refs[len(rows_in) : len(rows_in) + 3]
        outs = refs[len(rows_in) + 3 :]
        attns, (*away, lse) = outs[:chunks], outs[chunks : chunks + 5]
        if fresh:
            x, gains, *outs = outs[chunks + 5 :]
        else:
            x, outs = sources[0], outs[chunks + 5 :]
        bias, out_heads, query, key, value, weight, sems = outs
        copies = [
            pltpu.make_async_copy(source, target, sems.at[n])
            for n, (source, target) in enumerate(zip((query, key, value, weight), away))
        ]
        core, rank = place[0], place[1]
        half = LEN // 2
        place_pieces(pieces, places, weight, rank, slice(None), cols)
        mask_bias(doc_col, doc_row, bias)
        if fresh:
            gains[...] = weight[:, cols - 128 :].astype(F32).T
            gain = gains[64:65, :]
            for n, source in enumerate(sources):

                def norm(i, _, source=source, n=n):
                    block = pl.ds(pl.multiple_of(i * 128, 128), 128)
                    values = source[block, :].astype(F32)
                    target = pl.ds(pl.multiple_of(i * 128 + n * half, 128), 128)
                    x[target, :] = (values * rms_scale(values) * gain).astype(BF16)
                    return 0

                lax.fori_loop(0, half // 128, norm, 0)

        def project(i, _):
            lo = i * BQ
            block = dot(x[outer_rows(lo, BQ, core), :], weight[...])
            rows = pl.ds(pl.multiple_of(lo, BQ), BQ)
            scaled = jnp.concatenate(
                [block[:, c * 3 * part : c * 3 * part + part] * scale[:, :part] for c in range(chunks)], axis=1
            )
            head_rows(query, scaled, [h * HD for h in range(heads)], rows)
            head_rows(key, block, starts[1], rows)
            head_rows(value, block, starts[2], rows)
            return 0

        lax.fori_loop(0, LEN // BQ, project, 0)
        for copy in copies:
            copy.start()

        def attend(h, _):
            keys = key[h]
            value_t = value[h].T
            blocks = []
            for i in range(LEN // BQ):
                lo, hi = i * BQ, (i + 1) * BQ
                scores = dot(keys[:hi], query[h, lo:hi, :], NT) + bias[bias_rows(i), :]
                top = jnp.max(scores, axis=0, keepdims=True)
                probs = jnp.exp(scores - top)
                total = jnp.sum(probs, axis=0, keepdims=True)
                blocks.append(dot(value_t[:, :hi], probs.astype(BF16)) / total)
                lse[h, :, lo:hi] = top + jnp.log(total)
            out_heads[h] = jnp.concatenate(blocks, axis=1).T.astype(BF16)
            return 0

        def attend_two(n, _):
            attend(2 * n, 0)
            return attend(2 * n + 1, 0)

        lax.fori_loop(0, heads // 2, attend_two, 0)
        for c in range(chunks):
            joined = join_heads(out_heads, range(c * per_chunk, (c + 1) * per_chunk))
            for a in range(2):
                attns[c][outer_rows(a * half, half, core), :] = joined[a * half : (a + 1) * half]
        for copy in copies:
            copy.wait()

    per_head = jax.ShapeDtypeStruct((heads, LEN, HD), BF16)
    out_shape = (
        *(jax.ShapeDtypeStruct((LEN, part), BF16),) * chunks,
        per_head,
        per_head,
        per_head,
        jax.ShapeDtypeStruct((depth, cols), BF16),
        jax.ShapeDtypeStruct((heads, 1, LEN), F32),
    )
    scratch = [pltpu.VMEM((BIAS_ROWS, BQ), F32)] + [pltpu.VMEM((heads, LEN, HD), BF16)] * 4
    scratch += [pltpu.VMEM((depth, cols), BF16), pltpu.SemaphoreType.DMA((4,))]
    if fresh:
        out_shape += (jax.ShapeDtypeStruct((LEN, depth), BF16), jax.ShapeDtypeStruct((128, depth), F32))
    specs = [SMEM] + [VMEM] * (len(arrays) + len(rows_in) + 3)
    args = (place, *arrays, *rows_in, scale, doc_col, doc_row)
    outs = call(
        kernel, "attn_forward", specs, out_shape, scratch, 8, *args, near=True, away_out=range(chunks, chunks + 4)
    )
    saved = (*outs[chunks : chunks + 3], outs[chunks + 4])
    return outs[:chunks], saved, (outs[chunks + 3], *outs[chunks + 5 :])


SIDE = 32
SCALE_COLUMN = 4


def attn_backward(place, attns, saved, dout, x, doc_col, doc_row, scale, first, own, riders, other_sums):
    part = attns[0].shape[1]
    per_chunk = part // HD
    count = len(attns)
    heads = per_chunk * count
    depth = x.shape[1]
    size = lax.axis_size("fsdp")
    pieces_shape = far_shapes(depth, (3 * part + SIDE) * count, size, own, count)

    def kernel(place, *refs):
        attns, refs = refs[:count], refs[count:]
        *saved, lse, dout, x, doc_col, doc_row, scale, other_sums = refs[:10]
        riders, refs = refs[10 : 10 + len(riders_in)], refs[10 + len(riders_in) :]
        grads_out, sums_out, refs = refs[:count], refs[count], refs[count + 1 :]
        pieces, refs = refs[:-10], refs[-10:]
        dkey, dvalue, bias, douts, deltas, grads, query, key, value, sems = refs

        def copies(n):
            pair = pl.ds(2 * n, 2)
            return [
                pltpu.make_async_copy(source.at[pair], target.at[pair], sems.at[n, k])
                for k, (source, target) in enumerate(zip(saved, (query, key, value)))
            ]

        for n in range(heads // 2):
            for copy in copies(n):
                copy.start()
        core, rank = place[0], place[1]
        half = LEN // 2
        lanes = lax.broadcasted_iota(jnp.int32, (8, part), 1) // HD
        selector = jnp.where(lanes == lax.broadcasted_iota(jnp.int32, (8, part), 0), 1.0, 0.0)
        mask_bias(doc_col, doc_row, bias)
        for c in range(count):
            for i in range(LEN // BQ):
                lo, hi = i * BQ, (i + 1) * BQ
                rows = outer_rows(lo, BQ, core)
                dout_block = dout[rows, first + c * part : first + (c + 1) * part]
                products = attns[c][rows, :].astype(F32) * dout_block.astype(F32)
                delta = lax.dot_general(
                    selector, products, NT, precision=lax.Precision.HIGHEST, preferred_element_type=F32
                )
                for h in range(per_chunk):
                    deltas[c * per_chunk + h, :, lo:hi] = delta[h : h + 1, :]
                    douts[c * per_chunk + h, lo:hi, :] = dout_block[:, h * HD : (h + 1) * HD]

        def attend(h, sums):
            keys = key[h]
            key_t = keys.T
            dquery_parts = []
            for i in range(LEN // BQ):
                lo, hi = i * BQ, (i + 1) * BQ
                queries = query[h, lo:hi, :]
                dout_head = douts[h, lo:hi, :]
                scores = dot(keys[:hi], queries, NT) + bias[bias_rows(i), :]
                probs = jnp.exp(scores - lse[h, :, lo:hi])
                dprobs = dot(value[h, :hi, :], dout_head, NT)
                dscores = (probs * (dprobs - deltas[h, :, lo:hi])).astype(BF16)
                dv = dot(probs.astype(BF16), dout_head)
                dk = dot(dscores, queries)
                dquery_parts.append(dot(key_t[:, :hi], dscores))
                if i:
                    dkey[:lo] += dk[:lo]
                    dvalue[:lo] += dv[:lo]
                dkey[lo:hi] = dk[lo:]
                dvalue[lo:hi] = dv[lo:]
            dquery = jnp.concatenate(dquery_parts, axis=1).T
            grads[0, h] = (dquery * scale[...]).astype(BF16)
            grads[1, h] = dkey[...].astype(BF16)
            grads[2, h] = dvalue[...].astype(BF16)
            return sums + jnp.sum(dquery * query[h].astype(F32), axis=0, keepdims=True)

        def attend_two(n, sums):
            for copy in copies(n):
                copy.wait()
            return attend(2 * n + 1, attend(2 * n, sums))

        sums = lax.fori_loop(0, heads // 2, attend_two, jnp.zeros((1, HD), F32))
        sums = sums / scale[...]
        sums_out[...] = sums
        side = [jnp.zeros((depth, SIDE), BF16)] * count
        if size == 8:
            units = riders[0][:, 0 if own else units_width : units_width if own else 2 * units_width]
            units = [units[:, n * (depth // size) : (n + 1) * (depth // size)] for n in range(2)]
            nothing = jnp.zeros((1, depth), F32)
            rows = [r[...] for r in riders[1:]] if own else [nothing] * 2
            rows += [jnp.concatenate([u] * size, axis=1) for u in units] + [nothing] * 4
            columns = jnp.concatenate(rows).T
            if own:
                scales = jnp.broadcast_to(sums + other_sums[...], (128, HD)).T[:, :8]
                block = jnp.concatenate([scales, jnp.zeros((depth // size - HD, 8), F32)])
                column = lax.broadcasted_iota(jnp.int32, (depth, 8), 1) == SCALE_COLUMN
                columns = jnp.where(column, jnp.concatenate([block] * size), columns)
            side[-1] = jnp.concatenate([columns, jnp.zeros((depth, SIDE - 8), F32)], axis=1).astype(BF16)
        for c in range(count):
            mine = range(c * per_chunk, (c + 1) * per_chunk)
            joined = jnp.concatenate([grads[n, h] for n in range(3) for h in mine], axis=1)
            for a in range(2):
                grads_out[c][outer_rows(a * half, half, core), :] = joined[a * half : (a + 1) * half]
            for g in range(2):
                start = g * depth // 2
                block = dot(x[:, start : start + depth // 2], grads_out[c][...], TN).astype(BF16)
                block = jnp.concatenate([block, side[c][start : start + depth // 2]], axis=1)
                put_pieces(pieces, block, start, rank, own, c if count > 1 else None)

    out_shape = (
        *(jax.ShapeDtypeStruct((LEN, 3 * part), BF16),) * count,
        jax.ShapeDtypeStruct((1, HD), F32),
        *pieces_shape,
    )
    scratch = [
        pltpu.VMEM((LEN, HD), F32),
        pltpu.VMEM((LEN, HD), F32),
        pltpu.VMEM((BIAS_ROWS, BQ), F32),
        pltpu.VMEM((heads, LEN, HD), BF16),
        pltpu.VMEM((heads, 1, LEN), F32),
        pltpu.VMEM((3, heads, LEN, HD), BF16),
        *(pltpu.VMEM((heads, LEN, HD), BF16),) * 3,
        pltpu.SemaphoreType.DMA((heads // 2, 3)),
    ]
    riders_in = riders
    units_width = riders[0].shape[1] // 2
    args = (place, *attns, *saved, dout, x, doc_col, doc_row, scale, other_sums, *riders)
    specs = [SMEM] + [VMEM] * count + [ANY] * 3 + [VMEM] * (len(args) - 4 - count)
    outs = call(kernel, "attn_backward", specs, out_shape, scratch, 10, *args, near=True)
    return outs[:count], outs[count], outs[count + 1 :]


def put_both(outs, block, start, rank, size):
    width = block.shape[1] // 2
    count = len(outs) // 2 if size != 8 else 2
    put_pieces(outs[:count], block[:, :width], start, rank, True)
    put_pieces(outs[count:], block[:, width:], start, rank, False)


def weight_grads(place, pairs, name):
    rows, depth = pairs[0][0][0].shape
    width = pairs[0][1].shape[1] // 2
    size = lax.axis_size("fsdp")
    shapes = [far_shapes(depth, width * len(pairs), size, own) for own in (True, False)]

    def kernel(place, *refs):
        ins, outs = refs[: 3 * len(pairs)], refs[3 * len(pairs) :]
        for g in range(2):
            cols = slice(g * depth // 2, (g + 1) * depth // 2)
            blocks = []
            for n in range(len(pairs)):
                near, far, right = ins[3 * n : 3 * n + 3]
                block = dot(near[:, cols], right[:rows, :], TN) + dot(far[:, cols], right[rows:, :], TN)
                blocks.append(block.astype(BF16))
            joined = [b[:, r * width : (r + 1) * width] for r in range(2) for b in blocks]
            put_both(outs, jnp.concatenate(joined, axis=1), g * depth // 2, place[1], size)

    args = [a for halves, right in pairs for a in (*halves, right)]
    outs = call(
        kernel, name, [SMEM] + [VMEM] * len(args), (*shapes[0], *shapes[1]), [], 4 * len(pairs), place, *args, near=True
    )
    return outs[: len(shapes[0])], outs[len(shapes[0]) :]


def out_forward(attns, out_t, inputs):
    rows, depth = inputs.shape

    def kernel(*refs):
        attns, (out_t, inputs, sent, kept) = refs[:-4], refs[-4:]
        heads = jnp.concatenate([a[...] for a in attns], axis=1)
        for i in range(rows // BQ):
            lo, hi = i * BQ, (i + 1) * BQ
            sent[lo:hi, :] = dot(heads[rows + lo : rows + hi], out_t[...], NT).astype(BF16)
            kept[lo:hi, :] = inputs[lo:hi, :].astype(F32) + dot(heads[lo:hi], out_t[...], NT)

    out_shape = (jax.ShapeDtypeStruct((rows, depth), BF16), jax.ShapeDtypeStruct((rows, depth), F32))
    return call(kernel, "out_forward", [VMEM] * (len(attns) + 2), out_shape, [], 3, *attns, out_t, inputs, near=True)


def second_norm(kept, received, gain):
    def kernel(kept, received, gain, resid_out, normed_out):
        resid = kept[...] + received[...].astype(F32)
        resid_out[...] = resid
        normed_out[...] = (resid * rms_scale(resid) * gain[...]).astype(BF16)

    out_shape = (jax.ShapeDtypeStruct(kept.shape, F32), jax.ShapeDtypeStruct(kept.shape, BF16))
    return call(kernel, "second_norm", [VMEM] * 3, out_shape, [], 1, kept, received, gain, near=True)


def mlp(normed, cot, up, down_t, bias_up):
    rows, depth = normed[0].shape
    units = up.shape[1]

    def kernel(n_near, n_far, c_near, c_far, up, down_t, bias, hidden, grad_pre, bias_sum, *outs):
        sums = jnp.zeros((1, units), F32)
        for side, (n, c) in enumerate(((n_near, c_near), (n_far, c_far))):
            out_mlp, out_grad = outs[2 * side : 2 * side + 2]

            def step(i, sums, n=n, c=c, side=side, out_mlp=out_mlp, out_grad=out_grad):
                block = pl.ds(pl.multiple_of(i * BQ, BQ), BQ)
                target = pl.ds(pl.multiple_of(i * BQ + side * rows, BQ), BQ)
                pre = dot(n[block, :], up[...]) + bias[...]
                sig = 1.0 / (1.0 + jnp.exp(-pre))
                units_low = (pre * sig).astype(BF16)
                grad = dot(c[block, :], down_t[...])
                grad_low = (grad * (sig + pre * sig * (1.0 - sig))).astype(BF16)
                hidden[target, :] = units_low
                grad_pre[target, :] = grad_low
                out_mlp[block, :] = dot(units_low, down_t[...], NT).astype(BF16)
                out_grad[block, :] = dot(grad_low, up[...], NT).astype(BF16)
                return sums + jnp.sum(grad_low.astype(F32), axis=0, keepdims=True)

            sums = lax.fori_loop(0, rows // BQ, step, sums)
        bias_sum[...] = sums

    low = jax.ShapeDtypeStruct((rows, depth), BF16)
    out_shape = (
        jax.ShapeDtypeStruct((2 * rows, units), BF16),
        jax.ShapeDtypeStruct((2 * rows, units), BF16),
        jax.ShapeDtypeStruct((1, units), F32),
        low,
        low,
        low,
        low,
    )
    return call(kernel, "mlp", [VMEM] * 7, out_shape, [], 10, *normed, *cot, up, down_t, bias_up, near=True)


def resid_grads(grads, mlps, resid, cot, gain, bias):
    def kernel(grad_near, grad_far, mlp_near, mlp_far, resid, cot, gain, bias, low_out, sum_out, layer):
        for i in range(resid.shape[0] // BQ):
            block = slice(i * BQ, (i + 1) * BQ)
            held = resid[block, :]
            grad = grad_near[block, :].astype(F32) + grad_far[block, :].astype(F32)
            recip = rms_scale(held)
            unit = held * recip
            part = jnp.sum(grad * unit, axis=0, keepdims=True)
            sum_out[...] = part if i == 0 else sum_out[...] + part
            scaled = grad * gain[...]
            mean = jnp.mean(scaled * unit, axis=-1, keepdims=True)
            total = cot[block, :].astype(F32) + recip * (scaled - unit * mean)
            low_out[block, :] = total.astype(BF16)
            mlp = mlp_near[block, :].astype(F32) + mlp_far[block, :].astype(F32)
            layer[block, :] = (held + mlp + bias[...]).astype(BF16)

    out_shape = (
        jax.ShapeDtypeStruct(resid.shape, BF16),
        jax.ShapeDtypeStruct((1, resid.shape[1]), F32),
        jax.ShapeDtypeStruct(resid.shape, BF16),
    )
    args = (*grads, *mlps, resid, cot, gain, bias)
    return call(kernel, "resid_grads", [VMEM] * 8, out_shape, [], 2, *args, near=True)


def head_grads(place, grads, out_t, attns):
    rows, depth = grads[0].shape
    width = out_t.shape[1] // 2
    size = lax.axis_size("fsdp")
    shard = depth // size

    def kernel(place, near, far, out_t, *refs):
        attns, (heads_out, squares) = refs[:-2], refs[-2:]
        for i in range(2 * rows // BQ):
            source = near if i < rows // BQ else far
            block = slice(i * BQ % rows, i * BQ % rows + BQ)
            heads_out[i * BQ : (i + 1) * BQ, :] = dot(source[block, :], out_t[...]).astype(BF16)
        heads = jnp.concatenate([a[...] for a in attns], axis=1)
        for g in range(2):
            start = g * depth // 2
            cols = slice(start, start + depth // 2)
            block = (dot(near[:, cols], heads[:rows], TN) + dot(far[:, cols], heads[rows:], TN)).astype(BF16)
            for r in range(2):
                side = block[:, r * width : (r + 1) * width]
                if size != 8:
                    squares[r, start : start + depth // 2, :] = side
                    continue
                for n in range(side.shape[0] // shard):
                    j = (start // shard + n) ^ place[1]
                    squares[j >> 1, 2 * (j & 1) + r] = side[n * shard : (n + 1) * shard]

    squares_shape = (4, 4, shard, width) if size == 8 else (2, depth, width)
    out_shape = (jax.ShapeDtypeStruct((2 * rows, 2 * width), BF16), jax.ShapeDtypeStruct(squares_shape, BF16))
    args = (place, *grads, out_t, *attns)
    specs = [SMEM] + [VMEM] * (len(args) - 1)
    return call(kernel, "head_grads", specs, out_shape, [], 6, *args, near=True, away=range(3, len(args)))


def input_grads(grads, weights, rows):
    depth = weights[0].shape[0]
    counts = [len(g) for g in grads]

    def kernel(*refs):
        ins, weights, (sent, kept) = refs[: sum(counts)], refs[sum(counts) : -2], refs[-2:]
        for side, out in enumerate((kept, sent)):

            def step(i, _, side=side, out=out):
                total, at = None, 0
                block = pl.ds(pl.multiple_of(i * BQ + side * rows, BQ), BQ)
                for count, weight in zip(counts, weights):
                    left = jnp.concatenate([g[block, :] for g in ins[at : at + count]], axis=1)
                    at += count
                    partial = dot(left, weight[:, : left.shape[1]], NT)
                    total = partial if total is None else total + partial
                out[pl.ds(pl.multiple_of(i * BQ, BQ), BQ), :] = total.astype(BF16)
                return 0

            lax.fori_loop(0, rows // BQ, step, 0)

    out_shape = (jax.ShapeDtypeStruct((rows, depth), BF16),) * 2
    flat = [g for pair in grads for g in pair]
    return call(
        kernel, "input_grads", [VMEM] * (len(flat) + len(weights)), out_shape, [], 10, *flat, *weights, near=True
    )


def first_norm_grads(kept, received, inputs, resid_grad, gain):
    def kernel(kept, received, inputs, resid_grad, gain, grad_out):
        for i in range(inputs.shape[0] // BQ):
            block = slice(i * BQ, (i + 1) * BQ)
            values = inputs[block, :].astype(F32)
            recip = rms_scale(values)
            unit = values * recip
            scaled = (kept[block, :].astype(F32) + received[block, :].astype(F32)) * gain[...]
            mean = jnp.mean(scaled * unit, axis=-1, keepdims=True)
            grad_out[block, :] = (resid_grad[block, :].astype(F32) + recip * (scaled - unit * mean)).astype(BF16)

    out_shape = jax.ShapeDtypeStruct(inputs.shape, BF16)
    args = (kept, received, inputs, resid_grad, gain)
    return call(kernel, "first_norm_grads", [VMEM] * 5, out_shape, [], 0.01, *args)


def join_chunks(parts, weights, factors):
    counts = [len(p) for p in parts]
    _, shard, width = weights.shape
    part = width // len(parts)

    def kernel(*refs):
        *refs, weights, factors, out, rows = refs
        at = 0
        sums = []
        for count in counts:
            sums.append(sum(ref[...].astype(F32) for ref in refs[at : at + count]))
            at += count
        total = jnp.zeros((shard, 1), F32)
        for i in range(3):
            joined = jnp.concatenate([s[:, i * part : (i + 1) * part] for s in sums], axis=1)
            out[i] = joined
            total = total + jnp.sum(joined * weights[i].astype(BF16).astype(F32), axis=1, keepdims=True)
        side = jnp.concatenate([sums[-1][:, 3 * part : 3 * part + SIDE], jnp.zeros((shard, 128 - SIDE), F32)], axis=1)
        lane = lax.broadcasted_iota(jnp.int32, (shard, 128), 1)
        rows[...] = jnp.where(lane == SCALE_COLUMN + 1, total, side).T[:8, :] * factors[...]

    flat = [p for pieces in parts for p in pieces]
    out_shape = (jax.ShapeDtypeStruct((3, shard, width), F32), jax.ShapeDtypeStruct((8, shard), F32))
    return call(kernel, "join_chunks", [VMEM] * (len(flat) + 2), out_shape, [], 1, *flat, weights, factors)


def local(
    inputs,
    doc_ids,
    w_qkv,
    w_out,
    w_up,
    up_bias,
    w_down,
    down_bias,
    attn_gain,
    mlp_gain,
    dim_scale,
    cotangent,
):
    shard, _, width = w_qkv.shape
    size = lax.axis_size("fsdp")
    depth = shard * size
    rows = inputs.shape[0]
    core, tx, rank = lax.axis_index("core"), lax.axis_index("tx"), lax.axis_index("fsdp")
    place = jnp.stack([core, rank]).astype(jnp.int32)

    chunks = 2
    heads = width // HD
    part = width // chunks
    vectors = jnp.concatenate([jnp.stack([attn_gain, mlp_gain, down_bias]), jnp.zeros((5, shard), F32)])
    qkv = HalvesGather(pack_qkv(jnp.transpose(w_qkv, (1, 0, 2)), vectors, chunks))
    rest = Gather(jnp.concatenate([w_out.T, w_up, w_down.T], axis=1).astype(BF16))
    qkv.start(0)

    input_rows = (inputs, swap(inputs, "core", 1))
    cots = (cotangent, swap(cotangent, "core", 1))
    docs = lax.dynamic_slice_in_dim(doc_ids, tx * LEN, LEN, 0)
    doc_col, doc_row = docs[:, None], docs[None, :]
    scale_base = PERDIM_BASE / math.sqrt(HD)
    query_scale = scale_base * jax.nn.softplus(dim_scale)
    colscale = jnp.concatenate([jnp.tile(query_scale, heads // chunks), jnp.ones((2 * part,), F32)])[None]

    scale_factor = scale_base * jax.nn.sigmoid(dim_scale)
    factors = jnp.ones((8, shard), F32).at[SCALE_COLUMN + 1].set(1.0 / attn_gain.astype(BF16).astype(F32))
    if size == 8:
        factors = factors.at[SCALE_COLUMN, :HD].set(scale_factor)
    downbias_sum = jnp.sum(cotangent.astype(F32), axis=0)[None]

    bias_far = swap(tie(up_bias, input_rows[1], cots[1]), "tx", 1)
    now = (*qkv.along_z[0], input_rows[1], cots[1], bias_far)
    qkv.middle(0, *now)
    qkv.start(1, *now)
    now = (*qkv.along_xy[0], *qkv.along_z[1])
    qkv.middle(1, *now)
    rest.start(*now)
    now = qkv.along_xy[1]
    qkv.finish(*now)
    own_attns, own_saved, (weight_own, normed_first, gains) = attn_forward(
        place, qkv.own, (tie(inputs, *now), input_rows[1]), colscale, doc_col, doc_row, chunks, depth
    )
    now = (own_saved[3], *rest.along_z, *qkv.last)
    out_columns, mlp_columns = Columns(rest, slice(0, 2 * width)), Columns(rest, slice(2 * width, 3 * width))
    out_columns.middle(*now)
    mlp_columns.middle(*now, *out_columns.ready)
    other_attns, other_saved, (weight_other,) = attn_forward(
        place, qkv.other, (tie(normed_first, *now, *mlp_columns.ready),), colscale, doc_col, doc_row, chunks, depth
    )
    now = (other_saved[3], *out_columns.along_xy)
    out_columns.finish(*now)
    mlp_columns.finish(*now, *mlp_columns.along_xy)
    bias_up = jnp.concatenate([up_bias, bias_far])[None]
    attns = [*own_attns, *other_attns]
    gain_first, gain_second, bias_second = [gains[64 + i : 65 + i] for i in range(3)]
    if size == 8:
        out_columns.other[-1] = (tie(out_columns.other[-1][0], *mlp_columns.along_xy), out_columns.other[-1][1])
    out_t, up = assemble(place, (out_columns,), depth, width)
    sent, kept = out_forward([tie(attns[0], downbias_sum, factors), *attns[1:]], out_t, inputs)
    sent = tie(sent, *mlp_columns.last)
    resid_first, normed_own = second_norm(kept, swap(sent, "core", 1), gain_second)
    normeds = (normed_own, swap(normed_own, "core", 1))
    (down_t,) = assemble(place, (mlp_columns,), depth, width)
    hidden, grad_pre, upbias_sum, mlp_kept, grad_kept, mlp_sent, grad_sent = mlp(normeds, cots, up, down_t, bias_up)
    grads = (grad_kept, swap(grad_sent, "core", 1))
    mlps = (mlp_kept, swap(mlp_sent, "core", 1))
    updown_own, updown_other = weight_grads(place, [(normeds, grad_pre), (cots, hidden)], "updown_grads")
    updown, both = Reduction(), Reduction()
    now = (updown_own[-1], grads[1], mlps[1])
    updown.send_far([tie(p, *now) for p in updown_other[:2]] + list(updown_other[2:]))
    grad_own, mlpgain_sum, layer_out = resid_grads(
        (tie(grad_kept, *now), grads[1]), mlps, resid_first, cotangent, gain_second, bias_second
    )
    grad_attn = (grad_own, swap(grad_own, "core", 1))
    grad_heads, out_grads = head_grads(place, grad_attn, out_t, attns)
    out = ReductionFirstZ(out_grads)
    out.send_z(grad_heads)
    now = (grad_heads, *updown.sent_far)
    updown.send_xy(updown_own, *now)

    def back(attns, saved, first_col, own, riders, other_sums, *now):
        dout = tie(grad_heads, *now)
        return attn_backward(
            place, attns, saved, dout, normed_first, doc_col, doc_row, query_scale[None], first_col, own, riders, other_sums
        )

    grad_other, sums_other, pieces_other = back(
        other_attns, other_saved, width, False, (upbias_sum,), query_scale[None], *now, *updown.ready
    )
    now = (sums_other, updown.from_x, updown.from_y)
    both.send_far([tie(p, *now) for p in pieces_other[:2]] + list(pieces_other[2:]))
    grad_first, sums_first, pieces_first = back(
        own_attns, own_saved, 0, True, (upbias_sum, mlpgain_sum, downbias_sum), sums_other, *now
    )
    now = (sums_first, *both.sent_far, *out.from_z)
    first, second = both.split(chunks)
    near_far = [pieces_first[c::chunks] for c in range(chunks)]
    out.sum_z(*now)
    relay(updown, first, near_far[0], *now)
    sent, kept = input_grads(
        [[tie(grad_first[0], *first.ready, *updown.ready, *out.square), grad_first[1]], list(grad_other)],
        [weight_own, weight_other], rows,
    )
    now = (sent, first.from_x, first.from_y, *updown.parts[1:])
    relay(first, second, near_far[1], *now)
    now = (second.from_x, second.from_y, *first.parts[1:], *updown.parts[1:])
    second.send_z(*now)
    out.send_y(*now, *second.ready)
    received = swap(tie(sent, *now, *second.ready), "core", 1)
    out.send_x()
    input_grad = first_norm_grads(kept, received, inputs, grad_own, gain_first)
    updown_grad, out_grad = updown.total(), out.total()
    second_parts = (tie(second.parts[0], out.from_x, input_grad), *second.parts[1:])
    qkv_grad, small = join_chunks([first.parts, second_parts], jnp.transpose(w_qkv, (1, 0, 2)), factors)
    tensor = ("tx", "core")
    others = [lax.ppermute(small, tensor, [(i, i ^ bit) for i in range(4)]) for bit in (1, 2, 3)]
    summed = small + others[0] + others[1] + others[2]
    if size == 8:
        upbias_grad = small[2:4].reshape(-1)
        downbias_grad, mlpgain_grad, scale_sum = summed[1], summed[0], summed[SCALE_COLUMN, :HD]
    else:
        everything = ("fsdp", "tx", "core")
        upbias_grad = lax.psum(upbias_sum[0, :width] + swap(upbias_sum[0, width:], "tx", 1), "fsdp")
        vectors = lax.psum(jnp.concatenate([downbias_sum, mlpgain_sum]), everything)
        downbias_grad, mlpgain_grad = lax.dynamic_slice_in_dim(vectors, rank * shard, shard, 1)
        scale_sum = scale_factor * lax.psum(sums_other + sums_first, everything)[0]
    return (
        layer_out,
        input_grad,
        jnp.transpose(qkv_grad, (1, 0, 2)),
        out_grad.T,
        updown_grad[:, :width],
        upbias_grad,
        updown_grad[:, width:].T,
        downbias_grad,
        summed[SCALE_COLUMN + 1],
        mlpgain_grad,
        scale_sum,
    )


def solution(mesh):
    size, tensor = mesh.shape["fsdp"], mesh.shape["tensor"]
    split = Mesh(mesh.devices.reshape(size, tensor // 2, 2), ("fsdp", "tx", "core"))
    tokens = P(("fsdp", "tx", "core"), None)
    tensor_axes = ("tx", "core")
    in_specs = (
        tokens,
        P("fsdp"),
        P("fsdp", None, tensor_axes),
        P(tensor_axes, "fsdp"),
        P("fsdp", tensor_axes),
        P(tensor_axes),
        P(tensor_axes, "fsdp"),
        P("fsdp"),
        P("fsdp"),
        P("fsdp"),
        P(),
        tokens,
    )
    out_specs = (
        tokens,
        tokens,
        P("fsdp", None, tensor_axes),
        P(tensor_axes, "fsdp"),
        P("fsdp", tensor_axes),
        P(tensor_axes),
        P(tensor_axes, "fsdp"),
        P("fsdp"),
        P("fsdp"),
        P("fsdp"),
        P(),
    )
    return jax.shard_map(local, mesh=split, in_specs=in_specs, out_specs=out_specs, check_vma=False)
```
